32 devices in a mesh: fsdp: 8 (over y, x, core), tp: 4 (over z).
Axes of the slice: x: 2, y: 2, z: 4, core: 2. Of those that a mesh axis runs over, the one named last changes fastest.
Arguments:
- inputs: bfloat16 [2048, 16, 768], P('tp', 'fsdp'), may hold values from -6 to 6
- segments: int32 [2048, 16], P(None, 'fsdp'), may hold values from 0 to 2047, as said below
- w_qkv: bfloat16 [768, 3, 768], P('fsdp', None, 'tp'), may hold values from -0.21875 to 0.21875
- qkv_bias: float32 [3, 768], P(None, 'tp'), may hold values from -3 to 3
- pool_kernel: float32 [2, 5, 768], P(None, None, 'tp'), may hold values from -3 to 3
- w_out: bfloat16 [768, 768], P('fsdp', 'tp'), may hold values from -3.5 to 3.5
- out_bias: float32 [2, 768], replicated, may hold values from -3 to 3
- w_up: bfloat16 [768, 3072], P('fsdp', 'tp'), may hold values from -0.21875 to 0.21875
- up_bias: float32 [3072], P('tp'), may hold values from -3 to 3
- w_down: bfloat16 [768, 3072], P('fsdp', 'tp'), may hold values from -0.21875 to 0.21875
- norm_gains: float32 [2, 768], replicated, may hold values from 0.25 to 1.75
- norm_shifts: float32 [2, 768], replicated, may hold values from -3 to 3
- cotangent: bfloat16 [2048, 16, 768], P('tp', 'fsdp'), may hold values from -6 to 6
Outputs:
- outputs: bfloat16 [2048, 16, 768], P('tp', 'fsdp')
- grad_inputs: float32 [2048, 16, 768], P('tp', 'fsdp')
- grad_w_qkv: float32 [768, 3, 768], P('fsdp', None, 'tp')
- grad_qkv_bias: float32 [3, 768], P(None, 'tp')
- grad_pool_kernel: float32 [2, 5, 768], P(None, None, 'tp')
- grad_w_out: float32 [768, 768], P('fsdp', 'tp')
- grad_out_bias: float32 [2, 768], replicated
- grad_w_up: float32 [768, 3072], P('fsdp', 'tp')
- grad_up_bias: float32 [3072], P('tp')
- grad_w_down: float32 [768, 3072], P('fsdp', 'tp')
- grad_norm_gains: float32 [2, 768], replicated
- grad_norm_shifts: float32 [2, 768], replicated
The draws below stay inside these ranges and needn't reach their ends.
Inputs may be any that keep to these rules, and one draw needn't show every extreme that they name: `segments`: along each sequence a token's document number is the position of its document's first token, so it never falls; the last token of every sequence is a document of its own; one document of every sequence covers at least 1536 consecutive tokens.
All inputs are finite; a program needn't handle non-finite values.
Results may differ from the reference program's by a relative error of at most 0.02.
The reference program's roundings to bfloat16 on the way count: a program that leaves them out, or rounds other values in their place, can miss the bound.
Values may be sent and summed in bfloat16 or wider, within the bound.
No kernel may reach another device: no remote copies, remote signals or barrier semaphores. Data moves between devices by JAX's collectives and lax.ppermute only.
A program may use at most 192 MiB of HBM per device.

```python
import jax
import jax.numpy as jnp
from jax import lax

D = 768
HEADS = 12
HEAD_DIM = 64
FF = 3072
WINDOW = 128
POOL_STRIDE = 4
POOL_KERNEL = 5
SEQ_LEN = 2048
QBLOCK = 512
NSEQ = 16


def draw_segments(key, part):
    key_begin, key_finish, key_cuts, key_rate = jax.random.split(jax.random.fold_in(key, 17), 4)
    eighth = SEQ_LEN // 8
    begin = jax.random.randint(key_begin, (NSEQ,), 0, eighth)
    finish = SEQ_LEN - jax.random.randint(key_finish, (NSEQ,), 1, eighth)
    spacing = jax.random.randint(key_rate, (NSEQ,), 3, 40)
    cuts = jax.random.randint(key_cuts, (SEQ_LEN, NSEQ), 0, 1024)
    position = jnp.arange(SEQ_LEN, dtype=jnp.int32)[:, None]
    outside = (position < begin[None, :]) | (position >= finish[None, :])
    random_start = (cuts < (1024 // spacing)[None, :]) & outside
    starts = random_start | (position == 0) | (position == begin[None, :]) | (position == finish[None, :]) | (position == SEQ_LEN - 1)
    marked = jnp.where(starts, position, 0).astype(jnp.int32)
    return lax.cummax(marked, axis=0)


def block_scale(own_key, dims, cuts, low, largest):
    def one(dim, shards_of):
        draws = jax.random.uniform(jax.random.fold_in(jax.random.fold_in(own_key, 6), dim), (shards_of,), jnp.float32, low / len(cuts), largest / len(cuts))
        return jnp.repeat(jnp.exp(draws), dims[dim] // shards_of).reshape((-1,) + (1,) * (len(dims) - dim - 1))

    level = one(*cuts[0])
    for cut in cuts[1:]:
        level = level * one(*cut)
    return level


def normal_values(own_key, shape, scale, bound, cuts=(), kind=jnp.bfloat16):
    drawn = scale * jax.random.normal(own_key, shape, jnp.float32)
    if cuts:
        drawn = drawn * block_scale(own_key, shape, cuts, -0.22, 0.18)
    return jnp.clip(drawn, -bound, bound).astype(kind)


def setup_inputs(seed: int = 0) -> dict:
    key_list = jax.random.split(jax.random.key(seed), 14)
    inputs = normal_values(key_list[0], (SEQ_LEN, NSEQ, D), 1.0, 6.0, ((0, 4), (1, 8)))
    segments = draw_segments(jax.random.fold_in(key_list[13], 71), 0)
    w_qkv = normal_values(key_list[2], (D, 3, D), D ** -0.5, 0.21875, ((0, 8), (2, 4)))
    qkv_bias = normal_values(key_list[3], (3, D), 0.5, 3.0, ((1, 4),), jnp.float32)
    pool_kernel = normal_values(key_list[4], (2, POOL_KERNEL, D), 0.5, 3.0, ((2, 4),), jnp.float32)
    w_out = normal_values(key_list[5], (D, D), (max(D // 256, 1)) ** -0.5, 3.5, ((0, 8), (1, 4)))
    out_bias = normal_values(key_list[6], (2, D), 0.5, 3.0, (), jnp.float32)
    w_up = normal_values(key_list[7], (D, FF), D ** -0.5, 0.21875, ((0, 8), (1, 4)))
    up_bias = normal_values(key_list[8], (FF,), 0.5, 3.0, ((0, 4),), jnp.float32)
    w_down = normal_values(key_list[9], (D, FF), (FF // 4) ** -0.5, 0.21875, ((0, 8), (1, 4)))
    norm_gains = jnp.clip(1.0 + 0.15 * jax.random.normal(key_list[10], (2, D), jnp.float32), 0.25, 1.75)
    norm_shifts = normal_values(key_list[11], (2, D), 0.5, 3.0, (), jnp.float32)
    cotangent = normal_values(key_list[12], (SEQ_LEN, NSEQ, D), 1.0, 6.0, ((0, 4), (1, 8)))
    return dict(inputs=inputs, segments=segments, w_qkv=w_qkv, qkv_bias=qkv_bias, pool_kernel=pool_kernel, w_out=w_out, out_bias=out_bias, w_up=w_up, up_bias=up_bias, w_down=w_down, norm_gains=norm_gains, norm_shifts=norm_shifts, cotangent=cotangent)


@jax.custom_vjp
def low(v):
    return lax.optimization_barrier(v.astype(jnp.bfloat16)).astype(jnp.float32)

@jax.custom_vjp
def low_back(v):
    return v

def low_keep(v):
    return (low(v), None)

def low_pass(kept, grad):
    return (grad,)

def back_keep(v):
    return (v, None)

def back_low(kept, grad):
    return (low(grad),)
low.defvjp(low_keep, low_pass)
low_back.defvjp(back_keep, back_low)
EPSILON = 1e-05
PRECISE = lax.Precision.HIGHEST

def layer_norm(residual, norm_gain, norm_shift):
    row_mean = lax.optimization_barrier(jnp.mean(residual, axis=-1, keepdims=True))
    centered = residual - row_mean
    variance = lax.optimization_barrier(jnp.mean(centered * centered, axis=-1, keepdims=True))
    return centered * lax.rsqrt(variance + EPSILON) * norm_gain + norm_shift

def pool_pairs(pair_vals, kernel_vals, seg_rows):
    pair_count, seq_count, length, features = pair_vals.shape
    margin = POOL_KERNEL // 2
    pooled_len = length // POOL_STRIDE
    padded = jnp.pad(pair_vals, ((0, 0), (0, 0), (margin, margin), (0, 0)))
    seg_pad = jnp.pad(seg_rows, ((0, 0), (margin, margin)), constant_values=-1)
    centers = seg_rows.reshape(seq_count, pooled_len, POOL_STRIDE)[:, :, 0]
    pooled_sum = jnp.zeros((pair_count, seq_count, pooled_len, features), jnp.float32)
    for offset in range(POOL_KERNEL):
        tapped = padded[:, :, offset:offset + length].reshape(pair_count, seq_count, pooled_len, POOL_STRIDE, features)[:, :, :, 0]
        same_doc = seg_pad[:, offset:offset + length].reshape(seq_count, pooled_len, POOL_STRIDE)[:, :, 0] == centers
        pooled_sum = pooled_sum + kernel_vals[:, offset][:, None, None, :] * tapped * same_doc.astype(jnp.float32)[None, :, :, None]
    return pooled_sum

def attend(queries, key_rows, value_rows, pooled, seg_row):
    half_window = WINDOW // 2
    length = queries.shape[0]
    near_width = QBLOCK + 2 * half_window
    keys_pad = jnp.pad(key_rows, ((half_window, half_window), (0, 0), (0, 0)))
    values_pad = jnp.pad(value_rows, ((half_window, half_window), (0, 0), (0, 0)))
    seg_pad = jnp.pad(seg_row, (half_window, half_window), constant_values=-1)
    centers = seg_row.reshape(-1, POOL_STRIDE)[:, 0]

    def one_block(first_row):
        query_blk = lax.dynamic_slice_in_dim(queries, first_row, QBLOCK, 0)
        key_near = lax.dynamic_slice_in_dim(keys_pad, first_row, near_width, 0)
        value_near = lax.dynamic_slice_in_dim(values_pad, first_row, near_width, 0)
        seg_query = lax.dynamic_slice_in_dim(seg_row, first_row, QBLOCK, 0)
        seg_near = lax.dynamic_slice_in_dim(seg_pad, first_row, near_width, 0)
        near_scores = jnp.einsum('qhe,khe->hqk', query_blk, key_near, precision=PRECISE)
        far_scores = jnp.einsum('qhe,khe->hqk', query_blk, pooled[0], precision=PRECISE)
        scores = low_back(jnp.concatenate([near_scores, far_scores], axis=-1) * HEAD_DIM ** (-0.5))
        query_pos = first_row + jnp.arange(QBLOCK, dtype=jnp.int32)
        key_pos = first_row - half_window + jnp.arange(near_width, dtype=jnp.int32)
        near_mask = (jnp.abs(query_pos[:, None] - key_pos[None, :]) <= half_window) & (seg_query[:, None] == seg_near[None, :])
        far_mask = seg_query[:, None] == centers[None, :]
        allowed = jnp.concatenate([near_mask, far_mask], axis=-1)
        probs = low(jax.nn.softmax(jnp.where(allowed[None], scores, -1e+30), axis=-1))
        mixed_out = jnp.einsum('hqk,khe->qhe', probs[:, :, :near_width], value_near, precision=PRECISE)
        return mixed_out + jnp.einsum('hqk,khe->qhe', probs[:, :, near_width:], pooled[1], precision=PRECISE)
    starts = jnp.arange(length // QBLOCK, dtype=jnp.int32) * QBLOCK
    mixed_out = lax.map(jax.checkpoint(one_block), starts)
    return mixed_out.reshape(length, -1)

def sequence_forward(params, inputs_seq, seg_row):
    w_qkv, qkv_bias, pool_kernel, w_out, out_bias, w_up, up_bias, w_down, norm_gains, norm_shifts = params
    length = inputs_seq.shape[0]
    projected = jnp.einsum('td,dcf->tcf', inputs_seq, w_qkv, precision=PRECISE) + qkv_bias
    projected = low(low_back(projected))
    queries = projected[:, 0].reshape(length, HEADS, HEAD_DIM)
    key_rows = projected[:, 1]
    value_rows = projected[:, 2]
    pooled = pool_pairs(jnp.stack([key_rows, value_rows])[:, None], pool_kernel, seg_row[None])[:, 0]
    pooled = low(low_back(pooled)).reshape(2, -1, HEADS, HEAD_DIM)
    attended = attend(queries, key_rows.reshape(length, HEADS, HEAD_DIM), value_rows.reshape(length, HEADS, HEAD_DIM), pooled, seg_row)
    attended = low(low_back(attended))
    branch = low_back(jnp.dot(attended, w_out.T, precision=PRECISE) + out_bias[0])
    first_out = layer_norm(inputs_seq + branch, norm_gains[0], norm_shifts[0])
    pre_act = low_back(jnp.dot(low(first_out), w_up, precision=PRECISE) + up_bias)
    hidden = low(jax.nn.gelu(pre_act, approximate=False))
    ffn_out = low_back(jnp.dot(hidden, w_down.T, precision=PRECISE) + out_bias[1])
    return layer_norm(first_out + ffn_out, norm_gains[1], norm_shifts[1])

def reference(inputs, segments, w_qkv, qkv_bias, pool_kernel, w_out, out_bias, w_up, up_bias, w_down, norm_gains, norm_shifts, cotangent):
    params = (w_qkv.astype(jnp.float32), qkv_bias, pool_kernel, w_out.astype(jnp.float32), out_bias, w_up.astype(jnp.float32), up_bias, w_down.astype(jnp.float32), norm_gains, norm_shifts)
    seq_inputs = jnp.transpose(inputs.astype(jnp.float32), (1, 0, 2))
    seq_segments = segments.T

    def forward(layer_in, weights):

        def one_seq(operands):
            return sequence_forward(weights, operands[0], operands[1])
        return lax.map(jax.checkpoint(one_seq), (layer_in, seq_segments))
    outputs, back_fn = jax.vjp(forward, seq_inputs, params)
    grad_seq, param_grads = back_fn(jnp.transpose(cotangent.astype(jnp.float32), (1, 0, 2)))
    return (jnp.transpose(outputs, (1, 0, 2)).astype(jnp.bfloat16), jnp.transpose(grad_seq, (1, 0, 2)), param_grads[0], param_grads[1], param_grads[2], param_grads[3], param_grads[4], param_grads[5], param_grads[6], param_grads[7], param_grads[8], param_grads[9])
```

```python
from functools import partial

import jax
import jax.numpy as jnp
from jax import lax
from jax.experimental import pallas as pl
from jax.experimental.pallas import tpu as pltpu
from jax.sharding import PartitionSpec as P

HEAD_DIM = 64
HALF = 64
STRIDE = 4
TAPS = 5
MARGIN = TAPS // 2
PAIR = 2 * HEAD_DIM
QB = 128
EPSILON = 1e-05
NEG = -1e30
SCALE = HEAD_DIM**-0.5
BF = jnp.bfloat16
F32 = jnp.float32


def nt(a, b):
    return lax.dot_general(a, b, (((1,), (1,)), ((), ())), preferred_element_type=F32)


def nn(a, b):
    return lax.dot_general(a, b, (((1,), (0,)), ((), ())), preferred_element_type=F32)


def tn(a, b):
    return lax.dot_general(a, b, (((0,), (0,)), ((), ())), preferred_element_type=F32)


def fill_masks(segq_ref, segk_ref, cen_ref, near_bias, far_bias):
    rows = segq_ref.shape[1]
    shape = (QB, 2 * HALF + QB)
    gap = lax.broadcasted_iota(jnp.int32, shape, 1) - lax.broadcasted_iota(jnp.int32, shape, 0)
    band = (gap >= 0) & (gap <= 2 * HALF)
    for first in range(0, rows, QB):
        own = segq_ref[0, first : first + QB, :]
        keys = segk_ref[0, :, first : first + QB + 2 * HALF]
        near_bias[first : first + QB, :] = jnp.where(band & (own == keys), 0.0, NEG)
        far_bias[first : first + QB, :] = jnp.where(own == cen_ref[0], 0.0, NEG)


def join_rows(left_ref, own_ref, right_ref, joined):
    rows = own_ref.shape[1]
    joined[:HALF, :] = left_ref[0]
    joined[HALF : HALF + rows, :] = own_ref[0]
    joined[HALF + rows :, :] = right_ref[0]


def head_mask(head):
    lane = lax.broadcasted_iota(jnp.int32, (1, PAIR), 1)
    return lane < HEAD_DIM if head == 0 else lane >= HEAD_DIM


def softmax_block(query, keys_near, keys_far, bias_near, bias_far):
    near = nt(query, keys_near) + bias_near
    far = nt(query, keys_far) + bias_far
    top = jnp.maximum(
        jnp.max(near, axis=-1, keepdims=True), jnp.max(far, axis=-1, keepdims=True)
    )
    near = jnp.exp(near - top)
    far = jnp.exp(far - top)
    total = jnp.sum(near, axis=-1, keepdims=True) + jnp.sum(far, axis=-1, keepdims=True)
    inverse = 1.0 / total
    return near * inverse, far * inverse


def attend_forward_kernel(
    q_ref, k_ref, v_ref, kl_ref, kr_ref, vl_ref, vr_ref, pk_ref, pv_ref,
    segq_ref, segk_ref, cen_ref, out_ref, near_bias, far_bias, keys, values,
):
    @pl.when(pl.program_id(1) == 0)
    def _():
        fill_masks(segq_ref, segk_ref, cen_ref, near_bias, far_bias)

    rows = q_ref.shape[1]
    join_rows(kl_ref, k_ref, kr_ref, keys)
    join_rows(vl_ref, v_ref, vr_ref, values)
    far_keys = pk_ref[...].reshape(-1, PAIR)
    far_values = pv_ref[...].reshape(-1, PAIR)
    for first in range(0, rows, QB):
        block = slice(first, first + QB)
        span = slice(first, first + QB + 2 * HALF)
        query = q_ref[0, block, :] * BF(SCALE)
        halves = []
        for head in range(2):
            picked = jnp.where(head_mask(head), query, BF(0))
            near, far = softmax_block(
                picked, keys[span, :], far_keys, near_bias[block, :], far_bias[block, :]
            )
            halves.append(nn(near.astype(BF), values[span, :]) + nn(far.astype(BF), far_values))
        out_ref[0, block, :] = jnp.where(head_mask(0), halves[0], halves[1]).astype(BF)


def attend_backward_kernel(
    q_ref, k_ref, v_ref, kl_ref, kr_ref, vl_ref, vr_ref, pk_ref, pv_ref,
    segq_ref, segk_ref, cen_ref, grad_ref,
    dq_ref, dk_ref, dv_ref, dpk_ref, dpv_ref,
    near_bias, far_bias, keys, values, far_probs, far_grads,
):
    @pl.when(pl.program_id(1) == 0)
    def _():
        fill_masks(segq_ref, segk_ref, cen_ref, near_bias, far_bias)

    rows = q_ref.shape[1]
    join_rows(kl_ref, k_ref, kr_ref, keys)
    join_rows(vl_ref, v_ref, vr_ref, values)
    far_keys = pk_ref[...].reshape(-1, PAIR)
    far_values = pv_ref[...].reshape(-1, PAIR)
    dk_ref[...] = jnp.zeros_like(dk_ref)
    dv_ref[...] = jnp.zeros_like(dv_ref)
    for head in range(2):
        mask = head_mask(head)
        for first in range(0, rows, QB):
            block = slice(first, first + QB)
            span = slice(first, first + QB + 2 * HALF)
            query = jnp.where(mask, q_ref[0, block, :] * BF(SCALE), BF(0))
            grad = jnp.where(mask, grad_ref[0, block, :], BF(0))
            near, far = softmax_block(
                query, keys[span, :], far_keys, near_bias[block, :], far_bias[block, :]
            )
            grad_near = nt(grad, values[span, :])
            grad_far = nt(grad, far_values)
            row_dot = jnp.sum(near * grad_near, axis=-1, keepdims=True) + jnp.sum(
                far * grad_far, axis=-1, keepdims=True
            )
            ds_near = (near * (grad_near - row_dot)).astype(BF)
            ds_far = (far * (grad_far - row_dot)).astype(BF)
            far_probs[block, :] = far.astype(BF)
            far_grads[block, :] = ds_far
            dq = (nn(ds_near, keys[span, :]) + nn(ds_far, far_keys)) * SCALE
            if head == 0:
                dq_ref[0, block, :] = dq.astype(BF)
            else:
                dq_ref[0, block, :] = jnp.where(mask, dq.astype(BF), dq_ref[0, block, :])
            dk_ref[0, span, :] += tn(ds_near, query)
            dv_ref[0, span, :] += tn(near.astype(BF), grad)
        query = jnp.where(mask, q_ref[0] * BF(SCALE), BF(0))
        grad = jnp.where(mask, grad_ref[0], BF(0))
        dpk = tn(far_grads[...], query).reshape(dpk_ref.shape)
        dpv = tn(far_probs[...], grad).reshape(dpv_ref.shape)
        if head == 0:
            dpk_ref[...] = dpk.astype(BF)
            dpv_ref[...] = dpv.astype(BF)
        else:
            dpk_ref[...] = jnp.where(mask, dpk.astype(BF), dpk_ref[...])
            dpv_ref[...] = jnp.where(mask, dpv.astype(BF), dpv_ref[...])


def attention_specs(seqs, rows, parts, blocks, far_rows):
    def own(part):
        return pl.BlockSpec((None, 1, rows, PAIR), lambda s, h: (part, s, 0, h))

    def halo(part):
        return pl.BlockSpec((None, 1, HALF, PAIR), lambda s, h: (part, s, 0, h))

    def pooled(part):
        return pl.BlockSpec(
            (blocks, None, 1, far_rows, PAIR), lambda s, h: (0, part, s, 0, h)
        )

    return [
        own(0), own(1), own(2),
        halo(0), halo(0), halo(1), halo(1),
        pooled(0), pooled(1),
        pl.BlockSpec((1, rows, 1), lambda s, h: (s, 0, 0)),
        pl.BlockSpec((1, 1, rows + 2 * HALF), lambda s, h: (s, 0, 0)),
        pl.BlockSpec((1, 1, blocks * far_rows), lambda s, h: (s, 0, 0)),
    ]


def attention_scratch(rows, far_all):
    return [
        pltpu.VMEM((rows, 2 * HALF + QB), F32),
        pltpu.VMEM((rows, far_all), F32),
        pltpu.VMEM((rows + 2 * HALF, PAIR), BF),
        pltpu.VMEM((rows + 2 * HALF, PAIR), BF),
    ]


def attend_forward(projected, left, right, pooled, segs):
    _, seqs, rows, width = projected.shape
    blocks, _, _, far_rows, _ = pooled.shape
    cells = seqs * rows * (2 * HALF + QB + blocks * far_rows) * (width // HEAD_DIM)
    return pl.pallas_call(
        attend_forward_kernel,
        grid=(seqs, width // PAIR),
        in_specs=attention_specs(seqs, rows, 3, blocks, far_rows),
        out_specs=pl.BlockSpec((1, rows, PAIR), lambda s, h: (s, 0, h)),
        out_shape=jax.ShapeDtypeStruct((seqs, rows, width), BF),
        scratch_shapes=attention_scratch(rows, blocks * far_rows),
        compiler_params=pltpu.CompilerParams(vmem_limit_bytes=40 * 2**20),
        cost_estimate=pl.CostEstimate(
            flops=8 * 64 * cells, bytes_accessed=12 * 2**20, transcendentals=cells
        ),
    )(projected, projected, projected, left, right, left, right, pooled, pooled, *segs)


def attend_backward(projected, left, right, pooled, segs, grad):
    _, seqs, rows, width = projected.shape
    blocks, _, _, far_rows, _ = pooled.shape
    cells = seqs * rows * (2 * HALF + QB + blocks * far_rows) * (width // HEAD_DIM)
    wide = rows + 2 * HALF
    far_spec = pl.BlockSpec((blocks, 1, far_rows, PAIR), lambda s, h: (0, s, 0, h))
    far_shape = jax.ShapeDtypeStruct((blocks, seqs, far_rows, width), BF)
    wide_spec = pl.BlockSpec((1, wide, PAIR), lambda s, h: (s, 0, h))
    wide_shape = jax.ShapeDtypeStruct((seqs, wide, width), F32)
    own_spec = pl.BlockSpec((1, rows, PAIR), lambda s, h: (s, 0, h))
    return pl.pallas_call(
        attend_backward_kernel,
        grid=(seqs, width // PAIR),
        in_specs=attention_specs(seqs, rows, 3, blocks, far_rows) + [own_spec],
        out_specs=[own_spec, wide_spec, wide_spec, far_spec, far_spec],
        out_shape=[
            jax.ShapeDtypeStruct((seqs, rows, width), BF),
            wide_shape, wide_shape, far_shape, far_shape,
        ],
        scratch_shapes=attention_scratch(rows, blocks * far_rows)
        + [pltpu.VMEM((rows, blocks * far_rows), BF)] * 2,
        compiler_params=pltpu.CompilerParams(vmem_limit_bytes=40 * 2**20),
        cost_estimate=pl.CostEstimate(
            flops=20 * 64 * cells, bytes_accessed=24 * 2**20, transcendentals=cells
        ),
    )(projected, projected, projected, left, right, left, right, pooled, pooled, *segs, grad)


def norm_stats(residual):
    row_mean = jnp.mean(residual, axis=-1, keepdims=True)
    centered = residual - row_mean
    variance = jnp.mean(centered * centered, axis=-1, keepdims=True)
    inverse = lax.rsqrt(variance + EPSILON)
    return centered * inverse, inverse


def norm_back(grad, normed, inverse, gain):
    scaled = grad * gain
    first = jnp.mean(scaled, axis=-1, keepdims=True)
    second = jnp.mean(scaled * normed, axis=-1, keepdims=True)
    return (scaled - first - normed * second) * inverse


def gather_weight(shard):
    wide = lax.all_gather(shard, "tp", axis=shard.ndim - 1, tiled=True)
    return lax.all_gather(wide, "fsdp", axis=0, tiled=True)


def scatter_weight(grad):
    part = lax.psum_scatter(grad.astype(BF), "fsdp", scatter_dimension=0, tiled=True)
    return lax.psum_scatter(
        part, "tp", scatter_dimension=part.ndim - 1, tiled=True
    ).astype(F32)


def shift_right(rows):
    count = lax.axis_size("tp")
    return lax.ppermute(rows, "tp", [(i, i + 1) for i in range(count - 1)])


def shift_left(rows):
    count = lax.axis_size("tp")
    return lax.ppermute(rows, "tp", [(i + 1, i) for i in range(count - 1)])


def body(
    inputs, segments, w_qkv, qkv_bias, pool_kernel, w_out, out_bias,
    w_up, up_bias, w_down, norm_gains, norm_shifts, cotangent,
):
    rows, seqs, width = inputs.shape
    tp = lax.axis_size("tp")
    place = lax.axis_index("tp")
    full_len = rows * tp
    far_rows = rows // STRIDE

    seg_rows = segments.T
    padded = jnp.pad(seg_rows, ((0, 0), (HALF, HALF)), constant_values=-1)
    seg_keys = lax.dynamic_slice_in_dim(padded, place * rows, rows + 2 * HALF, 1)
    seg_own = seg_keys[:, HALF : HALF + rows]
    centers_all = seg_rows[:, ::STRIDE]
    segs = (seg_own[:, :, None], seg_keys[:, None, :], centers_all[:, None, :])
    centers = seg_own[:, ::STRIDE]
    near_seg = seg_keys[:, HALF - MARGIN : HALF + rows]
    same = [
        (near_seg[:, r : r + rows : STRIDE][:, :far_rows] == centers).astype(F32)
        for r in range(TAPS)
    ]

    tokens = inputs.transpose(1, 0, 2)
    full_qkv = gather_weight(w_qkv)
    bias_qkv = lax.all_gather(qkv_bias, "tp", axis=1, tiled=True)
    kernel = lax.all_gather(pool_kernel, "tp", axis=2, tiled=True)
    bias_up = lax.all_gather(up_bias, "tp", axis=0, tiled=True)
    full_out = gather_weight(w_out)
    full_up = gather_weight(w_up)
    full_down = gather_weight(w_down)

    made = jnp.einsum("sld,dcf->cslf", tokens, full_qkv, preferred_element_type=F32)
    projected = (made + bias_qkv[:, None, None, :]).astype(BF)
    left = shift_right(projected[1:, :, rows - HALF :])
    right = shift_left(projected[1:, :, :HALF])

    wide = jnp.concatenate([left[:, :, HALF - MARGIN :], projected[1:]], axis=2)
    tapped = [
        lax.slice_in_dim(wide, r, r + rows - STRIDE + 1, STRIDE, 2).astype(F32)
        for r in range(TAPS)
    ]
    pooled_own = sum(
        kernel[:, r][:, None, None, :] * tapped[r] * same[r][None, :, :, None]
        for r in range(TAPS)
    ).astype(BF)
    pooled = lax.all_gather(pooled_own, "tp", axis=0, tiled=False)
    attended = attend_forward(projected, left, right, pooled, segs)

    branch = (
        jnp.einsum("slf,ef->sle", attended, full_out, preferred_element_type=F32) + out_bias[0]
    )
    normed_one, inverse_one = norm_stats(tokens.astype(F32) + branch)
    first_out = normed_one * norm_gains[0] + norm_shifts[0]
    first_low = first_out.astype(BF)
    pre_act = (
        jnp.einsum("sld,df->slf", first_low, full_up, preferred_element_type=F32) + bias_up
    )
    hidden = jax.nn.gelu(pre_act, approximate=False).astype(BF)
    ffn_out = (
        jnp.einsum("slf,ef->sle", hidden, full_down, preferred_element_type=F32) + out_bias[1]
    )
    normed_two, inverse_two = norm_stats(first_out + ffn_out)
    outputs = normed_two * norm_gains[1] + norm_shifts[1]

    grad_out = cotangent.transpose(1, 0, 2).astype(F32)
    grad_second = norm_back(grad_out, normed_two, inverse_two, norm_gains[1])
    gain_two = jnp.sum(grad_out * normed_two, axis=(0, 1))
    shift_two = jnp.sum(grad_out, axis=(0, 1))
    grad_ffn_low = grad_second.astype(BF)
    grad_hidden = jnp.einsum("sle,ef->slf", grad_ffn_low, full_down, preferred_element_type=F32)
    gelu_back = jax.vjp(partial(jax.nn.gelu, approximate=False), pre_act)[1]
    grad_pre = gelu_back(grad_hidden)[0].astype(BF)
    grad_w_down = jnp.einsum("sle,slf->ef", grad_ffn_low, hidden, preferred_element_type=F32)
    grad_w_down = scatter_weight(grad_w_down)
    grad_w_up = jnp.einsum("sld,slf->df", first_low, grad_pre, preferred_element_type=F32)
    grad_w_up = scatter_weight(grad_w_up)
    grad_up_bias = jnp.sum(grad_pre, axis=(0, 1), dtype=F32)
    grad_first = grad_second + jnp.einsum(
        "slf,df->sld", grad_pre, full_up, preferred_element_type=F32
    )
    grad_residual = norm_back(grad_first, normed_one, inverse_one, norm_gains[0])
    gain_one = jnp.sum(grad_first * normed_one, axis=(0, 1))
    shift_one = jnp.sum(grad_first, axis=(0, 1))
    grad_branch_low = grad_residual.astype(BF)
    grad_attended = jnp.einsum(
        "sle,ef->slf", grad_branch_low, full_out, preferred_element_type=F32
    ).astype(BF)
    grad_w_out = jnp.einsum("sle,slf->ef", grad_branch_low, attended, preferred_element_type=F32)
    grad_w_out = scatter_weight(grad_w_out)

    dq, dk, dv, dpk, dpv = attend_backward(projected, left, right, pooled, segs, grad_attended)
    grad_pooled = lax.psum_scatter(
        jnp.stack([dpk, dpv], axis=1), "tp", scatter_dimension=0, tiled=False
    ).astype(F32)
    pair_grads = jnp.stack([dk, dv])
    to_left = pair_grads[:, :, :HALF]
    to_right = pair_grads[:, :, HALF + rows :]
    tap_grads = []
    grad_taps = []
    for r in range(TAPS):
        masked = grad_pooled * same[r][None, :, :, None]
        tap_grads.append(kernel[:, r][:, None, None, :] * masked)
        grad_taps.append(jnp.sum(masked * tapped[r], axis=(1, 2)))
    grad_kernel = jnp.stack(grad_taps, axis=1)
    later = jnp.pad(tap_grads[4], ((0, 0), (0, 0), (1, 0), (0, 0)))
    quads = jnp.stack(
        [
            jnp.pad(tap_grads[0], ((0, 0), (0, 0), (0, 1), (0, 0))) + later,
            jnp.pad(tap_grads[1], ((0, 0), (0, 0), (0, 1), (0, 0))),
            jnp.pad(tap_grads[2], ((0, 0), (0, 0), (0, 1), (0, 0))),
            jnp.pad(tap_grads[3], ((0, 0), (0, 0), (0, 1), (0, 0))),
        ],
        axis=3,
    ).reshape(2, seqs, rows + STRIDE, width)
    to_left = to_left.at[:, :, HALF - MARGIN :].add(quads[:, :, :MARGIN])
    own_pairs = pair_grads[:, :, HALF : HALF + rows] + quads[:, :, MARGIN : MARGIN + rows]
    from_right = shift_left(to_left.astype(BF)).astype(F32)
    from_left = shift_right(to_right.astype(BF)).astype(F32)
    own_pairs = own_pairs.at[:, :, rows - HALF :].add(from_right)
    own_pairs = own_pairs.at[:, :, :HALF].add(from_left)
    grad_projected = jnp.concatenate([dq[None], own_pairs.astype(BF)], axis=0)
    grad_qkv_bias = jnp.sum(grad_projected, axis=(1, 2), dtype=F32)
    grad_w_qkv = jnp.einsum("sld,cslf->dcf", tokens, grad_projected, preferred_element_type=F32)
    grad_w_qkv = scatter_weight(grad_w_qkv)
    grad_inputs = grad_residual + jnp.einsum(
        "cslf,dcf->sld", grad_projected, full_qkv, preferred_element_type=F32
    )

    grad_out_bias = jnp.stack(
        [
            jnp.sum(grad_branch_low, axis=(0, 1), dtype=F32),
            jnp.sum(grad_ffn_low, axis=(0, 1), dtype=F32),
        ]
    )
    grad_norm_gains = jnp.stack([gain_one, gain_two])
    grad_norm_shifts = jnp.stack([shift_one, shift_two])
    (
        grad_qkv_bias, grad_kernel, grad_up_bias, grad_out_bias, grad_norm_gains, grad_norm_shifts
    ) = lax.psum(
        (
            grad_qkv_bias, grad_kernel, grad_up_bias,
            grad_out_bias, grad_norm_gains, grad_norm_shifts,
        ),
        ("fsdp", "tp"),
    )

    def own_columns(whole):
        count = whole.shape[-1] // tp
        return lax.dynamic_slice_in_dim(whole, place * count, count, whole.ndim - 1)

    return (
        outputs.transpose(1, 0, 2).astype(BF),
        grad_inputs.transpose(1, 0, 2),
        grad_w_qkv,
        own_columns(grad_qkv_bias),
        own_columns(grad_kernel),
        grad_w_out,
        grad_out_bias,
        grad_w_up,
        own_columns(grad_up_bias),
        grad_w_down,
        grad_norm_gains,
        grad_norm_shifts,
    )


def solution(mesh):
    placed = (
        P("tp", "fsdp", None),
        P(None, "fsdp"),
        P("fsdp", None, "tp"),
        P(None, "tp"),
        P(None, None, "tp"),
        P("fsdp", "tp"),
        P(),
        P("fsdp", "tp"),
        P("tp"),
        P("fsdp", "tp"),
        P(),
        P(),
        P("tp", "fsdp", None),
    )
    return jax.shard_map(
        body,
        mesh=mesh,
        in_specs=placed,
        out_specs=(
            P("tp", "fsdp", None),
            P("tp", "fsdp", None),
            P("fsdp", None, "tp"),
            P(None, "tp"),
            P(None, None, "tp"),
            P("fsdp", "tp"),
            P(),
            P("fsdp", "tp"),
            P("tp"),
            P("fsdp", "tp"),
            P(),
            P(),
        ),
        check_vma=False,
    )
```

```python
from functools import partial

import jax
import jax.numpy as jnp
import numpy as np
from jax import lax
from jax.experimental import pallas as pl
from jax.experimental.pallas import tpu as pltpu
from jax.sharding import PartitionSpec as P

HEAD_DIM = 64
HALF = 64
STRIDE = 4
TAPS = 5
MARGIN = TAPS // 2
PAIR = 2 * HEAD_DIM
QB = 128
NEAR = QB + 2 * HALF
FB = 512
RC = 256
EPSILON = 1e-05
NEG = -1e30
SCALE = HEAD_DIM**-0.5
BF = jnp.bfloat16
F32 = jnp.float32
MIB = 2**20


def nt(a, b):
    return lax.dot_general(a, b, (((1,), (1,)), ((), ())), preferred_element_type=F32)


def nn(a, b):
    return lax.dot_general(a, b, (((1,), (0,)), ((), ())), preferred_element_type=F32)


def tn(a, b):
    return lax.dot_general(a, b, (((0,), (0,)), ((), ())), preferred_element_type=F32)


def params(mib):
    return pltpu.CompilerParams(vmem_limit_bytes=mib * MIB)


def cost(flops, mib, trans=0):
    return pl.CostEstimate(flops=flops, bytes_accessed=mib * MIB, transcendentals=trans)


def once(shape):
    zeros = (0,) * len(shape)
    return pl.BlockSpec(shape, lambda *_: zeros, pipeline_mode=pl.Buffered(1))


def project_kernel(count, offs, *refs):
    pieces = refs[:count]
    x_ref, bias_ref, taps_ref, same_ref, out_ref, pooled_ref, w_ref, plain = refs[count:]
    part = pl.program_id(0)
    for n in range(count):
        rows = pieces[n].shape[0]
        w_ref[0, pl.ds(pl.multiple_of(offs[n], 16), rows), :] = pieces[n][...]
    seqs, wide, _ = x_ref.shape
    far_rows = pooled_ref.shape[2]
    for s in range(seqs):
        made = (nn(x_ref[s], w_ref[0]) + bias_ref[0]).astype(BF)
        out_ref[0, s] = made
        for half in range(plain.shape[1]):
            plain[s, half] = made[:, half * PAIR : (half + 1) * PAIR].astype(F32)

    @pl.when(part > 0)
    def _():
        for s in range(seqs):
            for half in range(plain.shape[1]):
                lanes = slice(half * PAIR, (half + 1) * PAIR)
                total = jnp.zeros((far_rows, PAIR), F32)
                for r in range(TAPS):
                    rows = plain[s, half, pl.ds(HALF - MARGIN + r, far_rows, stride=STRIDE), :]
                    total = total + taps_ref[0, r : r + 1, lanes] * rows * same_ref[
                        s, :, r : r + 1
                    ]
                pooled_ref[0, s, :, lanes] = total.astype(BF)


def project(chunk, chunks, pieces, offs, x_wide, bias, taps, same, far_rows):
    seqs, wide, width = x_wide.shape
    span = width // chunks

    def piece_spec(piece):
        return pl.BlockSpec((piece.shape[0], span), lambda c, o: (0, c * chunks + chunk))

    def kv(c):
        return jnp.maximum(c - 1, 0)

    return pl.pallas_call(
        partial(project_kernel, len(pieces)),
        grid_spec=pltpu.PrefetchScalarGridSpec(
            num_scalar_prefetch=1,
            grid=(3,),
            in_specs=[piece_spec(p) for p in pieces]
            + [
                once(x_wide.shape),
                pl.BlockSpec((1, 1, span), lambda c, o: (c, 0, chunk)),
                pl.BlockSpec((1, 8, span), lambda c, o: (kv(c), 0, chunk)),
                once(same.shape),
            ],
            out_specs=[
                pl.BlockSpec((1, seqs, wide, span), lambda c, o: (c, 0, 0, 0)),
                pl.BlockSpec((1, seqs, far_rows, span), lambda c, o: (kv(c), 0, 0, 0)),
                pl.BlockSpec((1, width, span), lambda c, o: (c, 0, 0)),
            ],
            scratch_shapes=[pltpu.VMEM((seqs, span // PAIR, wide, PAIR), F32)],
        ),
        out_shape=[
            jax.ShapeDtypeStruct((3, seqs, wide, span), BF),
            jax.ShapeDtypeStruct((2, seqs, far_rows, span), BF),
            jax.ShapeDtypeStruct((3, width, span), BF),
        ],
        compiler_params=params(32),
        cost_estimate=cost(6 * seqs * wide * width * span, 8),
    )(offs, *pieces, x_wide, bias, taps, same)


def fill_masks(segq_ref, segk_ref, cen_ref, near_bias, far_bias):
    rows = segq_ref.shape[1]
    shape = (QB, NEAR)
    gap = lax.broadcasted_iota(jnp.int32, shape, 1) - lax.broadcasted_iota(jnp.int32, shape, 0)
    band = (gap >= 0) & (gap <= 2 * HALF)
    for first in range(0, rows, QB):
        own = segq_ref[0, first : first + QB, :]
        keys = segk_ref[0, :, first : first + NEAR]
        near_bias[first : first + QB, :] = jnp.where(band & (own == keys), 0.0, NEG)
        far_bias[first : first + QB, :] = jnp.where(own == cen_ref[0], 0.0, NEG)


def head_mask(head):
    lane = lax.broadcasted_iota(jnp.int32, (1, PAIR), 1)
    return lane < HEAD_DIM if head == 0 else lane >= HEAD_DIM


def softmax_block(query, keys_near, keys_far, bias_near, bias_far):
    near = nt(query, keys_near) + bias_near
    far = nt(query, keys_far) + bias_far
    top = jnp.maximum(
        jnp.max(near, axis=-1, keepdims=True), jnp.max(far, axis=-1, keepdims=True)
    )
    near = jnp.exp(near - top)
    far = jnp.exp(far - top)
    total = jnp.sum(near, axis=-1, keepdims=True) + jnp.sum(far, axis=-1, keepdims=True)
    inverse = 1.0 / total
    return near * inverse, far * inverse


def join_slots(slots, joined):
    rows = slots[0].shape[1]
    for n, slot in enumerate(slots):
        joined[n * rows : (n + 1) * rows, :] = slot[0]


def attend_forward_kernel(blocks, q_ref, k_ref, v_ref, *refs):
    pk, pv = refs[:blocks], refs[blocks : 2 * blocks]
    segq, segk, cen, out_ref, near_bias, far_bias, far_keys, far_values = refs[2 * blocks :]

    @pl.when(pl.program_id(1) == 0)
    def _():
        fill_masks(segq, segk, cen, near_bias, far_bias)

    join_slots(pk, far_keys)
    join_slots(pv, far_values)
    for first in range(0, out_ref.shape[1], QB):
        block = slice(first, first + QB)
        span = slice(first, first + NEAR)
        query = q_ref[0, HALF + first : HALF + first + QB, :] * BF(SCALE)
        halves = []
        for head in range(2):
            picked = jnp.where(head_mask(head), query, BF(0))
            near, far = softmax_block(
                picked, k_ref[0, span, :], far_keys[...], near_bias[block, :], far_bias[block, :]
            )
            halves.append(
                nn(near.astype(BF), v_ref[0, span, :]) + nn(far.astype(BF), far_values[...])
            )
        out_ref[0, block, :] = jnp.where(head_mask(0), halves[0], halves[1]).astype(BF)


def attend_backward_kernel(blocks, q_ref, k_ref, v_ref, *refs):
    pk, pv = refs[:blocks], refs[blocks : 2 * blocks]
    segq, segk, cen, grad_ref, dq_ref, dk_ref, dv_ref = refs[2 * blocks : 2 * blocks + 7]
    dp_refs = refs[2 * blocks + 7 : 3 * blocks + 7]
    near_bias, far_bias, far_keys, far_values, far_probs, far_grads = refs[3 * blocks + 7 :]

    @pl.when(pl.program_id(1) == 0)
    def _():
        fill_masks(segq, segk, cen, near_bias, far_bias)

    rows = dq_ref.shape[1]
    join_slots(pk, far_keys)
    join_slots(pv, far_values)
    dk_ref[...] = jnp.zeros_like(dk_ref)
    dv_ref[...] = jnp.zeros_like(dv_ref)
    pieces = []
    for head in range(2):
        mask = head_mask(head)
        for first in range(0, rows, QB):
            block = slice(first, first + QB)
            span = slice(first, first + NEAR)
            query = jnp.where(
                mask, q_ref[0, HALF + first : HALF + first + QB, :] * BF(SCALE), BF(0)
            )
            grad = jnp.where(mask, grad_ref[0, block, :], BF(0))
            near, far = softmax_block(
                query, k_ref[0, span, :], far_keys[...], near_bias[block, :], far_bias[block, :]
            )
            grad_near = nt(grad, v_ref[0, span, :])
            grad_far = nt(grad, far_values[...])
            row_dot = jnp.sum(near * grad_near, axis=-1, keepdims=True) + jnp.sum(
                far * grad_far, axis=-1, keepdims=True
            )
            ds_near = (near * (grad_near - row_dot)).astype(BF)
            ds_far = (far * (grad_far - row_dot)).astype(BF)
            far_probs[block, :] = far.astype(BF)
            far_grads[block, :] = ds_far
            dq = (nn(ds_near, k_ref[0, span, :]) + nn(ds_far, far_keys[...])) * SCALE
            if head == 0:
                dq_ref[0, block, :] = dq.astype(BF)
            else:
                dq_ref[0, block, :] = jnp.where(mask, dq.astype(BF), dq_ref[0, block, :])
            dk_ref[0, span, :] += tn(ds_near, query)
            dv_ref[0, span, :] += tn(near.astype(BF), grad)
        query = jnp.where(mask, q_ref[0, HALF : HALF + rows, :] * BF(SCALE), BF(0))
        grad = jnp.where(mask, grad_ref[0], BF(0))
        pieces.append((tn(far_grads[...], query), tn(far_probs[...], grad)))
    far_rows = dp_refs[0].shape[2]
    for n, ref in enumerate(dp_refs):
        span = slice(n * far_rows, (n + 1) * far_rows)
        for c in range(2):
            ref[c, 0] = jnp.where(head_mask(0), pieces[0][c][span], pieces[1][c][span]).astype(BF)


def attention_specs(wide, blocks, far_rows):
    def own(part):
        return pl.BlockSpec((None, 1, wide, PAIR), lambda s, h: (part, s, 0, h))

    def pooled(part):
        return pl.BlockSpec((None, 1, far_rows, PAIR), lambda s, h: (part, s, 0, h))

    rows = wide - 2 * HALF
    return (
        [own(0), own(1), own(2)]
        + [pooled(0)] * blocks
        + [pooled(1)] * blocks
        + [
            pl.BlockSpec((1, rows, 1), lambda s, h: (s, 0, 0)),
            pl.BlockSpec((1, 1, wide), lambda s, h: (s, 0, 0)),
            pl.BlockSpec((1, 1, blocks * far_rows), lambda s, h: (s, 0, 0)),
        ]
    )


def attention_scratch(rows, far_all):
    return [
        pltpu.VMEM((rows, NEAR), F32),
        pltpu.VMEM((rows, far_all), F32),
        pltpu.VMEM((far_all, PAIR), BF),
        pltpu.VMEM((far_all, PAIR), BF),
    ]


def attend_forward(proj, slots, segs):
    _, seqs, wide, span = proj.shape
    blocks, far_rows = len(slots), slots[0].shape[2]
    rows = wide - 2 * HALF
    cells = seqs * rows * (NEAR + blocks * far_rows) * (span // HEAD_DIM)
    return pl.pallas_call(
        partial(attend_forward_kernel, blocks),
        grid=(seqs, span // PAIR),
        in_specs=attention_specs(wide, blocks, far_rows),
        out_specs=pl.BlockSpec((1, rows, PAIR), lambda s, h: (s, 0, h)),
        out_shape=jax.ShapeDtypeStruct((seqs, rows, span), BF),
        scratch_shapes=attention_scratch(rows, blocks * far_rows),
        compiler_params=params(32),
        cost_estimate=cost(16 * 64 * cells, 8, cells),
    )(proj, proj, proj, *slots, *slots, *segs)


def attend_backward(proj, slots, segs, grad):
    _, seqs, wide, span = proj.shape
    blocks, far_rows = len(slots), slots[0].shape[2]
    rows = wide - 2 * HALF
    cells = seqs * rows * (NEAR + blocks * far_rows) * (span // HEAD_DIM)
    own_spec = pl.BlockSpec((1, rows, PAIR), lambda s, h: (s, 0, h))
    wide_spec = pl.BlockSpec((1, wide, PAIR), lambda s, h: (s, 0, h))
    wide_shape = jax.ShapeDtypeStruct((seqs, wide, span), F32)
    far_spec = pl.BlockSpec((2, 1, far_rows, PAIR), lambda s, h: (0, s, 0, h))
    far_shape = jax.ShapeDtypeStruct((2, seqs, far_rows, span), BF)
    out = pl.pallas_call(
        partial(attend_backward_kernel, blocks),
        grid=(seqs, span // PAIR),
        in_specs=attention_specs(wide, blocks, far_rows) + [own_spec],
        out_specs=[own_spec, wide_spec, wide_spec] + [far_spec] * blocks,
        out_shape=[jax.ShapeDtypeStruct((seqs, rows, span), BF), wide_shape, wide_shape]
        + [far_shape] * blocks,
        scratch_shapes=attention_scratch(rows, blocks * far_rows)
        + [pltpu.VMEM((rows, blocks * far_rows), BF)] * 2,
        compiler_params=params(40),
        cost_estimate=cost(40 * 64 * cells, 16, cells),
    )(proj, proj, proj, *slots, *slots, *segs, grad)
    return out[0], out[1], out[2], out[3:]


def norm_stats(residual):
    row_mean = jnp.mean(residual, axis=-1, keepdims=True)
    centered = residual - row_mean
    variance = jnp.mean(centered * centered, axis=-1, keepdims=True)
    inverse = lax.rsqrt(variance + EPSILON)
    return centered * inverse, inverse


def norm_back(grad, normed, inverse, gain):
    scaled = grad * gain
    first = jnp.mean(scaled, axis=-1, keepdims=True)
    second = jnp.mean(scaled * normed, axis=-1, keepdims=True)
    return (scaled - first - normed * second) * inverse


def column_sum(values):
    return jnp.sum(values.astype(F32), axis=0, keepdims=True)


def dense_kernel(chunks, steps, *refs):
    att = refs[:chunks]
    x_ref, cot_ref, wout_ref, up_ref, down_ref, bup_ref, misc_ref = refs[chunks : chunks + 7]
    outs = refs[chunks + 7 :]
    out_ref, gres_ref = outs[:2]
    gatt = outs[2 : 2 + chunks]
    gout = outs[2 + chunks : 2 + 2 * chunks]
    gud_ref, gbup_ref, small_ref = outs[2 + 2 * chunks : 5 + 2 * chunks]
    (
        normed, inverse, flow, flow_t, acc, gffn, gffn_t, hidden, slope, gpre
    ) = outs[5 + 2 * chunks :]
    step = pl.program_id(0)
    seqs, rows, width = cot_ref.shape
    total = seqs * rows
    span = width // chunks
    bias_one, bias_two = misc_ref[0:1, :], misc_ref[1:2, :]
    gain_one, gain_two = misc_ref[2:3, :], misc_ref[3:4, :]
    shift_one, shift_two = misc_ref[4:5, :], misc_ref[5:6, :]
    parts = [(first, first // rows, first % rows) for first in range(0, total, RC)]

    @pl.when(step == 0)
    def _():
        for first, s, row in parts:
            block = slice(first, first + RC)
            branch = bias_one
            for j in range(chunks):
                branch = branch + nt(
                    att[j][s, row : row + RC, :], wout_ref[:, j * span : (j + 1) * span]
                )
            n_one, inv = norm_stats(
                x_ref[s, HALF + row : HALF + row + RC, :].astype(F32) + branch
            )
            normed[block, :] = n_one
            inverse[block, :] = inv
            low = (n_one * gain_one + shift_one).astype(BF)
            flow[block, :] = low
            flow_t[:, block] = low.T
            acc[block, :] = jnp.zeros((RC, width), F32)

    @pl.when(step < steps)
    def _():
        for first, s, row in parts:
            block = slice(first, first + RC)
            pre = nn(flow[block, :], up_ref[...]) + bup_ref[...]
            cdf = 0.5 * (1.0 + lax.erf(pre * np.float32(np.sqrt(0.5))))
            pdf = jnp.exp(-0.5 * (pre * pre)) * np.float32(1.0 / np.sqrt(2.0 * np.pi))
            low = (pre * cdf).astype(BF)
            hidden[step, block, :] = low
            slope[step, block, :] = cdf + pre * pdf
            acc[block, :] += nt(low, down_ref[...])

    @pl.when(step == steps)
    def _():
        small_ref[...] = jnp.zeros_like(small_ref)
        for first, s, row in parts:
            block = slice(first, first + RC)
            first_out = normed[block, :] * gain_one + shift_one
            n_two, inv = norm_stats(first_out + (acc[block, :] + bias_two))
            out_ref[s, row : row + RC, :] = (n_two * gain_two + shift_two).astype(BF)
            grad = cot_ref[s, row : row + RC, :].astype(F32)
            second = norm_back(grad, n_two, inv, gain_two)
            acc[block, :] = second
            low = second.astype(BF)
            gffn[block, :] = low
            gffn_t[:, block] = low.T
            small_ref[1:2, :] += column_sum(low)
            small_ref[3:4, :] += column_sum(grad * n_two)
            small_ref[5:6, :] += column_sum(grad)

    @pl.when(step >= steps)
    def _():
        which = 2 * steps - 1 - step
        bias_sum = jnp.zeros((1, FB), F32)
        for first, s, row in parts:
            block = slice(first, first + RC)
            grad = nn(gffn[block, :], down_ref[...])
            low = (grad * slope[which, block, :]).astype(BF)
            gpre[block, :] = low
            bias_sum = bias_sum + column_sum(low)
            acc[block, :] += nt(low, up_ref[...])
        gbup_ref[...] = bias_sum
        lead = (gud_ref.shape[0], gud_ref.shape[2], FB)
        gud_ref[:, 0] = nn(flow_t[...], gpre[...]).astype(BF).reshape(lead)
        gud_ref[:, 1] = nn(gffn_t[...], hidden[which]).astype(BF).reshape(lead)

    @pl.when(step == 2 * steps - 1)
    def _():
        for first, s, row in parts:
            block = slice(first, first + RC)
            grad = acc[block, :]
            n_one = normed[block, :]
            back = norm_back(grad, n_one, inverse[block, :], gain_one)
            gres_ref[s, row : row + RC, :] = back
            low = back.astype(BF)
            flow_t[:, block] = low.T
            small_ref[0:1, :] += column_sum(low)
            small_ref[2:3, :] += column_sum(grad * n_one)
            small_ref[4:5, :] += column_sum(grad)
            for j in range(chunks):
                gatt[j][s, row : row + RC, :] = nn(
                    low, wout_ref[:, j * span : (j + 1) * span]
                ).astype(BF)
        for j in range(chunks):
            gout[j][...] = nn(flow_t[...], att[j][...].reshape(total, span)).astype(BF)


def dense(att, x_wide, cot, weights, bias_up, misc, hidden_units, row_blocks):
    chunks = len(att)
    seqs, rows, width = cot.shape
    total = seqs * rows
    span = width // chunks
    steps = hidden_units // FB

    def which(i):
        return jnp.where(i < steps, i, 2 * steps - 1 - i)

    def back(i):
        return jnp.where(i < steps, steps - 1, 2 * steps - 1 - i)

    lead = width // row_blocks
    out_shape = (
        [
            jax.ShapeDtypeStruct((seqs, rows, width), BF),
            jax.ShapeDtypeStruct((seqs, rows, width), F32),
        ]
        + [jax.ShapeDtypeStruct((seqs, rows, span), BF)] * chunks
        + [jax.ShapeDtypeStruct((width, span), BF)] * chunks
        + [
            jax.ShapeDtypeStruct((row_blocks, 2, lead, hidden_units), BF),
            jax.ShapeDtypeStruct((1, hidden_units), F32),
            jax.ShapeDtypeStruct((8, width), F32),
        ]
    )
    out_specs = [once(o.shape) for o in out_shape[: 2 + 2 * chunks]] + [
        pl.BlockSpec((row_blocks, 2, lead, FB), lambda i: (0, 0, 0, back(i))),
        pl.BlockSpec((1, FB), lambda i: (0, back(i))),
        once((8, width)),
    ]
    out = pl.pallas_call(
        partial(dense_kernel, chunks, steps),
        grid=(2 * steps,),
        in_specs=[once(a.shape) for a in att]
        + [
            once(x_wide.shape),
            once(cot.shape),
            pl.BlockSpec(
                (width, width),
                lambda i: (0, 2 * hidden_units // width),
                pipeline_mode=pl.Buffered(1),
            ),
            pl.BlockSpec((width, FB), lambda i: (0, which(i))),
            pl.BlockSpec((width, FB), lambda i: (0, steps + which(i))),
            pl.BlockSpec((1, FB), lambda i: (0, which(i))),
            once(misc.shape),
        ],
        out_specs=out_specs,
        out_shape=out_shape,
        scratch_shapes=[
            pltpu.VMEM((total, width), F32),
            pltpu.VMEM((total, 1), F32),
            pltpu.VMEM((total, width), BF),
            pltpu.VMEM((width, total), BF),
            pltpu.VMEM((total, width), F32),
            pltpu.VMEM((total, width), BF),
            pltpu.VMEM((width, total), BF),
            pltpu.VMEM((steps, total, FB), BF),
            pltpu.VMEM((steps, total, FB), F32),
            pltpu.VMEM((total, FB), BF),
        ],
        compiler_params=params(60),
        cost_estimate=cost(
            12 * total * width * hidden_units + 6 * total * width * width, 48, total * hidden_units
        ),
    )(*att, x_wide, cot, weights, weights, weights, bias_up, misc)
    return (
        out[0], out[1], out[2 : 2 + chunks], out[2 + chunks : 2 + 2 * chunks],
        out[-3], out[-2], out[-1],
    )


def gather_back_kernel(
    blocks, groups, first_chunk, offs, *refs
):
    dk_ref, dv_ref, dq_ref, proj_k, proj_v = refs[:5]
    dps = refs[5 : 5 + blocks]
    taps_ref, same_ref, xt_ref, w_ref, gout_ref, gx_in = refs[5 + blocks : 11 + blocks]
    outs = refs[11 + blocks :]
    gws = outs[:groups]
    gx_ref, small_ref, plain, spread, low_q, low_k, low_v, stage = outs[groups:]
    seqs, wide, span = dk_ref.shape
    rows = wide - 2 * HALF
    far_rows = dps[0].shape[2]
    small_ref[...] = jnp.zeros_like(small_ref)
    for c, (near, proj, low) in enumerate(((dk_ref, proj_k, low_k), (dv_ref, proj_v, low_v))):
        for s in range(seqs):
            for half in range(span // PAIR):
                lanes = slice(half * PAIR, (half + 1) * PAIR)
                plain[...] = proj[0, s, :, lanes].astype(F32)
                spread[...] = near[s, :, lanes]
                pooled = dps[0][c, s, :, lanes].astype(F32)
                for n in range(1, blocks):
                    pooled = pooled + dps[n][c, s, :, lanes].astype(F32)
                pooled = pooled.astype(BF).astype(F32)
                for r in range(TAPS):
                    place = pl.ds(HALF - MARGIN + r, far_rows, stride=STRIDE)
                    masked = pooled * same_ref[s, :, r : r + 1]
                    row = 8 + 8 * c + r
                    small_ref[row : row + 1, lanes] += column_sum(masked * plain[place, :])
                    spread[place, :] = spread[place, :] + taps_ref[c, r : r + 1, lanes] * masked
                made = spread[...].astype(BF)
                low[s * wide : (s + 1) * wide, lanes] = made
                small_ref[1 + c : 2 + c, lanes] += column_sum(made)
    for s in range(seqs):
        base = s * wide
        low_q[base : base + HALF, :] = jnp.zeros((HALF, span), BF)
        low_q[base + HALF : base + HALF + rows, :] = dq_ref[s]
        low_q[base + HALF + rows : base + wide, :] = jnp.zeros((HALF, span), BF)
        small_ref[0:1, :] += column_sum(dq_ref[s])
        grad = (
            nt(low_q[base : base + wide, :], w_ref[0])
            + nt(low_k[base : base + wide, :], w_ref[1])
            + nt(low_v[base : base + wide, :], w_ref[2])
        )
        gx_ref[s] = grad if first_chunk else gx_in[s] + grad
    heads = span // HEAD_DIM
    lane = lax.broadcasted_iota(jnp.int32, (1, PAIR), 1) < HEAD_DIM
    width = xt_ref.shape[0]
    for u in range(heads // 2):
        lanes = slice(u * PAIR, (u + 1) * PAIR)
        stage_q = nn(xt_ref[...], low_q[:, lanes])
        stage_k = nn(xt_ref[...], low_k[:, lanes])
        stage_v = nn(xt_ref[...], low_v[:, lanes])
        stage_o = gout_ref[:, lanes].astype(F32)
        for odd in range(2):
            t = 2 * u + odd
            if odd == 0:
                one = jnp.where(lane, stage_q, pltpu.roll(stage_k, HEAD_DIM, 1))
                two = jnp.where(lane, stage_v, pltpu.roll(stage_o, HEAD_DIM, 1))
            else:
                one = jnp.where(lane, pltpu.roll(stage_q, HEAD_DIM, 1), stage_k)
                two = jnp.where(lane, pltpu.roll(stage_v, HEAD_DIM, 1), stage_o)
            stage[t, :, :PAIR] = one.astype(BF)
            stage[t, :, PAIR:] = two.astype(BF)
    height = gws[0].shape[2]
    number = 0
    for group in gws:
        for n in range(group.shape[0]):
            place = pl.ds(pl.multiple_of(offs[number], 16), height)
            group[n] = stage[:, place, :]
            number += 1


def gather_back(first_chunk, chunk, offs, group_sizes, near, dps, proj, taps, same, xt, w, gout, gx):
    dq, dk, dv = near
    seqs, wide, span = dk.shape
    width = xt.shape[0]
    blocks, far_rows = len(dps), dps[0].shape[2]
    height = width // sum(group_sizes)
    heads = span // HEAD_DIM
    gx_block = (seqs, 8, width) if first_chunk else (seqs, wide, width)
    out = pl.pallas_call(
        partial(gather_back_kernel, blocks, len(group_sizes), first_chunk),
        grid_spec=pltpu.PrefetchScalarGridSpec(
            num_scalar_prefetch=1,
            grid=(1,),
            in_specs=[
                once(dk.shape), once(dv.shape), once(dq.shape),
                pl.BlockSpec((1, seqs, wide, span), lambda i, o: (1, 0, 0, 0)),
                pl.BlockSpec((1, seqs, wide, span), lambda i, o: (2, 0, 0, 0)),
            ]
            + [once(d.shape) for d in dps]
            + [
                pl.BlockSpec((2, 8, span), lambda i, o: (0, 0, chunk)),
                once(same.shape), once(xt.shape), once(w.shape), once(gout.shape),
                once(gx_block),
            ],
            out_specs=[once((size, heads, height, 4 * HEAD_DIM)) for size in group_sizes]
            + [once((seqs, wide, width)), once((24, span))],
            scratch_shapes=[
                pltpu.VMEM((wide, PAIR), F32),
                pltpu.VMEM((wide, PAIR), F32),
                pltpu.VMEM((seqs * wide, span), BF),
                pltpu.VMEM((seqs * wide, span), BF),
                pltpu.VMEM((seqs * wide, span), BF),
                pltpu.VMEM((heads, width, 4 * HEAD_DIM), BF),
            ],
        ),
        out_shape=[
            jax.ShapeDtypeStruct((size, heads, height, 4 * HEAD_DIM), BF) for size in group_sizes
        ]
        + [
            jax.ShapeDtypeStruct((seqs, wide, width), F32),
            jax.ShapeDtypeStruct((24, span), F32),
        ],
        compiler_params=params(48),
        cost_estimate=cost(12 * seqs * wide * width * span, 16),
    )(offs, dk, dv, dq, proj, proj, *dps, taps, same, xt, w, gout, gx)
    return out[: len(group_sizes)], out[-2], out[-1]


def cycle(values, axis, shift):
    count = lax.axis_size(axis)
    return lax.ppermute(values, axis, [(i, (i + shift) % count) for i in range(count)])


def swap(values, axis, mask):
    count = lax.axis_size(axis)
    return lax.ppermute(values, axis, [(i, i ^ mask) for i in range(count)])


def shift_right(rows):
    count = lax.axis_size("tp")
    return lax.ppermute(rows, "tp", [(i, i + 1) for i in range(count - 1)])


def shift_left(rows):
    count = lax.axis_size("tp")
    return lax.ppermute(rows, "tp", [(i + 1, i) for i in range(count - 1)])


def gather_pieces(shard):
    mine = lax.axis_index("fsdp")
    rows = shard.shape[0]
    half = rows // 2
    across = swap(shard, "fsdp", 2)
    along = swap(shard, "fsdp", 4)
    corner = [swap(across[:half], "fsdp", 4), swap(along[half:], "fsdp", 2)]
    own = [shard, across, along] + corner
    other = [swap(piece, "fsdp", 1) for piece in own]
    place = [
        (mine ^ mask) * rows + extra
        for core in (0, 1)
        for mask, extra in ((core, 0), (2 + core, 0), (4 + core, 0), (6 + core, 0), (6 + core, half))
    ]
    return own + other, jnp.stack(place).astype(jnp.int32)


def add_low(first, *others):
    total = first.astype(F32)
    for other in others:
        total = total + other.astype(F32)
    return total


def scatter_chain(keep, send):
    merged = add_low(keep, swap(send, "fsdp", 1)).astype(BF)
    merged = add_low(merged[0], *[swap(merged[n], "fsdp", 2 * n) for n in (1, 2, 3)]).astype(BF)
    return scatter_tp(merged)


def scatter_tp(blocks):
    count = lax.axis_size("tp")
    me = lax.axis_index("tp")

    def pick(d):
        return lax.dynamic_index_in_dim(blocks, (me + d) % count, 0, keepdims=False)

    return add_low(pick(0), *[cycle(pick(d), "tp", d) for d in range(1, count)])


def sum_everywhere(values):
    for axis in ("fsdp", "tp"):
        mask = 1
        while mask < lax.axis_size(axis):
            values = values + swap(values, axis, mask)
            mask *= 2
    return values


def split_three(values):
    high = lax.reduce_precision(values, 8, 7)
    rest = values - high
    middle = lax.reduce_precision(rest, 8, 7)
    return jnp.stack([high, middle, rest - middle]).astype(BF)


def body(
    inputs, segments, w_qkv, qkv_bias, pool_kernel, w_out, out_bias,
    w_up, up_bias, w_down, norm_gains, norm_shifts, cotangent,
):
    rows, seqs, width = inputs.shape
    tp = lax.axis_size("tp")
    fsdp = lax.axis_size("fsdp")
    place = lax.axis_index("tp")
    shard_rows = w_qkv.shape[0]
    local = w_qkv.shape[2]
    chunks = local // HEAD_DIM
    span = tp * HEAD_DIM
    hidden_local = w_up.shape[1]
    hidden_units = hidden_local * tp
    far_rows = rows // STRIDE
    fast = fsdp == 8 and shard_rows % 32 == 0

    bias_values = jnp.concatenate(
        [qkv_bias.reshape(-1), pool_kernel.reshape(-1), up_bias.reshape(-1)]
    )
    biases = split_three(bias_values)
    extra = -(-biases.size // (3 * local))
    packed = jnp.concatenate(
        [
            w_qkv.reshape(shard_rows, 3 * local),
            jnp.pad(biases.reshape(-1), (0, extra * 3 * local - biases.size)).reshape(
                extra, 3 * local
            ),
        ],
        axis=0,
    )
    columns = lax.all_gather(packed, "tp", axis=0, tiled=False)
    qkv_rows = (
        columns[:, :shard_rows]
        .reshape(tp, shard_rows, 3, chunks, HEAD_DIM)
        .transpose(1, 2, 3, 0, 4)
        .reshape(shard_rows, 3 * width)
    )
    if fast:
        pieces, offs = gather_pieces(qkv_rows)
    else:
        pieces = [lax.all_gather(qkv_rows, "fsdp", axis=0, tiled=True)]
        offs = jnp.zeros((1,), jnp.int32)
    whole_bias = jnp.sum(
        columns[:, shard_rows:].reshape(tp, -1)[:, : biases.size].reshape(tp, 3, -1).astype(F32),
        axis=1,
    )
    lead = (3 + 2 * TAPS) * local
    featured = (
        whole_bias[:, :lead]
        .reshape(tp, 3 + 2 * TAPS, chunks, HEAD_DIM)
        .transpose(1, 2, 0, 3)
        .reshape(3 + 2 * TAPS, width)
    )
    bias_qkv = featured[:3, None, :]
    taps = jnp.pad(featured[3:].reshape(2, TAPS, width), ((0, 0), (0, 8 - TAPS), (0, 0)))
    bias_up = whole_bias[:, lead:].reshape(1, hidden_units)

    columns, later = lax.optimization_barrier(
        (columns, jnp.concatenate([w_up, w_down, w_out], axis=1))
    )
    rest = lax.all_gather(later, "tp", axis=0, tiled=False)
    rest = jnp.concatenate(
        [
            rest[:, :, :hidden_local].transpose(1, 0, 2).reshape(shard_rows, hidden_units),
            rest[:, :, hidden_local : 2 * hidden_local]
            .transpose(1, 0, 2)
            .reshape(shard_rows, hidden_units),
            rest[:, :, 2 * hidden_local :]
            .reshape(tp, shard_rows, chunks, HEAD_DIM)
            .transpose(1, 2, 0, 3)
            .reshape(shard_rows, width),
        ],
        axis=1,
    )
    weights = lax.all_gather(rest, "fsdp", axis=0, tiled=True)

    left = shift_right(inputs[rows - HALF :])
    right = shift_left(inputs[:HALF])
    x_wide = jnp.concatenate([left, inputs, right], axis=0).transpose(1, 0, 2)
    wide = rows + 2 * HALF
    x_cols = x_wide.reshape(seqs * wide, width).T
    cot = cotangent.transpose(1, 0, 2)

    seg_rows = segments.T
    padded = jnp.pad(seg_rows, ((0, 0), (HALF, HALF)), constant_values=-1)
    seg_keys = lax.dynamic_slice_in_dim(padded, place * rows, wide, 1)
    seg_own = seg_keys[:, HALF : HALF + rows]
    centers = seg_rows[:, ::STRIDE].reshape(seqs, tp, far_rows)
    centers_cycle = jnp.concatenate(
        [
            lax.dynamic_index_in_dim(centers, (place - d) % tp, 1, keepdims=True)
            for d in range(tp)
        ],
        axis=1,
    ).reshape(seqs, 1, tp * far_rows)
    segs = (seg_own[:, :, None], seg_keys[:, None, :], centers_cycle)
    own_centers = seg_own[:, ::STRIDE]
    same = jnp.stack(
        [
            seg_keys[:, HALF - MARGIN + r : HALF - MARGIN + r + rows : STRIDE][:, :far_rows]
            == own_centers
            for r in range(TAPS)
        ]
        + [jnp.zeros_like(own_centers, dtype=bool)] * (8 - TAPS),
        axis=2,
    ).astype(F32)

    made = [
        project(j, chunks, pieces, offs, x_wide, bias_qkv, taps, same, far_rows)
        for j in range(chunks)
    ]
    slots = [
        [pooled] + [cycle(pooled, "tp", d) for d in range(1, tp)] for _, pooled, _ in made
    ]
    att = [attend_forward(made[j][0], slots[j], segs) for j in range(chunks)]
    misc = jnp.concatenate([out_bias, norm_gains, norm_shifts, jnp.zeros((2, width), F32)])
    row_blocks = fsdp if shard_rows % 16 == 0 else 1
    outputs, grad_residual, grad_att, grad_out, gud, grad_up_bias, small = dense(
        att, x_wide, cot, weights, bias_up, misc, hidden_units, row_blocks
    )
    if row_blocks == 1:
        gud = gud.reshape(2, fsdp, shard_rows, hidden_units).transpose(1, 0, 2, 3)
    gud = lax.psum_scatter(gud, "fsdp", scatter_dimension=0, tiled=False)
    gud = gud.reshape(2, shard_rows, tp, hidden_local).transpose(2, 0, 1, 3)
    gud = lax.psum_scatter(gud, "tp", scatter_dimension=0, tiled=False).astype(F32)

    if fast:
        mine = lax.axis_index("fsdp")
        group_sizes = (4, 4)
        out_offs = jnp.stack(
            [(mine ^ m) * shard_rows for m in (0, 2, 4, 6, 1, 3, 5, 7)]
        ).astype(jnp.int32)
    else:
        group_sizes = (1,)
        out_offs = jnp.zeros((1,), jnp.int32)
    backs = [attend_backward(made[j][0], slots[j], segs, grad_att[j]) for j in range(chunks)]
    gx = jnp.zeros((seqs, 8, width), F32)
    weight_grads, smalls = [], []
    for j in range(chunks):
        dq, dk, dv, dps = backs[j]
        arrived = [dps[0]] + [cycle(dps[d], "tp", -d) for d in range(1, tp)]
        groups, gx, small_j = gather_back(
            j == 0, j, out_offs, group_sizes, (dq, dk, dv), arrived,
            made[j][0], taps, same, x_cols, made[j][2], grad_out[j], gx,
        )
        smalls.append(small_j)
        if fast:
            weight_grads.append(scatter_chain(*groups))
        else:
            whole = groups[0].reshape(tp, fsdp, shard_rows, 4 * HEAD_DIM).transpose(1, 0, 2, 3)
            whole = lax.psum_scatter(whole, "fsdp", scatter_dimension=0, tiled=False)
            weight_grads.append(scatter_tp(whole))

    to_left = shift_left(gx[:, :HALF].astype(BF))
    to_right = shift_right(gx[:, HALF + rows :].astype(BF))
    middle = gx[:, HALF : HALF + rows] + grad_residual
    middle = middle.at[:, :HALF].add(to_right.astype(F32))
    middle = middle.at[:, rows - HALF :].add(to_left.astype(F32))
    grad_inputs = middle.transpose(1, 0, 2)

    small_rows = jnp.concatenate(smalls, axis=1)
    sums = sum_everywhere(
        jnp.concatenate(
            [small, small_rows, grad_up_bias.reshape(-1, width)],
            axis=0,
        )
    )
    grad_out_bias, grad_gains, grad_shifts = sums[0:2], sums[2:4], sums[4:6]
    mixed = lax.dynamic_index_in_dim(
        sums[8:32].reshape(24, chunks, tp, HEAD_DIM), place, 2, keepdims=False
    ).reshape(24, local)
    grad_up = lax.dynamic_slice_in_dim(sums[32:].reshape(-1), place * hidden_local, hidden_local)

    stacked = jnp.stack(
        [g.reshape(shard_rows, 4, HEAD_DIM) for g in weight_grads], axis=2
    ).reshape(shard_rows, 4, local)
    return (
        outputs.transpose(1, 0, 2),
        grad_inputs,
        stacked[:, :3],
        mixed[:3],
        jnp.stack([mixed[8 : 8 + TAPS], mixed[16 : 16 + TAPS]]),
        stacked[:, 3],
        grad_out_bias,
        gud[0],
        grad_up,
        gud[1],
        grad_gains,
        grad_shifts,
    )


def solution(mesh):
    placed = (
        P("tp", "fsdp", None),
        P(None, "fsdp"),
        P("fsdp", None, "tp"),
        P(None, "tp"),
        P(None, None, "tp"),
        P("fsdp", "tp"),
        P(),
        P("fsdp", "tp"),
        P("tp"),
        P("fsdp", "tp"),
        P(),
        P(),
        P("tp", "fsdp", None),
    )
    return jax.shard_map(
        body,
        mesh=mesh,
        in_specs=placed,
        out_specs=(
            P("tp", "fsdp", None),
            P("tp", "fsdp", None),
            P("fsdp", None, "tp"),
            P(None, "tp"),
            P(None, None, "tp"),
            P("fsdp", "tp"),
            P(),
            P("fsdp", "tp"),
            P("tp"),
            P("fsdp", "tp"),
            P(),
            P(),
        ),
        check_vma=False,
    )
```

```python
from functools import partial

import jax
import jax.numpy as jnp
import numpy as np
from jax import lax
from jax.experimental import pallas as pl
from jax.experimental.pallas import tpu as pltpu
from jax.sharding import PartitionSpec as P

HEAD_DIM = 64
HALF = 64
STRIDE = 4
TAPS = 5
MARGIN = TAPS // 2
PAIR = 2 * HEAD_DIM
QB = 128
NEAR = QB + 2 * HALF
EXTRA = 16
RC = 256
EPSILON = 1e-05
NEG = -1e30
SCALE = HEAD_DIM**-0.5
BF = jnp.bfloat16
F32 = jnp.float32
MIB = 2**20


def nt(a, b):
    return lax.dot_general(a, b, (((1,), (1,)), ((), ())), preferred_element_type=F32)


def nn(a, b):
    return lax.dot_general(a, b, (((1,), (0,)), ((), ())), preferred_element_type=F32)


def tn(a, b):
    return lax.dot_general(a, b, (((0,), (0,)), ((), ())), preferred_element_type=F32)


def params(mib):
    return pltpu.CompilerParams(vmem_limit_bytes=mib * MIB)


def cost(flops, mib, trans=0):
    return pl.CostEstimate(flops=1, bytes_accessed=1, transcendentals=0)


def once(shape):
    zeros = (0,) * len(shape)
    return pl.BlockSpec(shape, lambda *_: zeros, pipeline_mode=pl.Buffered(1))


def project_kernel(count, offs, *refs):
    pieces = refs[:count]
    x_ref, bias_ref, taps_ref, same_ref, out_ref, pooled_ref, w_ref, plain = refs[count:]
    part = pl.program_id(0)
    for n in range(count):
        rows = pieces[n].shape[0]
        w_ref[0, pl.ds(pl.multiple_of(offs[n], 16), rows), :] = pieces[n][...]
    seqs, wide, _ = x_ref.shape
    far_rows = pooled_ref.shape[2]
    for s in range(seqs):
        made = (nn(x_ref[s], w_ref[0]) + bias_ref[0]).astype(BF)
        out_ref[0, s] = made
        for half in range(plain.shape[1]):
            plain[s, half] = made[:, half * PAIR : (half + 1) * PAIR].astype(F32)

    @pl.when(part > 0)
    def _():
        for s in range(seqs):
            for half in range(plain.shape[1]):
                lanes = slice(half * PAIR, (half + 1) * PAIR)
                total = jnp.zeros((far_rows, PAIR), F32)
                for r in range(TAPS):
                    rows = plain[s, half, pl.ds(HALF - MARGIN + r, far_rows, stride=STRIDE), :]
                    total = total + taps_ref[0, r : r + 1, lanes] * rows * same_ref[
                        s, :, r : r + 1
                    ]
                pooled_ref[0, s, :, lanes] = total.astype(BF)


def project(chunk, chunks, pieces, offs, x_wide, bias, taps, same, far_rows):
    seqs, wide, width = x_wide.shape
    span = width // chunks

    def piece_spec(piece):
        return pl.BlockSpec((piece.shape[0], span), lambda c, o: (0, c * chunks + chunk))

    def kv(c):
        return jnp.maximum(c - 1, 0)

    return pl.pallas_call(
        partial(project_kernel, len(pieces)),
        grid_spec=pltpu.PrefetchScalarGridSpec(
            num_scalar_prefetch=1,
            grid=(3,),
            in_specs=[piece_spec(p) for p in pieces]
            + [
                once(x_wide.shape),
                pl.BlockSpec((1, 1, span), lambda c, o: (c, 0, chunk)),
                pl.BlockSpec((1, 8, span), lambda c, o: (kv(c), 0, chunk)),
                once(same.shape),
            ],
            out_specs=[
                pl.BlockSpec((1, seqs, wide, span), lambda c, o: (c, 0, 0, 0)),
                pl.BlockSpec((1, seqs, far_rows, span), lambda c, o: (kv(c), 0, 0, 0)),
                pl.BlockSpec((1, width, span), lambda c, o: (c, 0, 0)),
            ],
            scratch_shapes=[pltpu.VMEM((seqs, span // PAIR, wide, PAIR), F32)],
        ),
        out_shape=[
            jax.ShapeDtypeStruct((3, seqs, wide, span), BF),
            jax.ShapeDtypeStruct((2, seqs, far_rows, span), BF),
            jax.ShapeDtypeStruct((3, width, span), BF),
        ],
        compiler_params=params(32),
        cost_estimate=cost(6 * seqs * wide * width * span, 8),
    )(offs, *pieces, x_wide, bias, taps, same)


def fill_masks(segq_ref, segk_ref, cen_ref, near_bias, far_bias):
    rows = segq_ref.shape[1]
    shape = (QB, NEAR)
    gap = lax.broadcasted_iota(jnp.int32, shape, 1) - lax.broadcasted_iota(jnp.int32, shape, 0)
    band = (gap >= 0) & (gap <= 2 * HALF)
    for first in range(0, rows, QB):
        own = segq_ref[0, first : first + QB, :]
        keys = segk_ref[0, :, first : first + NEAR]
        near_bias[first : first + QB, :] = jnp.where(band & (own == keys), 0.0, NEG)
        far_bias[first : first + QB, :] = jnp.where(own == cen_ref[0], 0.0, NEG)


def head_mask(head):
    lane = lax.broadcasted_iota(jnp.int32, (1, PAIR), 1)
    return lane < HEAD_DIM if head == 0 else lane >= HEAD_DIM


def softmax_block(query, keys_near, keys_far, bias_near, bias_far):
    near = nt(query, keys_near) + bias_near
    far = nt(query, keys_far) + bias_far
    top = jnp.maximum(
        jnp.max(near, axis=-1, keepdims=True), jnp.max(far, axis=-1, keepdims=True)
    )
    near = jnp.exp(near - top)
    far = jnp.exp(far - top)
    total = jnp.sum(near, axis=-1, keepdims=True) + jnp.sum(far, axis=-1, keepdims=True)
    inverse = 1.0 / total
    return near * inverse, far * inverse


def join_slots(slots, joined):
    rows = slots[0].shape[1]
    for n, slot in enumerate(slots):
        joined[n * rows : (n + 1) * rows, :] = slot[0]


def attend_forward_kernel(blocks, q_ref, k_ref, v_ref, *refs):
    pk, pv = refs[:blocks], refs[blocks : 2 * blocks]
    segq, segk, cen, out_ref, near_bias, far_bias, far_keys, far_values = refs[2 * blocks :]

    @pl.when(pl.program_id(1) == 0)
    def _():
        fill_masks(segq, segk, cen, near_bias, far_bias)

    join_slots(pk, far_keys)
    join_slots(pv, far_values)
    for first in range(0, out_ref.shape[1], QB):
        block = slice(first, first + QB)
        span = slice(first, first + NEAR)
        query = q_ref[0, HALF + first : HALF + first + QB, :] * BF(SCALE)
        halves = []
        for head in range(2):
            picked = jnp.where(head_mask(head), query, BF(0))
            near, far = softmax_block(
                picked, k_ref[0, span, :], far_keys[...], near_bias[block, :], far_bias[block, :]
            )
            halves.append(
                nn(near.astype(BF), v_ref[0, span, :]) + nn(far.astype(BF), far_values[...])
            )
        out_ref[0, block, :] = jnp.where(head_mask(0), halves[0], halves[1]).astype(BF)


def attend_backward_kernel(blocks, q_ref, k_ref, v_ref, *refs):
    pk, pv = refs[:blocks], refs[blocks : 2 * blocks]
    segq, segk, cen, grad_ref, dq_ref, dk_ref, dv_ref = refs[2 * blocks : 2 * blocks + 7]
    dp_refs = refs[2 * blocks + 7 : 3 * blocks + 7]
    near_bias, far_bias, far_keys, far_values, far_probs, far_grads = refs[3 * blocks + 7 :]

    @pl.when(pl.program_id(1) == 0)
    def _():
        fill_masks(segq, segk, cen, near_bias, far_bias)

    rows = dq_ref.shape[1]
    join_slots(pk, far_keys)
    join_slots(pv, far_values)
    dk_ref[...] = jnp.zeros_like(dk_ref)
    dv_ref[...] = jnp.zeros_like(dv_ref)
    pieces = []
    for head in range(2):
        mask = head_mask(head)
        for first in range(0, rows, QB):
            block = slice(first, first + QB)
            span = slice(first, first + NEAR)
            query = jnp.where(
                mask, q_ref[0, HALF + first : HALF + first + QB, :] * BF(SCALE), BF(0)
            )
            grad = jnp.where(mask, grad_ref[0, block, :], BF(0))
            near, far = softmax_block(
                query, k_ref[0, span, :], far_keys[...], near_bias[block, :], far_bias[block, :]
            )
            grad_near = nt(grad, v_ref[0, span, :])
            grad_far = nt(grad, far_values[...])
            row_dot = jnp.sum(near * grad_near, axis=-1, keepdims=True) + jnp.sum(
                far * grad_far, axis=-1, keepdims=True
            )
            ds_near = (near * (grad_near - row_dot)).astype(BF)
            ds_far = (far * (grad_far - row_dot)).astype(BF)
            far_probs[block, :] = far.astype(BF)
            far_grads[block, :] = ds_far
            dq = (nn(ds_near, k_ref[0, span, :]) + nn(ds_far, far_keys[...])) * SCALE
            if head == 0:
                dq_ref[0, block, :] = dq.astype(BF)
            else:
                dq_ref[0, block, :] = jnp.where(mask, dq.astype(BF), dq_ref[0, block, :])
            dk_ref[0, span, :] += tn(ds_near, query)
            dv_ref[0, span, :] += tn(near.astype(BF), grad)
        query = jnp.where(mask, q_ref[0, HALF : HALF + rows, :] * BF(SCALE), BF(0))
        grad = jnp.where(mask, grad_ref[0], BF(0))
        pieces.append((tn(far_grads[...], query), tn(far_probs[...], grad)))
    far_rows = dp_refs[0].shape[2]
    for n, ref in enumerate(dp_refs):
        span = slice(n * far_rows, (n + 1) * far_rows)
        for c in range(2):
            ref[c, 0] = jnp.where(head_mask(0), pieces[0][c][span], pieces[1][c][span]).astype(BF)


def attention_specs(wide, blocks, far_rows):
    def own(part):
        return pl.BlockSpec((None, 1, wide, PAIR), lambda s, h: (part, s, 0, h))

    def pooled(part):
        return pl.BlockSpec((None, 1, far_rows, PAIR), lambda s, h: (part, s, 0, h))

    rows = wide - 2 * HALF
    return (
        [own(0), own(1), own(2)]
        + [pooled(0)] * blocks
        + [pooled(1)] * blocks
        + [
            pl.BlockSpec((1, rows, 1), lambda s, h: (s, 0, 0)),
            pl.BlockSpec((1, 1, wide), lambda s, h: (s, 0, 0)),
            pl.BlockSpec((1, 1, blocks * far_rows), lambda s, h: (s, 0, 0)),
        ]
    )


def attention_scratch(rows, far_all):
    return [
        pltpu.VMEM((rows, NEAR), F32),
        pltpu.VMEM((rows, far_all), F32),
        pltpu.VMEM((far_all, PAIR), BF),
        pltpu.VMEM((far_all, PAIR), BF),
    ]


def attend_forward(proj, slots, segs):
    _, seqs, wide, span = proj.shape
    blocks, far_rows = len(slots), slots[0].shape[2]
    rows = wide - 2 * HALF
    cells = seqs * rows * (NEAR + blocks * far_rows) * (span // HEAD_DIM)
    return pl.pallas_call(
        partial(attend_forward_kernel, blocks),
        grid=(seqs, span // PAIR),
        in_specs=attention_specs(wide, blocks, far_rows),
        out_specs=pl.BlockSpec((1, rows, PAIR), lambda s, h: (s, 0, h)),
        out_shape=jax.ShapeDtypeStruct((seqs, rows, span), BF),
        scratch_shapes=attention_scratch(rows, blocks * far_rows),
        compiler_params=params(60),
        cost_estimate=cost(16 * 64 * cells, 8, cells),
    )(proj, proj, proj, *slots, *slots, *segs)


def attend_backward(proj, slots, segs, grad):
    _, seqs, wide, span = proj.shape
    blocks, far_rows = len(slots), slots[0].shape[2]
    rows = wide - 2 * HALF
    cells = seqs * rows * (NEAR + blocks * far_rows) * (span // HEAD_DIM)
    own_spec = pl.BlockSpec((1, rows, PAIR), lambda s, h: (s, 0, h))
    wide_spec = pl.BlockSpec((1, wide, PAIR), lambda s, h: (s, 0, h))
    wide_shape = jax.ShapeDtypeStruct((seqs, wide, span), F32)
    far_spec = pl.BlockSpec((2, 1, far_rows, PAIR), lambda s, h: (0, s, 0, h))
    far_shape = jax.ShapeDtypeStruct((2, seqs, far_rows, span), BF)
    out = pl.pallas_call(
        partial(attend_backward_kernel, blocks),
        grid=(seqs, span // PAIR),
        in_specs=attention_specs(wide, blocks, far_rows) + [own_spec],
        out_specs=[own_spec, wide_spec, wide_spec] + [far_spec] * blocks,
        out_shape=[jax.ShapeDtypeStruct((seqs, rows, span), BF), wide_shape, wide_shape]
        + [far_shape] * blocks,
        scratch_shapes=attention_scratch(rows, blocks * far_rows)
        + [pltpu.VMEM((rows, blocks * far_rows), BF)] * 2,
        compiler_params=params(60),
        cost_estimate=cost(40 * 64 * cells, 16, cells),
    )(proj, proj, proj, *slots, *slots, *segs, grad)
    return out[0], out[1], out[2], out[3:]


def norm_stats(residual):
    row_mean = jnp.mean(residual, axis=-1, keepdims=True)
    centered = residual - row_mean
    variance = jnp.mean(centered * centered, axis=-1, keepdims=True)
    inverse = lax.rsqrt(variance + EPSILON)
    return centered * inverse, inverse


def norm_back(grad, normed, inverse, gain):
    scaled = grad * gain
    first = jnp.mean(scaled, axis=-1, keepdims=True)
    second = jnp.mean(scaled * normed, axis=-1, keepdims=True)
    return (scaled - first - normed * second) * inverse


def column_sum(values):
    return jnp.sum(values.astype(F32), axis=0, keepdims=True)


def dense_kernel(chunks, steps, *refs):
    att = refs[:chunks]
    x_ref, cot_ref, wout_ref, up_blk, down_blk, bup_ref, misc_ref = refs[chunks : chunks + 7]
    outs = refs[chunks + 7 :]
    out_ref, gres_ref = outs[:2]
    gatt = outs[2 : 2 + chunks]
    gout = outs[2 + chunks : 2 + 2 * chunks]
    gud_ref, small_ref = outs[2 + 2 * chunks : 4 + 2 * chunks]
    (
        inverse, flow, flow_t, acc, gffn, gffn_t, hidden, slope, gpre
    ) = outs[4 + 2 * chunks :]
    step = pl.program_id(0)
    seqs, rows, width = cot_ref.shape
    total = seqs * rows
    span = width // chunks
    units = gpre.shape[1]
    up_ref = up_blk[...].reshape(width, units)
    down_ref = down_blk[...].reshape(width, units)
    bias_one, bias_two = misc_ref[0:1, :], misc_ref[1:2, :]
    gain_one, gain_two = misc_ref[2:3, :], misc_ref[3:4, :]
    shift_one, shift_two = misc_ref[4:5, :], misc_ref[5:6, :]
    parts = [(first, first // rows, first % rows) for first in range(0, total, RC)]

    @pl.when(step == 0)
    def _():
        for first, s, row in parts:
            block = slice(first, first + RC)
            branch = bias_one
            for j in range(chunks):
                branch = branch + nt(
                    att[j][s, row : row + RC, :], wout_ref[:, j * span : (j + 1) * span]
                )
            n_one, inv = norm_stats(
                x_ref[s, HALF + row : HALF + row + RC, :].astype(F32) + branch
            )
            gres_ref[s, row : row + RC, :] = n_one
            inverse[block, :] = inv
            low = (n_one * gain_one + shift_one).astype(BF)
            flow[block, :] = low
            flow_t[:, block] = low.T
            acc[block, :] = jnp.zeros((RC, width), F32)

    @pl.when(step < steps)
    def _():
        for first, s, row in parts:
            block = slice(first, first + RC)
            pre = nn(flow[block, :], up_ref) + bup_ref[...]
            cdf = 0.5 * (1.0 + lax.erf(pre * np.float32(np.sqrt(0.5))))
            pdf = jnp.exp(-0.5 * (pre * pre)) * np.float32(1.0 / np.sqrt(2.0 * np.pi))
            low = (pre * cdf).astype(BF)
            hidden[step, block, :] = low
            slope[step, block, :] = cdf + pre * pdf
            acc[block, :] += nt(low, down_ref)

    @pl.when(step == steps)
    def _():
        small_ref[...] = jnp.zeros_like(small_ref)
        for first, s, row in parts:
            block = slice(first, first + RC)
            first_out = gres_ref[s, row : row + RC, :] * gain_one + shift_one
            n_two, inv = norm_stats(first_out + (acc[block, :] + bias_two))
            out_ref[s, row : row + RC, :] = (n_two * gain_two + shift_two).astype(BF)
            grad = cot_ref[s, row : row + RC, :].astype(F32)
            second = norm_back(grad, n_two, inv, gain_two)
            acc[block, :] = second
            low = second.astype(BF)
            gffn[block, :] = low
            gffn_t[:, block] = low.T
            small_ref[1:2, :] += column_sum(low)
            small_ref[3:4, :] += column_sum(grad * n_two)
            small_ref[5:6, :] += column_sum(grad)

    @pl.when(step >= steps)
    def _():
        which = 2 * steps - 1 - step
        bias_sum = jnp.zeros((1, units), F32)
        for first, s, row in parts:
            block = slice(first, first + RC)
            grad = nn(gffn[block, :], down_ref)
            low = (grad * slope[which, block, :]).astype(BF)
            gpre[block, :] = low
            bias_sum = bias_sum + column_sum(low)
            acc[block, :] += nt(low, up_ref)
        height = gud_ref.shape[2] - EXTRA
        lead = (gud_ref.shape[0], height, units)
        gud_ref[:, 0, :height] = nn(flow_t[...], gpre[...]).astype(BF).reshape(lead)
        gud_ref[:, 1, :height] = nn(gffn_t[...], hidden[which]).astype(BF).reshape(lead)
        head = lax.broadcasted_iota(jnp.int32, (EXTRA, 1), 0) == 0
        extra = jnp.where(head, bias_sum, 0.0).astype(BF)
        for m in range(gud_ref.shape[0]):
            gud_ref[m, 0, height:] = extra
            gud_ref[m, 1, height:] = jnp.zeros((EXTRA, units), BF)

    @pl.when(step == 2 * steps - 1)
    def _():
        for first, s, row in parts:
            block = slice(first, first + RC)
            grad = acc[block, :]
            n_one = gres_ref[s, row : row + RC, :]
            back = norm_back(grad, n_one, inverse[block, :], gain_one)
            gres_ref[s, row : row + RC, :] = back
            low = back.astype(BF)
            flow_t[:, block] = low.T
            small_ref[0:1, :] += column_sum(low)
            small_ref[2:3, :] += column_sum(grad * n_one)
            small_ref[4:5, :] += column_sum(grad)
            for j in range(chunks):
                gatt[j][s, row : row + RC, :] = nn(
                    low, wout_ref[:, j * span : (j + 1) * span]
                ).astype(BF)
        for j in range(chunks):
            gout[j][...] = nn(flow_t[...], att[j][...].reshape(total, span)).astype(BF)


def dense(att, x_wide, cot, w_out, weights, bias_up, misc):
    chunks = len(att)
    seqs, rows, width = cot.shape
    total = seqs * rows
    span = width // chunks
    row_blocks, steps, height, units = weights.shape
    units //= 2

    def which(i):
        return jnp.where(i < steps, i, 2 * steps - 1 - i)

    def back(i):
        return jnp.where(i < steps, steps - 1, 2 * steps - 1 - i)

    out_shape = (
        [
            jax.ShapeDtypeStruct((seqs, rows, width), BF),
            jax.ShapeDtypeStruct((seqs, rows, width), F32),
        ]
        + [jax.ShapeDtypeStruct((seqs, rows, span), BF)] * chunks
        + [jax.ShapeDtypeStruct((width, span), BF)] * chunks
        + [
            jax.ShapeDtypeStruct((row_blocks, 2, height + EXTRA, steps * units), BF),
            jax.ShapeDtypeStruct((8, width), F32),
        ]
    )
    out_specs = [once(o.shape) for o in out_shape[: 2 + 2 * chunks]] + [
        pl.BlockSpec((row_blocks, 2, height + EXTRA, units), lambda i: (0, 0, 0, back(i))),
        once((8, width)),
    ]
    out = pl.pallas_call(
        partial(dense_kernel, chunks, steps),
        grid=(2 * steps,),
        in_specs=[once(a.shape) for a in att]
        + [
            once(x_wide.shape),
            once(cot.shape),
            once(w_out.shape),
            pl.BlockSpec((row_blocks, None, height, units), lambda i: (0, which(i), 0, 0)),
            pl.BlockSpec((row_blocks, None, height, units), lambda i: (0, which(i), 0, 1)),
            pl.BlockSpec((1, units), lambda i: (0, which(i))),
            once(misc.shape),
        ],
        out_specs=out_specs,
        out_shape=out_shape,
        scratch_shapes=[
            pltpu.VMEM((total, 1), F32),
            pltpu.VMEM((total, width), BF),
            pltpu.VMEM((width, total), BF),
            pltpu.VMEM((total, width), F32),
            pltpu.VMEM((total, width), BF),
            pltpu.VMEM((width, total), BF),
            pltpu.VMEM((steps, total, units), BF),
            pltpu.VMEM((steps, total, units), F32),
            pltpu.VMEM((total, units), BF),
        ],
        compiler_params=params(63),
        cost_estimate=cost(1, 1),
    )(*att, x_wide, cot, w_out, weights, weights, bias_up, misc)
    return (
        out[0], out[1], out[2 : 2 + chunks], out[2 + chunks : 2 + 2 * chunks], out[-2], out[-1]
    )


def gather_back_kernel(blocks, chunks, groups, offs, *refs):
    taken = 5 + blocks + 1
    per_chunk = [refs[n * taken : (n + 1) * taken] for n in range(chunks)]
    taps_ref, same_ref, xt_ref, more_ref = refs[chunks * taken : chunks * taken + 4]
    outs = refs[chunks * taken + 4 :]
    gws = outs[:groups]
    lows = outs[groups : groups + chunks]
    small, plain, spread, low_q, total, stage = outs[groups + chunks :]
    width = xt_ref.shape[0]
    seq = pl.program_id(0)
    wide, span = per_chunk[0][0].shape[1:]
    rows = wide - 2 * HALF
    far_rows = per_chunk[0][3].shape[2]

    @pl.when(seq == 0)
    def _():
        small[...] = jnp.zeros_like(small)
        total[...] = jnp.zeros_like(total)

    for n, chunk_refs in enumerate(per_chunk):
        dk_ref, dv_ref, dq_ref = chunk_refs[:3]
        dps = chunk_refs[3 : 3 + blocks]
        proj_k, proj_v = chunk_refs[3 + blocks : 5 + blocks]
        low = lows[n]
        base = n * span
        low_q[:HALF, :] = jnp.zeros((HALF, span), BF)
        low_q[HALF : HALF + rows, :] = dq_ref[0]
        low_q[HALF + rows :, :] = jnp.zeros((HALF, span), BF)
        small[0, 0:1, base : base + span] += column_sum(dq_ref[0])
        for c, (near, proj) in enumerate(((dk_ref, proj_k), (dv_ref, proj_v))):
            for half in range(span // PAIR):
                lanes = slice(half * PAIR, (half + 1) * PAIR)
                wider = slice(base + half * PAIR, base + (half + 1) * PAIR)
                plain[...] = proj[0, 0, :, lanes].astype(F32)
                spread[...] = near[0, :, lanes]
                pooled = dps[0][c, 0, :, lanes].astype(F32)
                for d in range(1, blocks):
                    pooled = pooled + dps[d][c, 0, :, lanes].astype(F32)
                pooled = pooled.astype(BF).astype(F32)
                for r in range(TAPS):
                    place = pl.ds(HALF - MARGIN + r, far_rows, stride=STRIDE)
                    masked = pooled * same_ref[0, :, r : r + 1]
                    small[1 + c, 1 + r : 2 + r, wider] += column_sum(masked * plain[place, :])
                    spread[place, :] = spread[place, :] + taps_ref[c, r : r + 1, wider] * masked
                made = spread[...].astype(BF)
                low[c, 0, :, lanes] = made
                small[1 + c, 0:1, wider] += column_sum(made)
        total[n, 0] += nn(xt_ref[...], low_q[...])
        total[n, 1] += nn(xt_ref[...], low[0, 0])
        total[n, 2] += nn(xt_ref[...], low[1, 0])

    @pl.when(seq == pl.num_programs(0) - 1)
    def _():
        heads = span // HEAD_DIM
        lane = lax.broadcasted_iota(jnp.int32, (1, PAIR), 1) < HEAD_DIM

        def place_four(four, n, u, where):
            turned = [pltpu.roll(value, HEAD_DIM, 1) for value in four]
            for pair in range(2):
                one, two = 2 * pair, 2 * pair + 1
                first = (2 * n + pair) * PAIR
                lanes = slice(first, first + PAIR)
                stage[2 * u, where, lanes] = jnp.where(lane, four[one], turned[two]).astype(BF)
                stage[2 * u + 1, where, lanes] = jnp.where(lane, turned[one], four[two]).astype(BF)

        for n, chunk_refs in enumerate(per_chunk):
            gout_ref = chunk_refs[5 + blocks]
            for u in range(heads // 2):
                lanes = slice(u * PAIR, (u + 1) * PAIR)
                wider = slice(n * span + u * PAIR, n * span + (u + 1) * PAIR)
                four = [total[n, part, :, lanes] for part in range(3)]
                four.append(gout_ref[:, lanes].astype(F32))
                place_four(four, n, u, slice(0, width))
                place_four(
                    [small[part, :, wider] for part in range(4)], n, u, slice(width, width + EXTRA)
                )
        last = slice(width, width + EXTRA)
        head = lax.broadcasted_iota(jnp.int32, (EXTRA, 1), 0) <= TAPS
        for t in range(heads):
            stage[t, last, :] = jnp.where(
                head, stage[t, last, :].astype(F32), more_ref[...]
            ).astype(BF)
        height = gws[0].shape[2] - EXTRA
        number = 0
        for group in gws:
            for m in range(group.shape[0]):
                place = pl.ds(pl.multiple_of(offs[number], 16), height)
                group[m, :, :height] = stage[:, place, :]
                group[m, :, height:] = stage[:, last, :]
                number += 1


def gather_back(first_chunk, offs, group_sizes, parts, taps, same, xt, more):
    chunks = len(parts)
    seqs, wide, span = parts[0][1].shape
    width = xt.shape[0]
    rows = wide - 2 * HALF
    blocks, far_rows = len(parts[0][3]), parts[0][3][0].shape[2]
    height = width // sum(group_sizes)
    heads = span // HEAD_DIM
    in_specs, operands = [], []
    for dq, dk, dv, dps, proj, gout in parts:
        in_specs += [pl.BlockSpec((1, wide, span), lambda s, o: (s, 0, 0))] * 2
        in_specs += [pl.BlockSpec((1, rows, span), lambda s, o: (s, 0, 0))]
        in_specs += [pl.BlockSpec((2, 1, far_rows, span), lambda s, o: (0, s, 0, 0))] * blocks
        in_specs += [
            pl.BlockSpec((1, 1, wide, span), lambda s, o: (1, s, 0, 0)),
            pl.BlockSpec((1, 1, wide, span), lambda s, o: (2, s, 0, 0)),
            once(gout.shape),
        ]
        operands += [dk, dv, dq, *dps, proj, proj, gout]
    out = pl.pallas_call(
        partial(gather_back_kernel, blocks, chunks, len(group_sizes)),
        grid_spec=pltpu.PrefetchScalarGridSpec(
            num_scalar_prefetch=1,
            grid=(seqs,),
            in_specs=in_specs
            + [
                once((2, 8, span * chunks)),
                pl.BlockSpec((1, far_rows, 8), lambda s, o: (s, 0, 0)),
                pl.BlockSpec((width, wide), lambda s, o: (0, s)),
                once(more.shape),
            ],
            out_specs=[
                once((size, heads, height + EXTRA, 4 * HEAD_DIM * chunks)) for size in group_sizes
            ]
            + [pl.BlockSpec((2, 1, wide, span), lambda s, o: (0, s, 0, 0))] * chunks,
            scratch_shapes=[
                pltpu.VMEM((4, EXTRA, span * chunks), F32),
                pltpu.VMEM((wide, PAIR), F32),
                pltpu.VMEM((wide, PAIR), F32),
                pltpu.VMEM((wide, span), BF),
                pltpu.VMEM((chunks, 3, width, span), F32),
                pltpu.VMEM((heads, width + EXTRA, 4 * HEAD_DIM * chunks), BF),
            ],
        ),
        out_shape=[
            jax.ShapeDtypeStruct((size, heads, height + EXTRA, 4 * HEAD_DIM * chunks), BF)
            for size in group_sizes
        ]
        + [jax.ShapeDtypeStruct((2, seqs, wide, span), BF)] * chunks,
        compiler_params=params(60),
        cost_estimate=cost(6 * chunks * seqs * wide * width * span, 12 * chunks),
    )(offs, *operands, taps[:, :, first_chunk * span : (first_chunk + chunks) * span], same, xt, more)
    return out[: len(group_sizes)], out[len(group_sizes) :]


def input_grad_kernel(chunks, *refs):
    per_chunk = [refs[3 * n : 3 * n + 3] for n in range(chunks)]
    res_ref, mid_ref, first_ref, last_ref = refs[3 * chunks :]
    rows = mid_ref.shape[1]
    edge = None
    inner = res_ref[0]
    for dq_ref, low_ref, w_ref in per_chunk:
        inner = inner + nt(dq_ref[0], w_ref[0])
        for c in range(2):
            term = nt(low_ref[c, 0], w_ref[1 + c])
            edge = term if edge is None else edge + term
    mid_ref[0] = inner + edge[HALF : HALF + rows]
    first_ref[0] = edge[:HALF].astype(BF)
    last_ref[0] = edge[HALF + rows :].astype(BF)


def input_grad(parts, residual):
    seqs, rows, width = residual.shape
    wide, span = parts[0][1].shape[2:]
    in_specs, operands = [], []
    for dq, low, w in parts:
        in_specs += [
            pl.BlockSpec((1, rows, span), lambda s: (s, 0, 0)),
            pl.BlockSpec((2, 1, wide, span), lambda s: (0, s, 0, 0)),
            once(w.shape),
        ]
        operands += [dq, low, w]
    own = pl.BlockSpec((1, rows, width), lambda s: (s, 0, 0))
    edge = pl.BlockSpec((1, HALF, width), lambda s: (s, 0, 0))
    return pl.pallas_call(
        partial(input_grad_kernel, len(parts)),
        grid=(seqs,),
        in_specs=in_specs + [own],
        out_specs=[own, edge, edge],
        out_shape=[
            jax.ShapeDtypeStruct((seqs, rows, width), F32),
            jax.ShapeDtypeStruct((seqs, HALF, width), BF),
            jax.ShapeDtypeStruct((seqs, HALF, width), BF),
        ],
        compiler_params=params(60),
        cost_estimate=cost(6 * len(parts) * seqs * wide * width * span, 16),
    )(*operands, residual)


def after(value, *others):
    return lax.optimization_barrier((value,) + others)[0]


def cycle(values, axis, shift):
    count = lax.axis_size(axis)
    return lax.ppermute(values, axis, [(i, (i + shift) % count) for i in range(count)])


def swap(values, axis, mask):
    count = lax.axis_size(axis)
    return lax.ppermute(values, axis, [(i, i ^ mask) for i in range(count)])


def shift_right(rows):
    count = lax.axis_size("tp")
    return lax.ppermute(rows, "tp", [(i, i + 1) for i in range(count - 1)])


def shift_left(rows):
    count = lax.axis_size("tp")
    return lax.ppermute(rows, "tp", [(i + 1, i) for i in range(count - 1)])


def gather_columns(shard):
    if lax.axis_size("tp") != 4:
        return lax.all_gather(shard, "tp", axis=0, tiled=False)
    me = lax.axis_index("tp")
    found = [shard] + [swap(shard, "tp", mask) for mask in (1, 2, 3)]
    odd, high = me % 2 == 1, me >= 2
    found = [jnp.where(odd, found[n ^ 1], found[n]) for n in range(4)]
    return jnp.stack([jnp.where(high, found[n ^ 2], found[n]) for n in range(4)])


def gather_pieces(shard, beside):
    mine = lax.axis_index("fsdp")
    rows = shard.shape[0]
    half = rows // 2
    across = swap(shard, "fsdp", 2)
    along = swap(shard, "fsdp", 4)
    onward = after(across[:half], *beside)
    corner = [swap(onward, "fsdp", 4), swap(along[half:], "fsdp", 2)]
    own = [shard, across, along] + corner
    other = [swap(piece, "fsdp", 1) for piece in own]
    place = [
        (mine ^ mask) * rows + extra
        for core in (0, 1)
        for mask, extra in ((core, 0), (2 + core, 0), (4 + core, 0), (6 + core, 0), (6 + core, half))
    ]
    return own + other, jnp.stack(place).astype(jnp.int32)


def add_low(first, *others):
    total = first.astype(F32)
    for other in others:
        total = total + other.astype(F32)
    return total


def merge_cores(keep, send):
    return add_low(keep, swap(send, "fsdp", 1)).astype(BF)


def merge_chips(blocks):
    return add_low(blocks[0], *[swap(blocks[n], "fsdp", 2 * n) for n in (1, 2, 3)]).astype(BF)


def scatter_tp(blocks):
    count = lax.axis_size("tp")
    me = lax.axis_index("tp")

    def pick(d):
        return lax.dynamic_index_in_dim(blocks, (me + d) % count, 0, keepdims=False)

    return add_low(pick(0), *[cycle(pick(d), "tp", d) for d in range(1, count)])


def spread_rows(whole, blocks):
    parts, rows, cols = whole.shape
    rows -= EXTRA
    main = whole[:, :rows].reshape(parts, blocks, rows // blocks, cols).transpose(1, 0, 2, 3)
    more = jnp.broadcast_to(whole[None, :, rows:], (blocks, parts, EXTRA, cols))
    return jnp.concatenate([main, more], axis=2)


def split_three(values):
    high = lax.reduce_precision(values, 8, 7)
    rest = values - high
    middle = lax.reduce_precision(rest, 8, 7)
    return jnp.stack([high, middle, rest - middle]).astype(BF)


def body(
    inputs, segments, w_qkv, qkv_bias, pool_kernel, w_out, out_bias,
    w_up, up_bias, w_down, norm_gains, norm_shifts, cotangent,
):
    rows, seqs, width = inputs.shape
    tp = lax.axis_size("tp")
    fsdp = lax.axis_size("fsdp")
    place = lax.axis_index("tp")
    shard_rows = w_qkv.shape[0]
    local = w_qkv.shape[2]
    chunks = local // HEAD_DIM
    span = tp * HEAD_DIM
    hidden_local = w_up.shape[1]
    hidden_units = hidden_local * tp
    far_rows = rows // STRIDE
    fast = fsdp == 8 and shard_rows % 32 == 0

    bias_values = jnp.concatenate(
        [qkv_bias.reshape(-1), pool_kernel.reshape(-1), up_bias.reshape(-1)]
    )
    biases = split_three(bias_values)
    extra = -(-biases.size // (4 * local))
    packed = jnp.concatenate(
        [
            jnp.concatenate([w_qkv.reshape(shard_rows, 3 * local), w_out], axis=1),
            jnp.pad(biases.reshape(-1), (0, extra * 4 * local - biases.size)).reshape(
                extra, 4 * local
            ),
        ],
        axis=0,
    )
    left = shift_right(inputs[rows - HALF :])
    right = shift_left(inputs[:HALF])
    columns = gather_columns(packed)
    wide_rows = (
        columns[:, :shard_rows]
        .reshape(tp, shard_rows, 4, chunks, HEAD_DIM)
        .transpose(1, 2, 3, 0, 4)
        .reshape(shard_rows, 4 * width)
    )
    qkv_rows, out_rows = wide_rows[:, : 3 * width], wide_rows[:, 3 * width :]
    whole_bias = jnp.sum(
        columns[:, shard_rows:].reshape(tp, -1)[:, : biases.size].reshape(tp, 3, -1).astype(F32),
        axis=1,
    )
    lead = (3 + 2 * TAPS) * local
    featured = (
        whole_bias[:, :lead]
        .reshape(tp, 3 + 2 * TAPS, chunks, HEAD_DIM)
        .transpose(1, 2, 0, 3)
        .reshape(3 + 2 * TAPS, width)
    )
    bias_qkv = featured[:3, None, :]
    taps = jnp.pad(featured[3:].reshape(2, TAPS, width), ((0, 0), (0, 8 - TAPS), (0, 0)))
    bias_up = whole_bias[:, lead:].reshape(1, hidden_units)

    x_wide = jnp.concatenate([left, inputs, right], axis=0).transpose(1, 0, 2)
    wide = rows + 2 * HALF

    seg_rows = segments.T
    padded = jnp.pad(seg_rows, ((0, 0), (HALF, HALF)), constant_values=-1)
    seg_keys = lax.dynamic_slice_in_dim(padded, place * rows, wide, 1)
    seg_own = seg_keys[:, HALF : HALF + rows]
    centers = seg_rows[:, ::STRIDE].reshape(seqs, tp, far_rows)
    centers_cycle = jnp.concatenate(
        [
            lax.dynamic_index_in_dim(centers, (place - d) % tp, 1, keepdims=True)
            for d in range(tp)
        ],
        axis=1,
    ).reshape(seqs, 1, tp * far_rows)
    segs = (seg_own[:, :, None], seg_keys[:, None, :], centers_cycle)
    own_centers = seg_own[:, ::STRIDE]
    same = jnp.stack(
        [
            seg_keys[:, HALF - MARGIN + r : HALF - MARGIN + r + rows : STRIDE][:, :far_rows]
            == own_centers
            for r in range(TAPS)
        ]
        + [jnp.zeros_like(own_centers, dtype=bool)] * (8 - TAPS),
        axis=2,
    ).astype(F32)

    if fast:
        pieces, offs = gather_pieces(qkv_rows, (x_wide, same, bias_qkv, taps) + segs)
    else:
        pieces = [lax.all_gather(qkv_rows, "fsdp", axis=0, tiled=True)]
        offs = jnp.zeros((1,), jnp.int32)

    later = after(jnp.concatenate([w_up, w_down], axis=1), columns)
    weights = lax.all_gather(later, "tp", axis=0, tiled=False)

    made, slots, att = [], [], []

    def send_pooled(j, *waits):
        pooled = made[j][1]
        sent = after(pooled, *waits) if waits else pooled
        slots.append([pooled] + [cycle(sent, "tp", d) for d in range(1, tp)])

    for j in range(chunks):
        if j:
            offs = after(offs, made[-1][1])
        made.append(project(j, chunks, pieces, offs, x_wide, bias_qkv, taps, same, far_rows))
        if j == 0:
            send_pooled(0)
    if chunks > 1:
        send_pooled(1, made[-1][1])
    weights = after(weights, made[-1][1], *slots[0][1:])
    weights = lax.all_gather(weights, "fsdp", axis=0, tiled=False)
    full_out = lax.all_gather(after(out_rows, made[0][1]), "fsdp", axis=0, tiled=True)
    for j in range(chunks):
        order = segs if j == 0 else segs[:2] + (after(segs[2], att[-1]),)
        att.append(attend_forward(made[j][0], slots[j], order))
        if j + 2 < chunks:
            send_pooled(j + 2, att[j])
    if shard_rows % 16:
        weights = weights.transpose(1, 0, 2, 3).reshape(1, tp, width, 2 * hidden_local)

    x_cols = after(x_wide, att[0]).reshape(seqs * wide, width).T
    cot = after(cotangent, att[0]).transpose(1, 0, 2)
    misc = jnp.concatenate([out_bias, norm_gains, norm_shifts, jnp.zeros((2, width), F32)])
    outputs, grad_residual, grad_att, grad_out, gud, small = dense(
        att, x_wide, cot, full_out, weights, bias_up, misc
    )
    if gud.shape[0] == 1:
        gud = spread_rows(gud[0], fsdp)
    gud = lax.psum_scatter(gud, "fsdp", scatter_dimension=0, tiled=False)
    gud_parts = gud.reshape(2, shard_rows + EXTRA, tp, hidden_local).transpose(2, 0, 1, 3)
    gud = lax.psum_scatter(gud_parts, "tp", scatter_dimension=0, tiled=False).astype(F32)

    if fast:
        mine = lax.axis_index("fsdp")
        group_sizes = (4, 4)
        out_offs = jnp.stack(
            [(mine ^ m) * shard_rows for m in (0, 2, 4, 6, 1, 3, 5, 7)]
        ).astype(jnp.int32)
    else:
        group_sizes = (1,)
        out_offs = jnp.zeros((1,), jnp.int32)
    backs = []
    for j in range(chunks):
        order = segs
        if j:
            waits = (backs[-1][0],) + (tuple(backs[-2][3][1:]) if j > 1 else ())
            order = segs[:2] + (after(segs[2], *waits),)
        dq, dk, dv, dps = attend_backward(made[j][0], slots[j], order, grad_att[j])
        if j:
            dps = [after(d, *backs[-1][3][1:]) for d in dps]
        arrived = [dps[0]] + [cycle(dps[d], "tp", -d) for d in range(1, tp)]
        backs.append((dq, dk, dv, arrived, made[j][0], grad_out[j]))
    totals, lows, merged = [], [], []
    for low, high in ((0, chunks - 1), (chunks - 1, chunks)):
        if low == high:
            continue
        cols = (high - low) * 4 * HEAD_DIM
        more = jnp.zeros((EXTRA, cols), F32)
        if not merged:
            flat = small[:6].reshape(-1)
            lines = -(-flat.size // cols)
            flat = jnp.pad(flat, (0, lines * cols - flat.size)).reshape(lines, cols)
            more = jnp.pad(flat, ((TAPS + 1, EXTRA - TAPS - 1 - lines), (0, 0)))
        waits = [backs[-1][0], gud_parts]
        groups, low_kv = gather_back(
            low, after(out_offs, *waits), group_sizes, backs[low:high], taps, same, x_cols, more
        )
        lows += low_kv
        if fast:
            merged.append(merge_cores(*[after(g, *backs[-1][3][1:]) for g in groups]))
        else:
            merged.append(spread_rows(groups[0][0], fsdp))
    middle, first, last = input_grad(
        [(backs[n][0], lows[n], made[n][2]) for n in range(chunks)], grad_residual
    )
    chips = []
    for n, blocks in enumerate(merged):
        blocks = after(blocks, *chips) if chips else blocks
        if fast:
            chips.append(merge_chips(blocks))
        else:
            chips.append(lax.psum_scatter(blocks, "fsdp", scatter_dimension=0, tiled=False))
    for blocks in chips:
        if len(totals) + 1 == len(chips):
            blocks = after(blocks, middle)
        else:
            blocks = after(blocks, merged[-1])
        totals.append(scatter_tp(blocks))

    first, last = after(first, chips[-1]), after(last, chips[-1])
    to_left = shift_left(first)
    to_right = shift_right(last)
    middle = middle.at[:, :HALF].add(to_right.astype(F32))
    middle = middle.at[:, rows - HALF :].add(to_left.astype(F32))
    grad_inputs = middle.transpose(1, 0, 2)

    sums = totals[0][shard_rows + TAPS + 1 :].reshape(-1)[: 6 * width].reshape(6, width)
    stacked = jnp.concatenate(
        [t[: shard_rows + TAPS + 1].reshape(-1, t.shape[1] // (4 * HEAD_DIM), 4, HEAD_DIM)
         for t in totals],
        axis=1,
    )
    stacked = stacked.transpose(0, 2, 1, 3).reshape(-1, 4, local)
    main, bias_row, tap_rows = stacked[:shard_rows], stacked[shard_rows], stacked[shard_rows + 1 :]
    return (
        outputs.transpose(1, 0, 2),
        grad_inputs,
        main[:, :3],
        bias_row[:3],
        tap_rows[:, 1:3].transpose(1, 0, 2),
        main[:, 3],
        sums[0:2],
        gud[0, :shard_rows],
        gud[0, shard_rows],
        gud[1, :shard_rows],
        sums[2:4],
        sums[4:6],
    )


def solution(mesh):
    placed = (
        P("tp", "fsdp", None),
        P(None, "fsdp"),
        P("fsdp", None, "tp"),
        P(None, "tp"),
        P(None, None, "tp"),
        P("fsdp", "tp"),
        P(),
        P("fsdp", "tp"),
        P("tp"),
        P("fsdp", "tp"),
        P(),
        P(),
        P("tp", "fsdp", None),
    )
    return jax.shard_map(
        body,
        mesh=mesh,
        in_specs=placed,
        out_specs=(
            P("tp", "fsdp", None),
            P("tp", "fsdp", None),
            P("fsdp", None, "tp"),
            P(None, "tp"),
            P(None, None, "tp"),
            P("fsdp", "tp"),
            P(),
            P("fsdp", "tp"),
            P("tp"),
            P("fsdp", "tp"),
            P(),
            P(),
        ),
        check_vma=False,
    )
```

```python
from functools import partial

import jax
import jax.numpy as jnp
import numpy as np
from jax import lax
from jax.experimental import pallas as pl
from jax.experimental.pallas import tpu as pltpu
from jax.sharding import PartitionSpec as P

HEAD_DIM = 64
HALF = 64
STRIDE = 4
TAPS = 5
MARGIN = TAPS // 2
PAIR = 2 * HEAD_DIM
QB = 128
SB = 128
NEAR = QB + 2 * HALF
EXTRA = 16
RC = 256
EPSILON = 1e-05
NEG = -1e30
SCALE = HEAD_DIM**-0.5
BF = jnp.bfloat16
F32 = jnp.float32
MIB = 2**20


def nt(a, b):
    return lax.dot_general(a, b, (((1,), (1,)), ((), ())), preferred_element_type=F32)


def nn(a, b):
    return lax.dot_general(a, b, (((1,), (0,)), ((), ())), preferred_element_type=F32)


def tn(a, b):
    return lax.dot_general(a, b, (((0,), (0,)), ((), ())), preferred_element_type=F32)


def params(mib):
    return pltpu.CompilerParams(vmem_limit_bytes=mib * MIB)


def cost(flops, mib, trans=0):
    return pl.CostEstimate(flops=1, bytes_accessed=1, transcendentals=0)


def once(shape):
    zeros = (0,) * len(shape)
    return pl.BlockSpec(shape, lambda *_: zeros, pipeline_mode=pl.Buffered(1))


def project_kernel(count, offs, *refs):
    pieces = refs[:count]
    x_ref, bias_ref, taps_ref, same_ref, out_ref, pooled_ref, w_ref, plain = refs[count:]
    part = pl.program_id(0)
    for n in range(count):
        rows = pieces[n].shape[0]
        w_ref[0, pl.ds(pl.multiple_of(offs[n], 16), rows), :] = pieces[n][...]
    seqs, wide, _ = x_ref.shape
    far_rows = pooled_ref.shape[2]

    @pl.when(part < 3)
    def _():
        for s in range(seqs):
            made = (nn(x_ref[s], w_ref[0]) + bias_ref[0]).astype(BF)
            out_ref[0, s] = made
            for half in range(plain.shape[1]):
                plain[s, half] = made[:, half * PAIR : (half + 1) * PAIR].astype(F32)

    @pl.when((part > 0) & (part < 3))
    def _():
        for s in range(seqs):
            for half in range(plain.shape[1]):
                lanes = slice(half * PAIR, (half + 1) * PAIR)
                total = jnp.zeros((far_rows, PAIR), F32)
                for r in range(TAPS):
                    rows = plain[s, half, pl.ds(HALF - MARGIN + r, far_rows, stride=STRIDE), :]
                    total = total + taps_ref[0, r : r + 1, lanes] * rows * same_ref[
                        s, :, r : r + 1
                    ]
                pooled_ref[0, s, :, lanes] = total.astype(BF)


def project(chunk, chunks, pieces, offs, x_wide, bias, taps, same, far_rows):
    seqs, wide, width = x_wide.shape
    span = width // chunks

    def piece_spec(piece):
        return pl.BlockSpec((piece.shape[0], span), lambda c, o: (0, c * chunks + chunk))

    def three(c):
        return jnp.minimum(c, 2)

    def kv(c):
        return jnp.maximum(three(c) - 1, 0)

    return pl.pallas_call(
        partial(project_kernel, len(pieces)),
        grid_spec=pltpu.PrefetchScalarGridSpec(
            num_scalar_prefetch=1,
            grid=(4,),
            in_specs=[piece_spec(p) for p in pieces]
            + [
                once(x_wide.shape),
                pl.BlockSpec((1, 1, span), lambda c, o: (three(c), 0, chunk)),
                pl.BlockSpec((1, 8, span), lambda c, o: (kv(c), 0, chunk)),
                once(same.shape),
            ],
            out_specs=[
                pl.BlockSpec((1, seqs, wide, span), lambda c, o: (three(c), 0, 0, 0)),
                pl.BlockSpec((1, seqs, far_rows, span), lambda c, o: (kv(c), 0, 0, 0)),
                pl.BlockSpec((1, width, span), lambda c, o: (c, 0, 0)),
            ],
            scratch_shapes=[pltpu.VMEM((seqs, span // PAIR, wide, PAIR), F32)],
        ),
        out_shape=[
            jax.ShapeDtypeStruct((3, seqs, wide, span), BF),
            jax.ShapeDtypeStruct((2, seqs, far_rows, span), BF),
            jax.ShapeDtypeStruct((4, width, span), BF),
        ],
        compiler_params=params(32),
        cost_estimate=cost(6 * seqs * wide * width * span, 8),
    )(offs, *pieces, x_wide, bias, taps, same)


def fill_masks(segq_ref, segk_ref, cen_ref, near_bias, far_bias):
    rows = segq_ref.shape[1]
    shape = (QB, NEAR)
    gap = lax.broadcasted_iota(jnp.int32, shape, 1) - lax.broadcasted_iota(jnp.int32, shape, 0)
    band = (gap >= 0) & (gap <= 2 * HALF)
    for first in range(0, rows, QB):
        own = segq_ref[0, first : first + QB, :]
        keys = segk_ref[0, :, first : first + NEAR]
        near_bias[first : first + QB, :] = jnp.where(band & (own == keys), 0.0, NEG)
        far_bias[first : first + QB, :] = jnp.where(own == cen_ref[0], 0.0, NEG)


def head_mask(head):
    lane = lax.broadcasted_iota(jnp.int32, (1, PAIR), 1)
    return lane < HEAD_DIM if head == 0 else lane >= HEAD_DIM


def fold_lanes(*arrays):
    parts = [a[:, n : n + PAIR] for a in arrays for n in range(0, a.shape[1], PAIR)]
    while len(parts) > 1:
        parts = [sum(parts[n : n + 2]) for n in range(0, len(parts), 2)]
    return parts[0]


def softmax_rows(near, far):
    top = jnp.maximum(
        jnp.max(near, axis=-1, keepdims=True), jnp.max(far, axis=-1, keepdims=True)
    )
    near = jnp.exp(near - top)
    far = jnp.exp(far - top)
    total = jnp.sum(near, axis=-1, keepdims=True) + jnp.sum(far, axis=-1, keepdims=True)
    inverse = 1.0 / total
    return near * inverse, far * inverse


def stack_heads(rows, stacked):
    for first in range(0, rows.shape[0], QB):
        part = rows[first : first + QB]
        for head in range(2):
            stacked[2 * first + head * QB : 2 * first + (head + 1) * QB, :] = jnp.where(
                head_mask(head), part, BF(0)
            )


def join_slots(slots, joined):
    rows = slots[0].shape[1]
    for n, slot in enumerate(slots):
        joined[n * rows : (n + 1) * rows, :] = slot[0]


def attend_forward_kernel(blocks, q_ref, k_ref, v_ref, *refs):
    pk, pv = refs[:blocks], refs[blocks : 2 * blocks]
    segq, segk, cen, out_ref = refs[2 * blocks : 2 * blocks + 4]
    near_bias, far_bias, far_keys, far_values, query, far_scores, far_probs = refs[
        2 * blocks + 4 :
    ]

    @pl.when(pl.program_id(1) == 0)
    def _():
        fill_masks(segq, segk, cen, near_bias, far_bias)

    rows = out_ref.shape[1]
    join_slots(pk, far_keys)
    join_slots(pv, far_values)
    stack_heads(q_ref[0, HALF : HALF + rows, :] * BF(SCALE), query)
    far_scores[...] = nt(query[...], far_keys[...])
    outs = []
    for first in range(0, rows, QB):
        span = slice(first, first + NEAR)
        pair = slice(2 * first, 2 * first + 2 * QB)
        near_all = nt(query[pair, :], k_ref[0, span, :])
        lows = []
        for part in range(0, 2 * QB, SB):
            source = first + part % QB
            near, far = softmax_rows(
                near_all[part : part + SB] + near_bias[source : source + SB, :],
                far_scores[2 * first + part : 2 * first + part + SB, :]
                + far_bias[source : source + SB, :],
            )
            far_probs[2 * first + part : 2 * first + part + SB, :] = far.astype(BF)
            lows.append(near.astype(BF))
        outs.append(nn(jnp.concatenate(lows, axis=0), v_ref[0, span, :]))
    far_out = nn(far_probs[...], far_values[...])
    for n, first in enumerate(range(0, rows, QB)):
        both = outs[n] + far_out[2 * first : 2 * first + 2 * QB]
        out_ref[0, first : first + QB, :] = jnp.where(head_mask(0), both[:QB], both[QB:]).astype(BF)


def attend_backward_kernel(blocks, q_ref, k_ref, v_ref, *refs):
    pk, pv = refs[:blocks], refs[blocks : 2 * blocks]
    segq, segk, cen, grad_ref, dq_ref, dk_ref, dv_ref = refs[2 * blocks : 2 * blocks + 7]
    dp_refs = refs[2 * blocks + 7 : 3 * blocks + 7]
    (
        near_bias, far_bias, far_keys, far_values,
        query, far_scores, far_probs, grad, far_dots, far_grads,
    ) = refs[3 * blocks + 7 :]

    @pl.when(pl.program_id(1) == 0)
    def _():
        fill_masks(segq, segk, cen, near_bias, far_bias)

    rows = dq_ref.shape[1]
    join_slots(pk, far_keys)
    join_slots(pv, far_values)
    stack_heads(q_ref[0, HALF : HALF + rows, :] * BF(SCALE), query)
    stack_heads(grad_ref[0], grad)
    far_scores[...] = nt(query[...], far_keys[...])
    far_dots[...] = nt(grad[...], far_values[...])
    dk_ref[...] = jnp.zeros_like(dk_ref)
    dv_ref[...] = jnp.zeros_like(dv_ref)
    dqs = []
    for first in range(0, rows, QB):
        span = slice(first, first + NEAR)
        pair = slice(2 * first, 2 * first + 2 * QB)
        near_all = nt(query[pair, :], k_ref[0, span, :])
        dots_all = nt(grad[pair, :], v_ref[0, span, :])
        lows, grads = [], []
        for part in range(0, 2 * QB, SB):
            source = first + part % QB
            here = slice(2 * first + part, 2 * first + part + SB)
            near, far = softmax_rows(
                near_all[part : part + SB] + near_bias[source : source + SB, :],
                far_scores[here, :] + far_bias[source : source + SB, :],
            )
            near_dot, far_dot = dots_all[part : part + SB], far_dots[here, :]
            row_dot = jnp.sum(
                fold_lanes(near * near_dot, far * far_dot), axis=-1, keepdims=True
            )
            far_probs[here, :] = far.astype(BF)
            far_grads[here, :] = (far * (far_dot - row_dot)).astype(BF)
            lows.append(near.astype(BF))
            grads.append((near * (near_dot - row_dot)).astype(BF))
        low = jnp.concatenate(lows, axis=0)
        ds = jnp.concatenate(grads, axis=0)
        dqs.append(nn(ds, k_ref[0, span, :]))
        dk_ref[0, span, :] += nn(query[pair, :].T, ds).T
        dv_ref[0, span, :] += nn(grad[pair, :].T, low).T
    far_dq = nn(far_grads[...], far_keys[...])
    for n, first in enumerate(range(0, rows, QB)):
        both = (dqs[n] + far_dq[2 * first : 2 * first + 2 * QB]) * SCALE
        dq_ref[0, first : first + QB, :] = jnp.where(head_mask(0), both[:QB], both[QB:]).astype(BF)
    dpk = nn(query[...].T, far_grads[...]).T.astype(BF)
    dpv = nn(grad[...].T, far_probs[...]).T.astype(BF)
    far_rows = dp_refs[0].shape[2]
    for n, ref in enumerate(dp_refs):
        ref[0, 0] = dpk[n * far_rows : (n + 1) * far_rows]
        ref[1, 0] = dpv[n * far_rows : (n + 1) * far_rows]


def attention_specs(wide, blocks, far_rows):
    def own(part):
        return pl.BlockSpec((None, 1, wide, PAIR), lambda s, h: (part, s, 0, h))

    def pooled(part):
        return pl.BlockSpec((None, 1, far_rows, PAIR), lambda s, h: (part, s, 0, h))

    rows = wide - 2 * HALF
    return (
        [own(0), own(1), own(2)]
        + [pooled(0)] * blocks
        + [pooled(1)] * blocks
        + [
            pl.BlockSpec((1, rows, 1), lambda s, h: (s, 0, 0)),
            pl.BlockSpec((1, 1, wide), lambda s, h: (s, 0, 0)),
            pl.BlockSpec((1, 1, blocks * far_rows), lambda s, h: (s, 0, 0)),
        ]
    )


def attention_scratch(rows, far_all):
    return [
        pltpu.VMEM((rows, NEAR), F32),
        pltpu.VMEM((rows, far_all), F32),
        pltpu.VMEM((far_all, PAIR), BF),
        pltpu.VMEM((far_all, PAIR), BF),
        pltpu.VMEM((2 * rows, PAIR), BF),
        pltpu.VMEM((2 * rows, far_all), F32),
        pltpu.VMEM((2 * rows, far_all), BF),
    ]


def attend_forward(proj, slots, segs):
    _, seqs, wide, span = proj.shape
    blocks, far_rows = len(slots), slots[0].shape[2]
    rows = wide - 2 * HALF
    cells = seqs * rows * (NEAR + blocks * far_rows) * (span // HEAD_DIM)
    return pl.pallas_call(
        partial(attend_forward_kernel, blocks),
        grid=(seqs, span // PAIR),
        in_specs=attention_specs(wide, blocks, far_rows),
        out_specs=pl.BlockSpec((1, rows, PAIR), lambda s, h: (s, 0, h)),
        out_shape=jax.ShapeDtypeStruct((seqs, rows, span), BF),
        scratch_shapes=attention_scratch(rows, blocks * far_rows),
        compiler_params=params(60),
        cost_estimate=cost(16 * 64 * cells, 8, cells),
    )(proj, proj, proj, *slots, *slots, *segs)


def attend_backward(proj, slots, segs, grad):
    _, seqs, wide, span = proj.shape
    blocks, far_rows = len(slots), slots[0].shape[2]
    rows = wide - 2 * HALF
    cells = seqs * rows * (NEAR + blocks * far_rows) * (span // HEAD_DIM)
    own_spec = pl.BlockSpec((1, rows, PAIR), lambda s, h: (s, 0, h))
    wide_spec = pl.BlockSpec((1, wide, PAIR), lambda s, h: (s, 0, h))
    wide_shape = jax.ShapeDtypeStruct((seqs, wide, span), F32)
    far_spec = pl.BlockSpec((2, 1, far_rows, PAIR), lambda s, h: (0, s, 0, h))
    far_shape = jax.ShapeDtypeStruct((2, seqs, far_rows, span), BF)
    out = pl.pallas_call(
        partial(attend_backward_kernel, blocks),
        grid=(seqs, span // PAIR),
        in_specs=attention_specs(wide, blocks, far_rows) + [own_spec],
        out_specs=[own_spec, wide_spec, wide_spec] + [far_spec] * blocks,
        out_shape=[jax.ShapeDtypeStruct((seqs, rows, span), BF), wide_shape, wide_shape]
        + [far_shape] * blocks,
        scratch_shapes=attention_scratch(rows, blocks * far_rows)
        + [
            pltpu.VMEM((2 * rows, PAIR), BF),
            pltpu.VMEM((2 * rows, blocks * far_rows), F32),
            pltpu.VMEM((2 * rows, blocks * far_rows), BF),
        ],
        compiler_params=params(60),
        cost_estimate=cost(40 * 64 * cells, 16, cells),
    )(proj, proj, proj, *slots, *slots, *segs, grad)
    return out[0], out[1], out[2], out[3:]


def norm_stats(residual):
    row_mean = jnp.mean(residual, axis=-1, keepdims=True)
    centered = residual - row_mean
    variance = jnp.mean(centered * centered, axis=-1, keepdims=True)
    inverse = lax.rsqrt(variance + EPSILON)
    return centered * inverse, inverse


def norm_back(grad, normed, inverse, gain):
    scaled = grad * gain
    first = jnp.mean(scaled, axis=-1, keepdims=True)
    second = jnp.mean(scaled * normed, axis=-1, keepdims=True)
    return (scaled - first - normed * second) * inverse


def column_sum(values):
    return jnp.sum(values.astype(F32), axis=0, keepdims=True)


def dense_kernel(chunks, steps, *refs):
    att, wout = refs[:chunks], refs[chunks : 2 * chunks]
    x_ref, cot_ref, up_blk, down_blk, bup_ref, misc_ref = refs[2 * chunks : 2 * chunks + 6]
    outs = refs[2 * chunks + 6 :]
    out_ref, gres_ref = outs[:2]
    gatt = outs[2 : 2 + chunks]
    gout = outs[2 + chunks : 2 + 2 * chunks]
    gud_ref, small_ref = outs[2 + 2 * chunks : 4 + 2 * chunks]
    (
        inverse, flow, flow_t, acc, gffn, gffn_t, hidden, slope, gpre
    ) = outs[4 + 2 * chunks :]
    step = pl.program_id(0)
    seqs, rows, width = cot_ref.shape
    total = seqs * rows
    span = width // chunks
    units = gpre.shape[1]
    up_ref = up_blk[...].reshape(width, units)
    down_ref = down_blk[...].reshape(width, units)
    bias_one, bias_two = misc_ref[0:1, :], misc_ref[1:2, :]
    gain_one, gain_two = misc_ref[2:3, :], misc_ref[3:4, :]
    shift_one, shift_two = misc_ref[4:5, :], misc_ref[5:6, :]
    parts = [(first, first // rows, first % rows) for first in range(0, total, RC)]

    @pl.when(step == 0)
    def _():
        for first, s, row in parts:
            block = slice(first, first + RC)
            branch = bias_one
            for j in range(chunks):
                branch = branch + nt(
                    att[j][s, row : row + RC, :], wout[j][0]
                )
            n_one, inv = norm_stats(
                x_ref[s, HALF + row : HALF + row + RC, :].astype(F32) + branch
            )
            gres_ref[s, row : row + RC, :] = n_one
            inverse[block, :] = inv
            low = (n_one * gain_one + shift_one).astype(BF)
            flow[block, :] = low
            flow_t[:, block] = low.T
            acc[block, :] = jnp.zeros((RC, width), F32)

    @pl.when(step < steps)
    def _():
        for first, s, row in parts:
            block = slice(first, first + RC)
            pre = nn(flow[block, :], up_ref) + bup_ref[...]
            cdf = 0.5 * (1.0 + lax.erf(pre * np.float32(np.sqrt(0.5))))
            pdf = jnp.exp(-0.5 * (pre * pre)) * np.float32(1.0 / np.sqrt(2.0 * np.pi))
            low = (pre * cdf).astype(BF)
            hidden[step, block, :] = low
            slope[step, block, :] = cdf + pre * pdf
            acc[block, :] += nt(low, down_ref)

    @pl.when(step == steps)
    def _():
        small_ref[...] = jnp.zeros_like(small_ref)
        for first, s, row in parts:
            block = slice(first, first + RC)
            first_out = gres_ref[s, row : row + RC, :] * gain_one + shift_one
            n_two, inv = norm_stats(first_out + (acc[block, :] + bias_two))
            out_ref[s, row : row + RC, :] = (n_two * gain_two + shift_two).astype(BF)
            grad = cot_ref[s, row : row + RC, :].astype(F32)
            second = norm_back(grad, n_two, inv, gain_two)
            acc[block, :] = second
            low = second.astype(BF)
            gffn[block, :] = low
            gffn_t[:, block] = low.T
            small_ref[1:2, :] += column_sum(low)
            small_ref[3:4, :] += column_sum(grad * n_two)
            small_ref[5:6, :] += column_sum(grad)

    @pl.when(step >= steps)
    def _():
        which = 2 * steps - 1 - step
        bias_sum = jnp.zeros((1, units), F32)
        for first, s, row in parts:
            block = slice(first, first + RC)
            grad = nn(gffn[block, :], down_ref)
            low = (grad * slope[which, block, :]).astype(BF)
            gpre[block, :] = low
            bias_sum = bias_sum + column_sum(low)
            acc[block, :] += nt(low, up_ref)
        height = gud_ref.shape[2] - EXTRA
        lead = (gud_ref.shape[0], height, units)
        gud_ref[:, 0, :height] = nn(flow_t[...], gpre[...]).astype(BF).reshape(lead)
        gud_ref[:, 1, :height] = nn(gffn_t[...], hidden[which]).astype(BF).reshape(lead)
        head = lax.broadcasted_iota(jnp.int32, (EXTRA, 1), 0) == 0
        extra = jnp.where(head, bias_sum, 0.0).astype(BF)
        for m in range(gud_ref.shape[0]):
            gud_ref[m, 0, height:] = extra
            gud_ref[m, 1, height:] = jnp.zeros((EXTRA, units), BF)

    @pl.when(step == 2 * steps - 1)
    def _():
        for first, s, row in parts:
            block = slice(first, first + RC)
            grad = acc[block, :]
            n_one = gres_ref[s, row : row + RC, :]
            back = norm_back(grad, n_one, inverse[block, :], gain_one)
            gres_ref[s, row : row + RC, :] = back
            low = back.astype(BF)
            flow_t[:, block] = low.T
            small_ref[0:1, :] += column_sum(low)
            small_ref[2:3, :] += column_sum(grad * n_one)
            small_ref[4:5, :] += column_sum(grad)
            for j in range(chunks):
                gatt[j][s, row : row + RC, :] = nn(
                    low, wout[j][0]
                ).astype(BF)
        for j in range(chunks):
            gout[j][...] = nn(flow_t[...], att[j][...].reshape(total, span)).astype(BF)


def dense(att, projected_weights, x_wide, cot, weights, bias_up, misc):
    chunks = len(att)
    seqs, rows, width = cot.shape
    total = seqs * rows
    span = width // chunks
    row_blocks, steps, height, units = weights.shape
    units //= 2

    def which(i):
        return jnp.where(i < steps, i, 2 * steps - 1 - i)

    def back(i):
        return jnp.where(i < steps, steps - 1, 2 * steps - 1 - i)

    out_shape = (
        [
            jax.ShapeDtypeStruct((seqs, rows, width), BF),
            jax.ShapeDtypeStruct((seqs, rows, width), F32),
        ]
        + [jax.ShapeDtypeStruct((seqs, rows, span), BF)] * chunks
        + [jax.ShapeDtypeStruct((width, span), BF)] * chunks
        + [
            jax.ShapeDtypeStruct((row_blocks, 2, height + EXTRA, steps * units), BF),
            jax.ShapeDtypeStruct((8, width), F32),
        ]
    )
    out_specs = [once(o.shape) for o in out_shape[: 2 + 2 * chunks]] + [
        pl.BlockSpec((row_blocks, 2, height + EXTRA, units), lambda i: (0, 0, 0, back(i))),
        once((8, width)),
    ]
    out = pl.pallas_call(
        partial(dense_kernel, chunks, steps),
        grid=(2 * steps,),
        in_specs=[once(a.shape) for a in att]
        + [
            pl.BlockSpec(
                (1, width, span), lambda i: (3, 0, 0), pipeline_mode=pl.Buffered(1)
            )
        ]
        * chunks
        + [
            once(x_wide.shape),
            once(cot.shape),
            pl.BlockSpec((row_blocks, None, height, units), lambda i: (0, which(i), 0, 0)),
            pl.BlockSpec((row_blocks, None, height, units), lambda i: (0, which(i), 0, 1)),
            pl.BlockSpec((1, units), lambda i: (0, which(i))),
            once(misc.shape),
        ],
        out_specs=out_specs,
        out_shape=out_shape,
        scratch_shapes=[
            pltpu.VMEM((total, 1), F32),
            pltpu.VMEM((total, width), BF),
            pltpu.VMEM((width, total), BF),
            pltpu.VMEM((total, width), F32),
            pltpu.VMEM((total, width), BF),
            pltpu.VMEM((width, total), BF),
            pltpu.VMEM((steps, total, units), BF),
            pltpu.VMEM((steps, total, units), F32),
            pltpu.VMEM((total, units), BF),
        ],
        compiler_params=params(63),
        cost_estimate=cost(1, 1),
    )(*att, *projected_weights, x_wide, cot, weights, weights, bias_up, misc)
    return (
        out[0], out[1], out[2 : 2 + chunks], out[2 + chunks : 2 + 2 * chunks], out[-2], out[-1]
    )


def gather_back_kernel(blocks, chunks, groups, offs, *refs):
    taken = 5 + blocks + 1
    per_chunk = [refs[n * taken : (n + 1) * taken] for n in range(chunks)]
    taps_ref, same_ref, xt_ref, more_ref = refs[chunks * taken : chunks * taken + 4]
    outs = refs[chunks * taken + 4 :]
    gws = outs[:groups]
    lows = outs[groups : groups + chunks]
    small, plain, spread, low_q, total, stage = outs[groups + chunks :]
    width = xt_ref.shape[0]
    seq = pl.program_id(0)
    wide, span = per_chunk[0][0].shape[1:]
    rows = wide - 2 * HALF
    far_rows = per_chunk[0][3].shape[2]

    @pl.when(seq == 0)
    def _():
        small[...] = jnp.zeros_like(small)
        total[...] = jnp.zeros_like(total)

    for n, chunk_refs in enumerate(per_chunk):
        dk_ref, dv_ref, dq_ref = chunk_refs[:3]
        dps = chunk_refs[3 : 3 + blocks]
        proj_k, proj_v = chunk_refs[3 + blocks : 5 + blocks]
        low = lows[n]
        base = n * span
        low_q[:HALF, :] = jnp.zeros((HALF, span), BF)
        low_q[HALF : HALF + rows, :] = dq_ref[0]
        low_q[HALF + rows :, :] = jnp.zeros((HALF, span), BF)
        small[0, 0:1, base : base + span] += column_sum(dq_ref[0])
        for c, (near, proj) in enumerate(((dk_ref, proj_k), (dv_ref, proj_v))):
            for half in range(span // PAIR):
                lanes = slice(half * PAIR, (half + 1) * PAIR)
                wider = slice(base + half * PAIR, base + (half + 1) * PAIR)
                plain[...] = proj[0, 0, :, lanes].astype(F32)
                spread[...] = near[0, :, lanes]
                pooled = dps[0][c, 0, :, lanes].astype(F32)
                for d in range(1, blocks):
                    pooled = pooled + dps[d][c, 0, :, lanes].astype(F32)
                pooled = pooled.astype(BF).astype(F32)
                for r in range(TAPS):
                    place = pl.ds(HALF - MARGIN + r, far_rows, stride=STRIDE)
                    masked = pooled * same_ref[0, :, r : r + 1]
                    small[1 + c, 1 + r : 2 + r, wider] += column_sum(masked * plain[place, :])
                    spread[place, :] = spread[place, :] + taps_ref[c, r : r + 1, wider] * masked
                made = spread[...].astype(BF)
                low[c, 0, :, lanes] = made
                small[1 + c, 0:1, wider] += column_sum(made)
        total[n, 0] += nn(xt_ref[...], low_q[...])
        total[n, 1] += nn(xt_ref[...], low[0, 0])
        total[n, 2] += nn(xt_ref[...], low[1, 0])

    @pl.when(seq == pl.num_programs(0) - 1)
    def _():
        heads = span // HEAD_DIM
        lane = lax.broadcasted_iota(jnp.int32, (1, PAIR), 1) < HEAD_DIM

        def place_four(four, n, u, where):
            turned = [pltpu.roll(value, HEAD_DIM, 1) for value in four]
            for pair in range(2):
                one, two = 2 * pair, 2 * pair + 1
                first = (2 * n + pair) * PAIR
                lanes = slice(first, first + PAIR)
                stage[2 * u, where, lanes] = jnp.where(lane, four[one], turned[two]).astype(BF)
                stage[2 * u + 1, where, lanes] = jnp.where(lane, turned[one], four[two]).astype(BF)

        for n, chunk_refs in enumerate(per_chunk):
            gout_ref = chunk_refs[5 + blocks]
            for u in range(heads // 2):
                lanes = slice(u * PAIR, (u + 1) * PAIR)
                wider = slice(n * span + u * PAIR, n * span + (u + 1) * PAIR)
                four = [total[n, part, :, lanes] for part in range(3)]
                four.append(gout_ref[:, lanes].astype(F32))
                place_four(four, n, u, slice(0, width))
                place_four(
                    [small[part, :, wider] for part in range(4)], n, u, slice(width, width + EXTRA)
                )
        last = slice(width, width + EXTRA)
        head = lax.broadcasted_iota(jnp.int32, (EXTRA, 1), 0) <= TAPS
        for t in range(heads):
            stage[t, last, :] = jnp.where(
                head, stage[t, last, :].astype(F32), more_ref[...]
            ).astype(BF)
        height = gws[0].shape[2] - EXTRA
        number = 0
        for group in gws:
            for m in range(group.shape[0]):
                place = pl.ds(pl.multiple_of(offs[number], 16), height)
                group[m, :, :height] = stage[:, place, :]
                group[m, :, height:] = stage[:, last, :]
                number += 1


def gather_back(first_chunk, offs, group_sizes, parts, taps, same, xt, more):
    chunks = len(parts)
    seqs, wide, span = parts[0][1].shape
    width = xt.shape[0]
    rows = wide - 2 * HALF
    blocks, far_rows = len(parts[0][3]), parts[0][3][0].shape[2]
    height = width // sum(group_sizes)
    heads = span // HEAD_DIM
    in_specs, operands = [], []
    for dq, dk, dv, dps, proj, gout in parts:
        in_specs += [pl.BlockSpec((1, wide, span), lambda s, o: (s, 0, 0))] * 2
        in_specs += [pl.BlockSpec((1, rows, span), lambda s, o: (s, 0, 0))]
        in_specs += [pl.BlockSpec((2, 1, far_rows, span), lambda s, o: (0, s, 0, 0))] * blocks
        in_specs += [
            pl.BlockSpec((1, 1, wide, span), lambda s, o: (1, s, 0, 0)),
            pl.BlockSpec((1, 1, wide, span), lambda s, o: (2, s, 0, 0)),
            once(gout.shape),
        ]
        operands += [dk, dv, dq, *dps, proj, proj, gout]
    out = pl.pallas_call(
        partial(gather_back_kernel, blocks, chunks, len(group_sizes)),
        grid_spec=pltpu.PrefetchScalarGridSpec(
            num_scalar_prefetch=1,
            grid=(seqs,),
            in_specs=in_specs
            + [
                once((2, 8, span * chunks)),
                pl.BlockSpec((1, far_rows, 8), lambda s, o: (s, 0, 0)),
                pl.BlockSpec((width, wide), lambda s, o: (0, s)),
                once(more.shape),
            ],
            out_specs=[
                once((size, heads, height + EXTRA, 4 * HEAD_DIM * chunks)) for size in group_sizes
            ]
            + [pl.BlockSpec((2, 1, wide, span), lambda s, o: (0, s, 0, 0))] * chunks,
            scratch_shapes=[
                pltpu.VMEM((4, EXTRA, span * chunks), F32),
                pltpu.VMEM((wide, PAIR), F32),
                pltpu.VMEM((wide, PAIR), F32),
                pltpu.VMEM((wide, span), BF),
                pltpu.VMEM((chunks, 3, width, span), F32),
                pltpu.VMEM((heads, width + EXTRA, 4 * HEAD_DIM * chunks), BF),
            ],
        ),
        out_shape=[
            jax.ShapeDtypeStruct((size, heads, height + EXTRA, 4 * HEAD_DIM * chunks), BF)
            for size in group_sizes
        ]
        + [jax.ShapeDtypeStruct((2, seqs, wide, span), BF)] * chunks,
        compiler_params=params(60),
        cost_estimate=cost(6 * chunks * seqs * wide * width * span, 12 * chunks),
    )(offs, *operands, taps[:, :, first_chunk * span : (first_chunk + chunks) * span], same, xt, more)
    return out[: len(group_sizes)], out[len(group_sizes) :]


def input_grad_kernel(chunks, *refs):
    per_chunk = [refs[3 * n : 3 * n + 3] for n in range(chunks)]
    res_ref, mid_ref, first_ref, last_ref = refs[3 * chunks :]
    rows = mid_ref.shape[1]
    edge = None
    inner = res_ref[0]
    for dq_ref, low_ref, w_ref in per_chunk:
        inner = inner + nt(dq_ref[0], w_ref[0])
        for c in range(2):
            term = nt(low_ref[c, 0], w_ref[1 + c])
            edge = term if edge is None else edge + term
    mid_ref[0] = inner + edge[HALF : HALF + rows]
    first_ref[0] = edge[:HALF].astype(BF)
    last_ref[0] = edge[HALF + rows :].astype(BF)


def input_grad(parts, residual):
    seqs, rows, width = residual.shape
    wide, span = parts[0][1].shape[2:]
    in_specs, operands = [], []
    for dq, low, w in parts:
        in_specs += [
            pl.BlockSpec((1, rows, span), lambda s: (s, 0, 0)),
            pl.BlockSpec((2, 1, wide, span), lambda s: (0, s, 0, 0)),
            pl.BlockSpec(
                (3,) + w.shape[1:], lambda s: (0, 0, 0), pipeline_mode=pl.Buffered(1)
            ),
        ]
        operands += [dq, low, w]
    own = pl.BlockSpec((1, rows, width), lambda s: (s, 0, 0))
    edge = pl.BlockSpec((1, HALF, width), lambda s: (s, 0, 0))
    return pl.pallas_call(
        partial(input_grad_kernel, len(parts)),
        grid=(seqs,),
        in_specs=in_specs + [own],
        out_specs=[own, edge, edge],
        out_shape=[
            jax.ShapeDtypeStruct((seqs, rows, width), F32),
            jax.ShapeDtypeStruct((seqs, HALF, width), BF),
            jax.ShapeDtypeStruct((seqs, HALF, width), BF),
        ],
        compiler_params=params(60),
        cost_estimate=cost(6 * len(parts) * seqs * wide * width * span, 16),
    )(*operands, residual)


def after(value, *others):
    return lax.optimization_barrier((value,) + others)[0]


def finish_kernel(terms, chunks, *refs):
    groups = [refs[:terms], refs[terms : 2 * terms]]
    qkv_ref, out_ref, extra_ref, sums_ref = refs[2 * terms :]
    totals = []
    for group in groups:
        total = group[0][...].astype(F32)
        for ref in group[1:]:
            total = total + ref[...].astype(F32)
        totals.append(total)
    rows = out_ref.shape[0]
    sums_ref[...] = totals[0][rows:]
    lane = lax.broadcasted_iota(jnp.int32, (1, PAIR), 1) < HEAD_DIM
    first_count = totals[0].shape[1] // (4 * HEAD_DIM)

    def part(chunk, which, high):
        source = totals[0] if chunk < first_count else totals[1]
        chunk = chunk if chunk < first_count else chunk - first_count
        tile = 2 * chunk + which // 2
        values = source[:, tile * PAIR : (tile + 1) * PAIR]
        return values if which % 2 == high else pltpu.roll(values, HEAD_DIM, 1)

    for which in range(4):
        for chunk in range(0, chunks, 2):
            first = chunk * HEAD_DIM
            if chunk + 1 < chunks:
                made = jnp.where(lane, part(chunk, which, 0), part(chunk + 1, which, 1))
            else:
                made = part(chunk, which, 0)[:, :HEAD_DIM]
            lanes = slice(first, first + made.shape[1])
            if which < 3:
                qkv_ref[which, :, lanes] = made[:rows]
                extra_ref[which, :, lanes] = made[rows:]
            else:
                out_ref[:, lanes] = made[:rows]


def finish(groups, chunks):
    rows = groups[0][0].shape[0] - EXTRA
    local = chunks * HEAD_DIM
    return pl.pallas_call(
        partial(finish_kernel, len(groups[0]), chunks),
        out_shape=[
            jax.ShapeDtypeStruct((3, rows, local), F32),
            jax.ShapeDtypeStruct((rows, local), F32),
            jax.ShapeDtypeStruct((3, EXTRA, local), F32),
            jax.ShapeDtypeStruct((EXTRA, groups[0][0].shape[1]), F32),
        ],
        compiler_params=params(16),
        cost_estimate=cost(1, 1),
    )(*groups[0], *groups[1])


def swap(values, axis, mask):
    count = lax.axis_size(axis)
    return lax.ppermute(values, axis, [(i, i ^ mask) for i in range(count)])


def shift_right(rows):
    count = lax.axis_size("tp")
    return lax.ppermute(rows, "tp", [(i, i + 1) for i in range(count - 1)])


def shift_left(rows):
    count = lax.axis_size("tp")
    return lax.ppermute(rows, "tp", [(i + 1, i) for i in range(count - 1)])


def gather_columns(shard):
    if lax.axis_size("tp") != 4:
        return lax.all_gather(shard, "tp", axis=0, tiled=False)
    me = lax.axis_index("tp")
    found = [shard] + [swap(shard, "tp", mask) for mask in (1, 2, 3)]
    odd, high = me % 2 == 1, me >= 2
    found = [jnp.where(odd, found[n ^ 1], found[n]) for n in range(4)]
    return jnp.stack([jnp.where(high, found[n ^ 2], found[n]) for n in range(4)])


def gather_pieces(shard, beside):
    mine = lax.axis_index("fsdp")
    rows = shard.shape[0]
    half = rows // 2
    across = swap(shard, "fsdp", 2)
    along = swap(shard, "fsdp", 4)
    onward = after(across[:half], *beside)
    corner = [swap(onward, "fsdp", 4), swap(along[half:], "fsdp", 2)]
    own = [shard, across, along] + corner
    other = [swap(piece, "fsdp", 1) for piece in own]
    place = [
        (mine ^ mask) * rows + extra
        for core in (0, 1)
        for mask, extra in ((core, 0), (2 + core, 0), (4 + core, 0), (6 + core, 0), (6 + core, half))
    ]
    return own + other, jnp.stack(place).astype(jnp.int32)


def spread_line(values):
    return [swap(values, "tp", d) for d in range(1, lax.axis_size("tp"))]


def add_low(first, *others):
    total = first.astype(F32)
    for other in others:
        total = total + other.astype(F32)
    return total


def merge_cores(keep, send):
    return add_low(keep, swap(send, "fsdp", 1)).astype(BF)


def merge_chips(blocks, *beside):
    own = after(blocks[0], *beside) if beside else blocks[0]
    return add_low(own, *[swap(blocks[n], "fsdp", 2 * n) for n in (1, 2, 3)]).astype(BF)


def scatter_tp(blocks):
    count = lax.axis_size("tp")
    me = lax.axis_index("tp")

    def pick(d):
        return lax.dynamic_index_in_dim(blocks, me ^ d, 0, keepdims=False)

    return [pick(0)] + [swap(pick(d), "tp", d) for d in range(1, count)]


def spread_rows(whole, blocks):
    parts, rows, cols = whole.shape
    rows -= EXTRA
    main = whole[:, :rows].reshape(parts, blocks, rows // blocks, cols).transpose(1, 0, 2, 3)
    more = jnp.broadcast_to(whole[None, :, rows:], (blocks, parts, EXTRA, cols))
    return jnp.concatenate([main, more], axis=2)


def split_three(values):
    high = lax.reduce_precision(values, 8, 7)
    rest = values - high
    middle = lax.reduce_precision(rest, 8, 7)
    return jnp.stack([high, middle, rest - middle]).astype(BF)


def body(
    inputs, segments, w_qkv, qkv_bias, pool_kernel, w_out, out_bias,
    w_up, up_bias, w_down, norm_gains, norm_shifts, cotangent,
):
    rows, seqs, width = inputs.shape
    tp = lax.axis_size("tp")
    fsdp = lax.axis_size("fsdp")
    place = lax.axis_index("tp")
    shard_rows = w_qkv.shape[0]
    local = w_qkv.shape[2]
    chunks = local // HEAD_DIM
    span = tp * HEAD_DIM
    hidden_local = w_up.shape[1]
    hidden_units = hidden_local * tp
    far_rows = rows // STRIDE
    fast = fsdp == 8 and shard_rows % 32 == 0

    bias_values = jnp.concatenate(
        [qkv_bias.reshape(-1), pool_kernel.reshape(-1), up_bias.reshape(-1)]
    )
    biases = split_three(bias_values)
    extra = -(-biases.size // (4 * local))
    packed = jnp.concatenate(
        [
            jnp.concatenate([w_qkv.reshape(shard_rows, 3 * local), w_out], axis=1),
            jnp.pad(biases.reshape(-1), (0, extra * 4 * local - biases.size)).reshape(
                extra, 4 * local
            ),
        ],
        axis=0,
    )
    left = shift_right(inputs[rows - HALF :])
    right = shift_left(inputs[:HALF])
    columns = gather_columns(packed)
    wide_rows = (
        columns[:, :shard_rows]
        .reshape(tp, shard_rows, 4, chunks, HEAD_DIM)
        .transpose(1, 2, 3, 0, 4)
        .reshape(shard_rows, 4 * width)
    )
    whole_bias = jnp.sum(
        columns[:, shard_rows:].reshape(tp, -1)[:, : biases.size].reshape(tp, 3, -1).astype(F32),
        axis=1,
    )
    lead = (3 + 2 * TAPS) * local
    featured = (
        whole_bias[:, :lead]
        .reshape(tp, 3 + 2 * TAPS, chunks, HEAD_DIM)
        .transpose(1, 2, 0, 3)
        .reshape(3 + 2 * TAPS, width)
    )
    bias_qkv = featured[:3, None, :]
    taps = jnp.pad(featured[3:].reshape(2, TAPS, width), ((0, 0), (0, 8 - TAPS), (0, 0)))
    bias_up = whole_bias[:, lead:].reshape(1, hidden_units)

    x_wide = jnp.concatenate([left, inputs, right], axis=0).transpose(1, 0, 2)
    wide = rows + 2 * HALF

    seg_rows = segments.T
    padded = jnp.pad(seg_rows, ((0, 0), (HALF, HALF)), constant_values=-1)
    seg_keys = lax.dynamic_slice_in_dim(padded, place * rows, wide, 1)
    seg_own = seg_keys[:, HALF : HALF + rows]
    centers = seg_rows[:, ::STRIDE].reshape(seqs, tp, far_rows)
    centers_cycle = jnp.concatenate(
        [
            lax.dynamic_index_in_dim(centers, place ^ d, 1, keepdims=True)
            for d in range(tp)
        ],
        axis=1,
    ).reshape(seqs, 1, tp * far_rows)
    segs = (seg_own[:, :, None], seg_keys[:, None, :], centers_cycle)
    own_centers = seg_own[:, ::STRIDE]
    same = jnp.stack(
        [
            seg_keys[:, HALF - MARGIN + r : HALF - MARGIN + r + rows : STRIDE][:, :far_rows]
            == own_centers
            for r in range(TAPS)
        ]
        + [jnp.zeros_like(own_centers, dtype=bool)] * (8 - TAPS),
        axis=2,
    ).astype(F32)

    if fast:
        pieces, offs = gather_pieces(wide_rows, (x_wide, same, bias_qkv, taps) + segs)
    else:
        pieces = [lax.all_gather(wide_rows, "fsdp", axis=0, tiled=True)]
        offs = jnp.zeros((1,), jnp.int32)

    weights = lax.all_gather(
        jnp.concatenate([w_up, w_down], axis=1), "tp", axis=0, tiled=False
    )

    made, slots, att = [], [], []

    def send_pooled(j, *waits):
        pooled = made[j][1]
        sent = after(pooled, *waits) if waits else pooled
        slots.append([pooled] + spread_line(sent))

    for j in range(chunks):
        if j:
            offs = after(offs, made[-1][1])
        made.append(project(j, chunks, pieces, offs, x_wide, bias_qkv, taps, same, far_rows))
        if j == 0:
            send_pooled(0)
    if chunks > 1:
        send_pooled(1, made[-1][1], *slots[0][1:])
    weights = after(weights, made[0][1])
    weights = lax.all_gather(weights, "fsdp", axis=0, tiled=False)
    for j in range(chunks):
        order = segs
        if j == 1:
            x_cols = after(x_wide, att[0]).reshape(seqs * wide, width).T
            cot = after(cotangent, att[0]).transpose(1, 0, 2)
        if j:
            order = segs[:2] + (after(segs[2], att[-1], x_cols, cot),)
        att.append(attend_forward(made[j][0], slots[j], order))
        if j + 2 < chunks:
            send_pooled(j + 2, att[j])
    if shard_rows % 16:
        weights = weights.transpose(1, 0, 2, 3).reshape(1, tp, width, -1)

    misc = jnp.concatenate([out_bias, norm_gains, norm_shifts, jnp.zeros((2, width), F32)])
    outputs, grad_residual, grad_att, grad_out, gud, small = dense(
        att, [m[2] for m in made], x_wide, cot, weights, bias_up, misc
    )
    if gud.shape[0] == 1:
        gud = spread_rows(gud[0], fsdp)
    gud = lax.psum_scatter(gud, "fsdp", scatter_dimension=0, tiled=False)
    gud_parts = gud.reshape(2, shard_rows + EXTRA, tp, hidden_local).transpose(2, 0, 1, 3)
    gud = lax.psum_scatter(gud_parts, "tp", scatter_dimension=0, tiled=False).astype(F32)

    if fast:
        mine = lax.axis_index("fsdp")
        group_sizes = (4, 4)
        out_offs = jnp.stack(
            [(mine ^ m) * shard_rows for m in (0, 2, 4, 6, 1, 3, 5, 7)]
        ).astype(jnp.int32)
    else:
        group_sizes = (1,)
        out_offs = jnp.zeros((1,), jnp.int32)
    backs = []
    for j in range(chunks):
        order = segs
        if j:
            waits = (backs[-1][0],) + (tuple(backs[-2][3][1:]) if j > 1 else ())
            order = segs[:2] + (after(segs[2], *waits),)
        dq, dk, dv, dps = attend_backward(made[j][0], slots[j], order, grad_att[j])
        if j:
            dps = [after(d, *backs[-1][3][1:]) for d in dps]
        arrived = [dps[0]] + [swap(dps[d], "tp", d) for d in range(1, tp)]
        backs.append((dq, dk, dv, arrived, made[j][0], grad_out[j]))
    totals, lows, merged = [], [], []
    for low, high in ((0, chunks - 1), (chunks - 1, chunks)):
        if low == high:
            continue
        cols = (high - low) * 4 * HEAD_DIM
        more = jnp.zeros((EXTRA, cols), F32)
        if not merged:
            flat = small[:6].reshape(-1)
            lines = -(-flat.size // cols)
            flat = jnp.pad(flat, (0, lines * cols - flat.size)).reshape(lines, cols)
            more = jnp.pad(flat, ((TAPS + 1, EXTRA - TAPS - 1 - lines), (0, 0)))
        waits = [backs[-1][0]] + ([gud_parts] if merged else [])
        groups, low_kv = gather_back(
            low, after(out_offs, *waits), group_sizes, backs[low:high], taps, same, x_cols, more
        )
        lows += low_kv
        if fast:
            merged.append(merge_cores(*[after(g, *backs[-1][3][1:]) for g in groups]))
        else:
            merged.append(spread_rows(groups[0][0], fsdp))
    middle, first, last = input_grad(
        [(backs[n][0], lows[n], made[n][2]) for n in range(chunks)], grad_residual
    )
    middle = middle.transpose(1, 0, 2)
    chips = []
    for n, blocks in enumerate(merged):
        blocks = after(blocks, *chips) if chips else blocks
        if fast:
            chips.append(merge_chips(blocks, *([] if chips else [middle])))
        else:
            chips.append(lax.psum_scatter(blocks, "fsdp", scatter_dimension=0, tiled=False))
    for blocks in chips:
        if len(totals) + 1 == len(chips):
            blocks = after(blocks, middle)
        else:
            blocks = after(blocks, merged[-1])
        totals.append(scatter_tp(blocks))

    first, last = after(first, chips[-1]), after(last, chips[-1])
    to_left = shift_left(first).transpose(1, 0, 2)
    to_right = shift_right(last).transpose(1, 0, 2)
    grad_inputs = middle.at[:HALF].add(to_right.astype(F32))
    grad_inputs = grad_inputs.at[rows - HALF :].add(to_left.astype(F32))

    grad_w_qkv, grad_w_out, extra_rows, sums = finish(totals, chunks)
    sums = sums[TAPS + 1 :].reshape(-1)[: 6 * width].reshape(6, width)
    return (
        outputs.transpose(1, 0, 2),
        grad_inputs,
        grad_w_qkv.transpose(1, 0, 2),
        extra_rows[:, 0],
        extra_rows[1:, 1 : TAPS + 1],
        grad_w_out,
        sums[0:2],
        gud[0, :shard_rows],
        gud[0, shard_rows],
        gud[1, :shard_rows],
        sums[2:4],
        sums[4:6],
    )


def solution(mesh):
    placed = (
        P("tp", "fsdp", None),
        P(None, "fsdp"),
        P("fsdp", None, "tp"),
        P(None, "tp"),
        P(None, None, "tp"),
        P("fsdp", "tp"),
        P(),
        P("fsdp", "tp"),
        P("tp"),
        P("fsdp", "tp"),
        P(),
        P(),
        P("tp", "fsdp", None),
    )
    return jax.shard_map(
        body,
        mesh=mesh,
        in_specs=placed,
        out_specs=(
            P("tp", "fsdp", None),
            P("tp", "fsdp", None),
            P("fsdp", None, "tp"),
            P(None, "tp"),
            P(None, None, "tp"),
            P("fsdp", "tp"),
            P(),
            P("fsdp", "tp"),
            P("tp"),
            P("fsdp", "tp"),
            P(),
            P(),
        ),
        check_vma=False,
    )
```

```python
from functools import partial

import jax
import jax.numpy as jnp
import numpy as np
from jax import lax
from jax.experimental import pallas as pl
from jax.experimental.pallas import tpu as pltpu
from jax.sharding import PartitionSpec as P

HEAD_DIM = 64
HALF = 64
STRIDE = 4
TAPS = 5
MARGIN = TAPS // 2
PAIR = 2 * HEAD_DIM
QB = 128
SB = 128
NEAR = QB + 2 * HALF
EXTRA = 16
RC = 256
EPSILON = 1e-05
NEG = -1e30
SCALE = HEAD_DIM**-0.5
BF = jnp.bfloat16
F32 = jnp.float32
MIB = 2**20


def nt(a, b):
    return lax.dot_general(a, b, (((1,), (1,)), ((), ())), preferred_element_type=F32)


def nn(a, b):
    return lax.dot_general(a, b, (((1,), (0,)), ((), ())), preferred_element_type=F32)


def tn(a, b):
    return lax.dot_general(a, b, (((0,), (0,)), ((), ())), preferred_element_type=F32)


def params(mib):
    return pltpu.CompilerParams(vmem_limit_bytes=mib * MIB)


def cost(flops, mib, trans=0):
    return pl.CostEstimate(flops=1, bytes_accessed=1, transcendentals=0)


def once(shape):
    zeros = (0,) * len(shape)
    return pl.BlockSpec(shape, lambda *_: zeros, pipeline_mode=pl.Buffered(1))


def project_kernel(count, offs, *refs):
    pieces = refs[:count]
    x_ref, bias_ref, taps_ref, same_ref, out_ref, pooled_ref, w_ref, plain = refs[count:]
    part = pl.program_id(0)
    for n in range(count):
        rows = pieces[n].shape[0]
        w_ref[0, pl.ds(pl.multiple_of(offs[n], 16), rows), :] = pieces[n][...]
    seqs, wide, _ = x_ref.shape
    far_rows = pooled_ref.shape[2]

    @pl.when(part < 3)
    def _():
        for s in range(seqs):
            made = (nn(x_ref[s], w_ref[0]) + bias_ref[0]).astype(BF)
            out_ref[0, s] = made
            for half in range(plain.shape[1]):
                plain[s, half] = made[:, half * PAIR : (half + 1) * PAIR].astype(F32)

    @pl.when((part > 0) & (part < 3))
    def _():
        for s in range(seqs):
            for half in range(plain.shape[1]):
                lanes = slice(half * PAIR, (half + 1) * PAIR)
                total = jnp.zeros((far_rows, PAIR), F32)
                for r in range(TAPS):
                    rows = plain[s, half, pl.ds(HALF - MARGIN + r, far_rows, stride=STRIDE), :]
                    total = total + taps_ref[0, r : r + 1, lanes] * rows * same_ref[
                        s, :, r : r + 1
                    ]
                pooled_ref[0, s, :, lanes] = total.astype(BF)


def project(chunk, chunks, pieces, offs, x_wide, bias, taps, same, far_rows):
    seqs, wide, width = x_wide.shape
    span = width // chunks

    def piece_spec(piece):
        return pl.BlockSpec((piece.shape[0], span), lambda c, o: (0, c * chunks + chunk))

    def three(c):
        return jnp.minimum(c, 2)

    def kv(c):
        return jnp.maximum(three(c) - 1, 0)

    return pl.pallas_call(
        partial(project_kernel, len(pieces)),
        grid_spec=pltpu.PrefetchScalarGridSpec(
            num_scalar_prefetch=1,
            grid=(4,),
            in_specs=[piece_spec(p) for p in pieces]
            + [
                once(x_wide.shape),
                pl.BlockSpec((1, 1, span), lambda c, o: (three(c), 0, chunk)),
                pl.BlockSpec((1, 8, span), lambda c, o: (kv(c), 0, chunk)),
                once(same.shape),
            ],
            out_specs=[
                pl.BlockSpec((1, seqs, wide, span), lambda c, o: (three(c), 0, 0, 0)),
                pl.BlockSpec((1, seqs, far_rows, span), lambda c, o: (kv(c), 0, 0, 0)),
                pl.BlockSpec((1, width, span), lambda c, o: (c, 0, 0)),
            ],
            scratch_shapes=[pltpu.VMEM((seqs, span // PAIR, wide, PAIR), F32)],
        ),
        out_shape=[
            jax.ShapeDtypeStruct((3, seqs, wide, span), BF),
            jax.ShapeDtypeStruct((2, seqs, far_rows, span), BF),
            jax.ShapeDtypeStruct((4, width, span), BF),
        ],
        compiler_params=params(32),
        cost_estimate=cost(6 * seqs * wide * width * span, 8),
    )(offs, *pieces, x_wide, bias, taps, same)


def fill_masks(segq_ref, segk_ref, cen_ref, near_bias, far_bias):
    rows = segq_ref.shape[1]
    shape = (QB, NEAR)
    gap = lax.broadcasted_iota(jnp.int32, shape, 1) - lax.broadcasted_iota(jnp.int32, shape, 0)
    band = (gap >= 0) & (gap <= 2 * HALF)
    for first in range(0, rows, QB):
        own = segq_ref[0, first : first + QB, :]
        keys = segk_ref[0, :, first : first + NEAR]
        near_bias[first : first + QB, :] = jnp.where(band & (own == keys), 0.0, NEG)
        far_bias[first : first + QB, :] = jnp.where(own == cen_ref[0], 0.0, NEG)


def head_mask(head):
    lane = lax.broadcasted_iota(jnp.int32, (1, PAIR), 1)
    return lane < HEAD_DIM if head == 0 else lane >= HEAD_DIM


def fold_lanes(*arrays):
    parts = [a[:, n : n + PAIR] for a in arrays for n in range(0, a.shape[1], PAIR)]
    while len(parts) > 1:
        parts = [sum(parts[n : n + 2]) for n in range(0, len(parts), 2)]
    return parts[0]


def softmax_rows(near, far):
    top = jnp.maximum(
        jnp.max(near, axis=-1, keepdims=True), jnp.max(far, axis=-1, keepdims=True)
    )
    near = jnp.exp(near - top)
    far = jnp.exp(far - top)
    total = jnp.sum(near, axis=-1, keepdims=True) + jnp.sum(far, axis=-1, keepdims=True)
    inverse = 1.0 / total
    return near * inverse, far * inverse


def stack_heads(rows, stacked):
    for first in range(0, rows.shape[0], QB):
        part = rows[first : first + QB]
        for head in range(2):
            stacked[2 * first + head * QB : 2 * first + (head + 1) * QB, :] = jnp.where(
                head_mask(head), part, BF(0)
            )


def join_slots(slots, joined):
    rows = slots[0].shape[1]
    for n, slot in enumerate(slots):
        joined[n * rows : (n + 1) * rows, :] = slot[0]


def attend_forward_kernel(blocks, q_ref, k_ref, v_ref, *refs):
    pk, pv = refs[:blocks], refs[blocks : 2 * blocks]
    segq, segk, cen, out_ref = refs[2 * blocks : 2 * blocks + 4]
    near_bias, far_bias, far_keys, far_values, query, far_scores, far_probs = refs[
        2 * blocks + 4 :
    ]

    @pl.when(pl.program_id(1) == 0)
    def _():
        fill_masks(segq, segk, cen, near_bias, far_bias)

    rows = out_ref.shape[1]
    join_slots(pk, far_keys)
    join_slots(pv, far_values)
    stack_heads(q_ref[0, HALF : HALF + rows, :] * BF(SCALE), query)
    far_scores[...] = nt(query[...], far_keys[...])
    outs = []
    for first in range(0, rows, QB):
        span = slice(first, first + NEAR)
        pair = slice(2 * first, 2 * first + 2 * QB)
        near_all = nt(query[pair, :], k_ref[0, span, :])
        lows = []
        for part in range(0, 2 * QB, SB):
            source = first + part % QB
            near, far = softmax_rows(
                near_all[part : part + SB] + near_bias[source : source + SB, :],
                far_scores[2 * first + part : 2 * first + part + SB, :]
                + far_bias[source : source + SB, :],
            )
            far_probs[2 * first + part : 2 * first + part + SB, :] = far.astype(BF)
            lows.append(near.astype(BF))
        outs.append(nn(jnp.concatenate(lows, axis=0), v_ref[0, span, :]))
    far_out = nn(far_probs[...], far_values[...])
    for n, first in enumerate(range(0, rows, QB)):
        both = outs[n] + far_out[2 * first : 2 * first + 2 * QB]
        out_ref[0, first : first + QB, :] = jnp.where(head_mask(0), both[:QB], both[QB:]).astype(BF)


def attend_backward_kernel(blocks, q_ref, k_ref, v_ref, *refs):
    pk, pv = refs[:blocks], refs[blocks : 2 * blocks]
    segq, segk, cen, grad_ref, dq_ref, dk_ref, dv_ref = refs[2 * blocks : 2 * blocks + 7]
    dp_refs = refs[2 * blocks + 7 : 2 * blocks + 9]
    (
        near_bias, far_bias, far_keys, far_values,
        query, far_scores, far_probs, grad, far_dots, far_grads,
    ) = refs[2 * blocks + 9 :]

    @pl.when(pl.program_id(1) == 0)
    def _():
        fill_masks(segq, segk, cen, near_bias, far_bias)

    rows = dq_ref.shape[1]
    join_slots(pk, far_keys)
    join_slots(pv, far_values)
    stack_heads(q_ref[0, HALF : HALF + rows, :] * BF(SCALE), query)
    stack_heads(grad_ref[0], grad)
    far_scores[...] = nt(query[...], far_keys[...])
    far_dots[...] = nt(grad[...], far_values[...])
    dk_ref[...] = jnp.zeros_like(dk_ref)
    dv_ref[...] = jnp.zeros_like(dv_ref)
    dqs = []
    for first in range(0, rows, QB):
        span = slice(first, first + NEAR)
        pair = slice(2 * first, 2 * first + 2 * QB)
        near_all = nt(query[pair, :], k_ref[0, span, :])
        dots_all = nt(grad[pair, :], v_ref[0, span, :])
        lows, grads = [], []
        for part in range(0, 2 * QB, SB):
            source = first + part % QB
            here = slice(2 * first + part, 2 * first + part + SB)
            near, far = softmax_rows(
                near_all[part : part + SB] + near_bias[source : source + SB, :],
                far_scores[here, :] + far_bias[source : source + SB, :],
            )
            near_dot, far_dot = dots_all[part : part + SB], far_dots[here, :]
            row_dot = jnp.sum(
                fold_lanes(near * near_dot, far * far_dot), axis=-1, keepdims=True
            )
            far_probs[here, :] = far.astype(BF)
            far_grads[here, :] = (far * (far_dot - row_dot)).astype(BF)
            lows.append(near.astype(BF))
            grads.append((near * (near_dot - row_dot)).astype(BF))
        low = jnp.concatenate(lows, axis=0)
        ds = jnp.concatenate(grads, axis=0)
        dqs.append(nn(ds, k_ref[0, span, :]))
        dk_ref[0, span, :] += nn(query[pair, :].T, ds).T
        dv_ref[0, span, :] += nn(grad[pair, :].T, low).T
    far_dq = nn(far_grads[...], far_keys[...])
    for n, first in enumerate(range(0, rows, QB)):
        both = (dqs[n] + far_dq[2 * first : 2 * first + 2 * QB]) * SCALE
        dq_ref[0, first : first + QB, :] = jnp.where(head_mask(0), both[:QB], both[QB:]).astype(BF)
    dpk = nn(query[...].T, far_grads[...]).T.astype(BF)
    dpv = nn(grad[...].T, far_probs[...]).T.astype(BF)
    far_rows = dp_refs[0].shape[3]
    for n in range(blocks):
        span = slice(n * far_rows, (n + 1) * far_rows)
        dp_refs[n % 2][n // 2, 0, 0] = dpk[span]
        dp_refs[n % 2][n // 2, 1, 0] = dpv[span]


def attention_specs(wide, blocks, far_rows):
    def own(part):
        return pl.BlockSpec((None, 1, wide, PAIR), lambda s, h: (part, s, 0, h))

    def pooled(part):
        return pl.BlockSpec((None, 1, far_rows, PAIR), lambda s, h: (part, s, 0, h))

    rows = wide - 2 * HALF
    return (
        [own(0), own(1), own(2)]
        + [pooled(0)] * blocks
        + [pooled(1)] * blocks
        + [
            pl.BlockSpec((1, rows, 1), lambda s, h: (s, 0, 0)),
            pl.BlockSpec((1, 1, wide), lambda s, h: (s, 0, 0)),
            pl.BlockSpec((1, 1, blocks * far_rows), lambda s, h: (s, 0, 0)),
        ]
    )


def attention_scratch(rows, far_all):
    return [
        pltpu.VMEM((rows, NEAR), F32),
        pltpu.VMEM((rows, far_all), F32),
        pltpu.VMEM((far_all, PAIR), BF),
        pltpu.VMEM((far_all, PAIR), BF),
        pltpu.VMEM((2 * rows, PAIR), BF),
        pltpu.VMEM((2 * rows, far_all), F32),
        pltpu.VMEM((2 * rows, far_all), BF),
    ]


def attend_forward(proj, slots, segs):
    _, seqs, wide, span = proj.shape
    blocks, far_rows = len(slots), slots[0].shape[2]
    rows = wide - 2 * HALF
    cells = seqs * rows * (NEAR + blocks * far_rows) * (span // HEAD_DIM)
    return pl.pallas_call(
        partial(attend_forward_kernel, blocks),
        grid=(seqs, span // PAIR),
        in_specs=attention_specs(wide, blocks, far_rows),
        out_specs=pl.BlockSpec((1, rows, PAIR), lambda s, h: (s, 0, h)),
        out_shape=jax.ShapeDtypeStruct((seqs, rows, span), BF),
        scratch_shapes=attention_scratch(rows, blocks * far_rows),
        compiler_params=params(60),
        cost_estimate=cost(16 * 64 * cells, 8, cells),
    )(proj, proj, proj, *slots, *slots, *segs)


def attend_backward(proj, slots, segs, grad):
    _, seqs, wide, span = proj.shape
    blocks, far_rows = len(slots), slots[0].shape[2]
    rows = wide - 2 * HALF
    cells = seqs * rows * (NEAR + blocks * far_rows) * (span // HEAD_DIM)
    own_spec = pl.BlockSpec((1, rows, PAIR), lambda s, h: (s, 0, h))
    wide_spec = pl.BlockSpec((1, wide, PAIR), lambda s, h: (s, 0, h))
    wide_shape = jax.ShapeDtypeStruct((seqs, wide, span), F32)
    far_spec = pl.BlockSpec((blocks // 2, 2, 1, far_rows, PAIR), lambda s, h: (0, 0, s, 0, h))
    far_shape = jax.ShapeDtypeStruct((blocks // 2, 2, seqs, far_rows, span), BF)
    out = pl.pallas_call(
        partial(attend_backward_kernel, blocks),
        grid=(seqs, span // PAIR),
        in_specs=attention_specs(wide, blocks, far_rows) + [own_spec],
        out_specs=[own_spec, wide_spec, wide_spec] + [far_spec] * 2,
        out_shape=[jax.ShapeDtypeStruct((seqs, rows, span), BF), wide_shape, wide_shape]
        + [far_shape] * 2,
        scratch_shapes=attention_scratch(rows, blocks * far_rows)
        + [
            pltpu.VMEM((2 * rows, PAIR), BF),
            pltpu.VMEM((2 * rows, blocks * far_rows), F32),
            pltpu.VMEM((2 * rows, blocks * far_rows), BF),
        ],
        compiler_params=params(60),
        cost_estimate=cost(40 * 64 * cells, 16, cells),
    )(proj, proj, proj, *slots, *slots, *segs, grad)
    return out[0], out[1], out[2], out[3:]


def norm_stats(residual):
    row_mean = jnp.mean(residual, axis=-1, keepdims=True)
    centered = residual - row_mean
    variance = jnp.mean(centered * centered, axis=-1, keepdims=True)
    inverse = lax.rsqrt(variance + EPSILON)
    return centered * inverse, inverse


def norm_back(grad, normed, inverse, gain):
    scaled = grad * gain
    first = jnp.mean(scaled, axis=-1, keepdims=True)
    second = jnp.mean(scaled * normed, axis=-1, keepdims=True)
    return (scaled - first - normed * second) * inverse


def column_sum(values):
    return jnp.sum(values.astype(F32), axis=0, keepdims=True)


def dense_kernel(chunks, steps, *refs):
    att, wout = refs[:chunks], refs[chunks : 2 * chunks]
    x_ref, cot_ref, up_blk, down_blk, bup_ref, misc_ref = refs[2 * chunks : 2 * chunks + 6]
    outs = refs[2 * chunks + 6 :]
    out_ref, gres_ref = outs[:2]
    gatt = outs[2 : 2 + chunks]
    gout = outs[2 + chunks : 2 + 2 * chunks]
    gud_ref, small_ref = outs[2 + 2 * chunks : 4 + 2 * chunks]
    (
        inverse, flow, flow_t, acc, gffn, gffn_t, hidden, slope, gpre
    ) = outs[4 + 2 * chunks :]
    step = pl.program_id(0)
    seqs, rows, width = cot_ref.shape
    total = seqs * rows
    span = width // chunks
    units = gpre.shape[1]
    up_ref = up_blk[...].reshape(width, units)
    down_ref = down_blk[...].reshape(width, units)
    bias_one, bias_two = misc_ref[0:1, :], misc_ref[1:2, :]
    gain_one, gain_two = misc_ref[2:3, :], misc_ref[3:4, :]
    shift_one, shift_two = misc_ref[4:5, :], misc_ref[5:6, :]
    parts = [(first, first // rows, first % rows) for first in range(0, total, RC)]

    @pl.when(step == 0)
    def _():
        for first, s, row in parts:
            block = slice(first, first + RC)
            branch = bias_one
            for j in range(chunks):
                branch = branch + nt(
                    att[j][s, row : row + RC, :], wout[j][0]
                )
            n_one, inv = norm_stats(
                x_ref[s, HALF + row : HALF + row + RC, :].astype(F32) + branch
            )
            gres_ref[s, row : row + RC, :] = n_one
            inverse[block, :] = inv
            low = (n_one * gain_one + shift_one).astype(BF)
            flow[block, :] = low
            flow_t[:, block] = low.T
            acc[block, :] = jnp.zeros((RC, width), F32)

    @pl.when(step < steps)
    def _():
        for first, s, row in parts:
            block = slice(first, first + RC)
            pre = nn(flow[block, :], up_ref) + bup_ref[...]
            cdf = 0.5 * (1.0 + lax.erf(pre * np.float32(np.sqrt(0.5))))
            pdf = jnp.exp(-0.5 * (pre * pre)) * np.float32(1.0 / np.sqrt(2.0 * np.pi))
            low = (pre * cdf).astype(BF)
            hidden[step, block, :] = low
            slope[step, block, :] = cdf + pre * pdf
            acc[block, :] += nt(low, down_ref)

    @pl.when(step == steps)
    def _():
        small_ref[...] = jnp.zeros_like(small_ref)
        for first, s, row in parts:
            block = slice(first, first + RC)
            first_out = gres_ref[s, row : row + RC, :] * gain_one + shift_one
            n_two, inv = norm_stats(first_out + (acc[block, :] + bias_two))
            out_ref[s, row : row + RC, :] = (n_two * gain_two + shift_two).astype(BF)
            grad = cot_ref[s, row : row + RC, :].astype(F32)
            second = norm_back(grad, n_two, inv, gain_two)
            acc[block, :] = second
            low = second.astype(BF)
            gffn[block, :] = low
            gffn_t[:, block] = low.T
            small_ref[1:2, :] += column_sum(low)
            small_ref[3:4, :] += column_sum(grad * n_two)
            small_ref[5:6, :] += column_sum(grad)

    @pl.when(step >= steps)
    def _():
        which = 2 * steps - 1 - step
        bias_sum = jnp.zeros((1, units), F32)
        for first, s, row in parts:
            block = slice(first, first + RC)
            grad = nn(gffn[block, :], down_ref)
            low = (grad * slope[which, block, :]).astype(BF)
            gpre[block, :] = low
            bias_sum = bias_sum + column_sum(low)
            acc[block, :] += nt(low, up_ref)
        height = gud_ref.shape[3] - EXTRA
        lead = (gud_ref.shape[0], height, units)
        gud_ref[:, 0, 0, :height] = nn(flow_t[...], gpre[...]).astype(BF).reshape(lead)
        gud_ref[:, 0, 1, :height] = nn(gffn_t[...], hidden[which]).astype(BF).reshape(lead)
        head = lax.broadcasted_iota(jnp.int32, (EXTRA, 1), 0) == 0
        extra = jnp.where(head, bias_sum, 0.0).astype(BF)
        for m in range(gud_ref.shape[0]):
            gud_ref[m, 0, 0, height:] = extra
            gud_ref[m, 0, 1, height:] = jnp.zeros((EXTRA, units), BF)

    @pl.when(step == 2 * steps - 1)
    def _():
        for first, s, row in parts:
            block = slice(first, first + RC)
            grad = acc[block, :]
            n_one = gres_ref[s, row : row + RC, :]
            back = norm_back(grad, n_one, inverse[block, :], gain_one)
            gres_ref[s, row : row + RC, :] = back
            low = back.astype(BF)
            flow_t[:, block] = low.T
            small_ref[0:1, :] += column_sum(low)
            small_ref[2:3, :] += column_sum(grad * n_one)
            small_ref[4:5, :] += column_sum(grad)
            for j in range(chunks):
                gatt[j][s, row : row + RC, :] = nn(
                    low, wout[j][0]
                ).astype(BF)
        for j in range(chunks):
            gout[j][...] = nn(flow_t[...], att[j][...].reshape(total, span)).astype(BF)


def dense(att, projected_weights, x_wide, cot, weights, bias_up, misc):
    chunks = len(att)
    seqs, rows, width = cot.shape
    total = seqs * rows
    span = width // chunks
    row_blocks, steps, height, units = weights.shape
    units //= 2

    def which(i):
        return jnp.where(i < steps, i, 2 * steps - 1 - i)

    def back(i):
        return jnp.where(i < steps, steps - 1, 2 * steps - 1 - i)

    out_shape = (
        [
            jax.ShapeDtypeStruct((seqs, rows, width), BF),
            jax.ShapeDtypeStruct((seqs, rows, width), F32),
        ]
        + [jax.ShapeDtypeStruct((seqs, rows, span), BF)] * chunks
        + [jax.ShapeDtypeStruct((width, span), BF)] * chunks
        + [
            jax.ShapeDtypeStruct((row_blocks, steps, 2, height + EXTRA, units), BF),
            jax.ShapeDtypeStruct((8, width), F32),
        ]
    )
    out_specs = [once(o.shape) for o in out_shape[: 2 + 2 * chunks]] + [
        pl.BlockSpec(
            (row_blocks, 1, 2, height + EXTRA, units), lambda i: (0, back(i), 0, 0, 0)
        ),
        once((8, width)),
    ]
    out = pl.pallas_call(
        partial(dense_kernel, chunks, steps),
        grid=(2 * steps,),
        in_specs=[once(a.shape) for a in att]
        + [
            pl.BlockSpec(
                (1, width, span), lambda i: (3, 0, 0), pipeline_mode=pl.Buffered(1)
            )
        ]
        * chunks
        + [
            once(x_wide.shape),
            once(cot.shape),
            pl.BlockSpec((row_blocks, None, height, units), lambda i: (0, which(i), 0, 0)),
            pl.BlockSpec((row_blocks, None, height, units), lambda i: (0, which(i), 0, 1)),
            pl.BlockSpec((1, units), lambda i: (0, which(i))),
            once(misc.shape),
        ],
        out_specs=out_specs,
        out_shape=out_shape,
        scratch_shapes=[
            pltpu.VMEM((total, 1), F32),
            pltpu.VMEM((total, width), BF),
            pltpu.VMEM((width, total), BF),
            pltpu.VMEM((total, width), F32),
            pltpu.VMEM((total, width), BF),
            pltpu.VMEM((width, total), BF),
            pltpu.VMEM((steps, total, units), BF),
            pltpu.VMEM((steps, total, units), F32),
            pltpu.VMEM((total, units), BF),
        ],
        compiler_params=params(63),
        cost_estimate=cost(1, 1),
    )(*att, *projected_weights, x_wide, cot, weights, weights, bias_up, misc)
    return (
        out[0], out[1], out[2 : 2 + chunks], out[2 + chunks : 2 + 2 * chunks], out[-2], out[-1]
    )


def gather_back_kernel(blocks, chunks, groups, offs, *refs):
    taken = 5 + blocks + 1
    per_chunk = [refs[n * taken : (n + 1) * taken] for n in range(chunks)]
    taps_ref, same_ref, xt_ref, more_ref = refs[chunks * taken : chunks * taken + 4]
    outs = refs[chunks * taken + 4 :]
    gws = outs[:groups]
    lows = outs[groups : groups + chunks]
    small, plain, spread, low_q, total, stage = outs[groups + chunks :]
    width = xt_ref.shape[0]
    seq = pl.program_id(0)
    wide, span = per_chunk[0][0].shape[1:]
    rows = wide - 2 * HALF
    far_rows = per_chunk[0][3].shape[2]

    @pl.when(seq == 0)
    def _():
        small[...] = jnp.zeros_like(small)
        total[...] = jnp.zeros_like(total)

    for n, chunk_refs in enumerate(per_chunk):
        dk_ref, dv_ref, dq_ref = chunk_refs[:3]
        dps = chunk_refs[3 : 3 + blocks]
        proj_k, proj_v = chunk_refs[3 + blocks : 5 + blocks]
        low = lows[n]
        base = n * span
        low_q[:HALF, :] = jnp.zeros((HALF, span), BF)
        low_q[HALF : HALF + rows, :] = dq_ref[0]
        low_q[HALF + rows :, :] = jnp.zeros((HALF, span), BF)
        small[0, 0:1, base : base + span] += column_sum(dq_ref[0])
        for c, (near, proj) in enumerate(((dk_ref, proj_k), (dv_ref, proj_v))):
            for half in range(span // PAIR):
                lanes = slice(half * PAIR, (half + 1) * PAIR)
                wider = slice(base + half * PAIR, base + (half + 1) * PAIR)
                plain[...] = proj[0, 0, :, lanes].astype(F32)
                spread[...] = near[0, :, lanes]
                pooled = dps[0][c, 0, :, lanes].astype(F32)
                for d in range(1, blocks):
                    pooled = pooled + dps[d][c, 0, :, lanes].astype(F32)
                pooled = pooled.astype(BF).astype(F32)
                for r in range(TAPS):
                    place = pl.ds(HALF - MARGIN + r, far_rows, stride=STRIDE)
                    masked = pooled * same_ref[0, :, r : r + 1]
                    small[1 + c, 1 + r : 2 + r, wider] += column_sum(masked * plain[place, :])
                    spread[place, :] = spread[place, :] + taps_ref[c, r : r + 1, wider] * masked
                made = spread[...].astype(BF)
                low[c, 0, :, lanes] = made
                small[1 + c, 0:1, wider] += column_sum(made)
        total[n, 0] += nn(xt_ref[...], low_q[...])
        total[n, 1] += nn(xt_ref[...], low[0, 0])
        total[n, 2] += nn(xt_ref[...], low[1, 0])

    @pl.when(seq == pl.num_programs(0) - 1)
    def _():
        heads = span // HEAD_DIM
        lane = lax.broadcasted_iota(jnp.int32, (1, PAIR), 1) < HEAD_DIM

        def place_four(four, n, u, where):
            turned = [pltpu.roll(value, HEAD_DIM, 1) for value in four]
            for pair in range(2):
                one, two = 2 * pair, 2 * pair + 1
                first = (2 * n + pair) * PAIR
                lanes = slice(first, first + PAIR)
                stage[2 * u, where, lanes] = jnp.where(lane, four[one], turned[two]).astype(BF)
                stage[2 * u + 1, where, lanes] = jnp.where(lane, turned[one], four[two]).astype(BF)

        for n, chunk_refs in enumerate(per_chunk):
            gout_ref = chunk_refs[5 + blocks]
            for u in range(heads // 2):
                lanes = slice(u * PAIR, (u + 1) * PAIR)
                wider = slice(n * span + u * PAIR, n * span + (u + 1) * PAIR)
                four = [total[n, part, :, lanes] for part in range(3)]
                four.append(gout_ref[:, lanes].astype(F32))
                place_four(four, n, u, slice(0, width))
                place_four(
                    [small[part, :, wider] for part in range(4)], n, u, slice(width, width + EXTRA)
                )
        last = slice(width, width + EXTRA)
        head = lax.broadcasted_iota(jnp.int32, (EXTRA, 1), 0) <= TAPS
        for t in range(heads):
            stage[t, last, :] = jnp.where(
                head, stage[t, last, :].astype(F32), more_ref[...]
            ).astype(BF)
        height = gws[0].shape[2] - EXTRA
        number = 0
        for group in gws:
            for m in range(group.shape[0]):
                place = pl.ds(pl.multiple_of(offs[number], 16), height)
                group[m, :, :height] = stage[:, place, :]
                group[m, :, height:] = stage[:, last, :]
                number += 1


def gather_back(first_chunk, offs, group_sizes, parts, taps, same, xt, more):
    chunks = len(parts)
    seqs, wide, span = parts[0][1].shape
    width = xt.shape[0]
    rows = wide - 2 * HALF
    blocks, far_rows = len(parts[0][3]), parts[0][3][0].shape[2]
    height = width // sum(group_sizes)
    heads = span // HEAD_DIM
    in_specs, operands = [], []
    for dq, dk, dv, dps, proj, gout in parts:
        in_specs += [pl.BlockSpec((1, wide, span), lambda s, o: (s, 0, 0))] * 2
        in_specs += [pl.BlockSpec((1, rows, span), lambda s, o: (s, 0, 0))]
        in_specs += [pl.BlockSpec((2, 1, far_rows, span), lambda s, o: (0, s, 0, 0))] * blocks
        in_specs += [
            pl.BlockSpec((1, 1, wide, span), lambda s, o: (1, s, 0, 0)),
            pl.BlockSpec((1, 1, wide, span), lambda s, o: (2, s, 0, 0)),
            once(gout.shape),
        ]
        operands += [dk, dv, dq, *dps, proj, proj, gout]
    out = pl.pallas_call(
        partial(gather_back_kernel, blocks, chunks, len(group_sizes)),
        grid_spec=pltpu.PrefetchScalarGridSpec(
            num_scalar_prefetch=1,
            grid=(seqs,),
            in_specs=in_specs
            + [
                once((2, 8, span * chunks)),
                pl.BlockSpec((1, far_rows, 8), lambda s, o: (s, 0, 0)),
                pl.BlockSpec((width, wide), lambda s, o: (0, s)),
                once(more.shape),
            ],
            out_specs=[
                once((size, heads, height + EXTRA, 4 * HEAD_DIM * chunks)) for size in group_sizes
            ]
            + [pl.BlockSpec((2, 1, wide, span), lambda s, o: (0, s, 0, 0))] * chunks,
            scratch_shapes=[
                pltpu.VMEM((4, EXTRA, span * chunks), F32),
                pltpu.VMEM((wide, PAIR), F32),
                pltpu.VMEM((wide, PAIR), F32),
                pltpu.VMEM((wide, span), BF),
                pltpu.VMEM((chunks, 3, width, span), F32),
                pltpu.VMEM((heads, width + EXTRA, 4 * HEAD_DIM * chunks), BF),
            ],
        ),
        out_shape=[
            jax.ShapeDtypeStruct((size, heads, height + EXTRA, 4 * HEAD_DIM * chunks), BF)
            for size in group_sizes
        ]
        + [jax.ShapeDtypeStruct((2, seqs, wide, span), BF)] * chunks,
        compiler_params=params(60),
        cost_estimate=cost(6 * chunks * seqs * wide * width * span, 12 * chunks),
    )(offs, *operands, taps[:, :, first_chunk * span : (first_chunk + chunks) * span], same, xt, more)
    return out[: len(group_sizes)], out[len(group_sizes) :]


def input_grad_kernel(chunks, *refs):
    per_chunk = [refs[3 * n : 3 * n + 3] for n in range(chunks)]
    res_ref, mid_ref, first_ref, last_ref = refs[3 * chunks :]
    rows = mid_ref.shape[1]
    edge = None
    inner = res_ref[0]
    for dq_ref, low_ref, w_ref in per_chunk:
        inner = inner + nt(dq_ref[0], w_ref[0])
        for c in range(2):
            term = nt(low_ref[c, 0], w_ref[1 + c])
            edge = term if edge is None else edge + term
    mid_ref[0] = inner + edge[HALF : HALF + rows]
    first_ref[0] = edge[:HALF].astype(BF)
    last_ref[0] = edge[HALF + rows :].astype(BF)


def input_grad(parts, residual):
    seqs, rows, width = residual.shape
    wide, span = parts[0][1].shape[2:]
    in_specs, operands = [], []
    for dq, low, w in parts:
        in_specs += [
            pl.BlockSpec((1, rows, span), lambda s: (s, 0, 0)),
            pl.BlockSpec((2, 1, wide, span), lambda s: (0, s, 0, 0)),
            pl.BlockSpec(
                (3,) + w.shape[1:], lambda s: (0, 0, 0), pipeline_mode=pl.Buffered(1)
            ),
        ]
        operands += [dq, low, w]
    own = pl.BlockSpec((1, rows, width), lambda s: (s, 0, 0))
    edge = pl.BlockSpec((1, HALF, width), lambda s: (s, 0, 0))
    return pl.pallas_call(
        partial(input_grad_kernel, len(parts)),
        grid=(seqs,),
        in_specs=in_specs + [own],
        out_specs=[own, edge, edge],
        out_shape=[
            jax.ShapeDtypeStruct((seqs, rows, width), F32),
            jax.ShapeDtypeStruct((seqs, HALF, width), BF),
            jax.ShapeDtypeStruct((seqs, HALF, width), BF),
        ],
        compiler_params=params(60),
        cost_estimate=cost(6 * len(parts) * seqs * wide * width * span, 16),
    )(*operands, residual)


def after(value, *others):
    return lax.optimization_barrier((value,) + others)[0]


def finish_kernel(terms, chunks, *refs):
    groups = [refs[:terms], refs[terms : 2 * terms]]
    qkv_ref, out_ref, extra_ref, sums_ref = refs[2 * terms :]
    totals = []
    for group in groups:
        total = group[0][...].astype(F32)
        for ref in group[1:]:
            total = total + ref[...].astype(F32)
        totals.append(total)
    rows = out_ref.shape[0]
    sums_ref[...] = totals[0][rows:]
    lane = lax.broadcasted_iota(jnp.int32, (1, PAIR), 1) < HEAD_DIM
    first_count = totals[0].shape[1] // (4 * HEAD_DIM)

    def part(chunk, which, high):
        source = totals[0] if chunk < first_count else totals[1]
        chunk = chunk if chunk < first_count else chunk - first_count
        tile = 2 * chunk + which // 2
        values = source[:, tile * PAIR : (tile + 1) * PAIR]
        return values if which % 2 == high else pltpu.roll(values, HEAD_DIM, 1)

    for which in range(4):
        for chunk in range(0, chunks, 2):
            first = chunk * HEAD_DIM
            if chunk + 1 < chunks:
                made = jnp.where(lane, part(chunk, which, 0), part(chunk + 1, which, 1))
            else:
                made = part(chunk, which, 0)[:, :HEAD_DIM]
            lanes = slice(first, first + made.shape[1])
            if which < 3:
                qkv_ref[which, :, lanes] = made[:rows]
                extra_ref[which, :, lanes] = made[rows:]
            else:
                out_ref[:, lanes] = made[:rows]


def finish(groups, chunks):
    rows = groups[0][0].shape[0] - EXTRA
    local = chunks * HEAD_DIM
    return pl.pallas_call(
        partial(finish_kernel, len(groups[0]), chunks),
        out_shape=[
            jax.ShapeDtypeStruct((3, rows, local), F32),
            jax.ShapeDtypeStruct((rows, local), F32),
            jax.ShapeDtypeStruct((3, EXTRA, local), F32),
            jax.ShapeDtypeStruct((EXTRA, groups[0][0].shape[1]), F32),
        ],
        compiler_params=params(16),
        cost_estimate=cost(1, 1),
    )(*groups[0], *groups[1])


def swap(values, axis, mask):
    count = lax.axis_size(axis)
    return lax.ppermute(values, axis, [(i, i ^ mask) for i in range(count)])


def shift_right(rows):
    count = lax.axis_size("tp")
    return lax.ppermute(rows, "tp", [(i, i + 1) for i in range(count - 1)])


def shift_left(rows):
    count = lax.axis_size("tp")
    return lax.ppermute(rows, "tp", [(i + 1, i) for i in range(count - 1)])


def gather_columns(shard):
    if lax.axis_size("tp") != 4:
        return lax.all_gather(shard, "tp", axis=0, tiled=False)
    me = lax.axis_index("tp")
    found = [shard] + [swap(shard, "tp", mask) for mask in (1, 2, 3)]
    odd, high = me % 2 == 1, me >= 2
    found = [jnp.where(odd, found[n ^ 1], found[n]) for n in range(4)]
    return jnp.stack([jnp.where(high, found[n ^ 2], found[n]) for n in range(4)])


def gather_pieces(shard, beside):
    mine = lax.axis_index("fsdp")
    rows = shard.shape[0]
    half = rows // 2
    across = swap(shard, "fsdp", 2)
    along = swap(shard, "fsdp", 4)
    onward = after(across[:half], *beside)
    corner = [swap(onward, "fsdp", 4), swap(along[half:], "fsdp", 2)]
    own = [shard, across, along] + corner
    other = [swap(piece, "fsdp", 1) for piece in own]
    place = [
        (mine ^ mask) * rows + extra
        for core in (0, 1)
        for mask, extra in ((core, 0), (2 + core, 0), (4 + core, 0), (6 + core, 0), (6 + core, half))
    ]
    return own + other, jnp.stack(place).astype(jnp.int32)


def spread_line(values):
    two = swap(values, "tp", 2)
    return [swap(values, "tp", 1), two, swap(two, "tp", 1)]


def merge_line(own, other, *waits):
    sent = after(other, *waits) if waits else other
    merged = add_low(own, swap(sent, "tp", 1)).astype(BF)
    return [merged[0], swap(merged[1], "tp", 2)]


def add_low(first, *others):
    total = first.astype(F32)
    for other in others:
        total = total + other.astype(F32)
    return total


def merge_cores(keep, send):
    return add_low(keep, swap(send, "fsdp", 1)).astype(BF)


def merge_chips(blocks, *beside):
    own = after(blocks[0], *beside) if beside else blocks[0]
    return add_low(own, *[swap(blocks[n], "fsdp", 2 * n) for n in (1, 2, 3)]).astype(BF)


def scatter_tp(blocks):
    count = lax.axis_size("tp")
    me = lax.axis_index("tp")

    def pick(d):
        return lax.dynamic_index_in_dim(blocks, me ^ d, 0, keepdims=False)

    return [pick(0)] + [swap(pick(d), "tp", d) for d in range(1, count)]


def spread_rows(whole, blocks):
    parts, rows, cols = whole.shape
    rows -= EXTRA
    main = whole[:, :rows].reshape(parts, blocks, rows // blocks, cols).transpose(1, 0, 2, 3)
    more = jnp.broadcast_to(whole[None, :, rows:], (blocks, parts, EXTRA, cols))
    return jnp.concatenate([main, more], axis=2)


def split_three(values):
    high = lax.reduce_precision(values, 8, 7)
    rest = values - high
    middle = lax.reduce_precision(rest, 8, 7)
    return jnp.stack([high, middle, rest - middle]).astype(BF)


def body(
    inputs, segments, w_qkv, qkv_bias, pool_kernel, w_out, out_bias,
    w_up, up_bias, w_down, norm_gains, norm_shifts, cotangent,
):
    rows, seqs, width = inputs.shape
    tp = lax.axis_size("tp")
    fsdp = lax.axis_size("fsdp")
    place = lax.axis_index("tp")
    shard_rows = w_qkv.shape[0]
    local = w_qkv.shape[2]
    chunks = local // HEAD_DIM
    span = tp * HEAD_DIM
    hidden_local = w_up.shape[1]
    hidden_units = hidden_local * tp
    far_rows = rows // STRIDE
    fast = fsdp == 8 and shard_rows % 32 == 0

    bias_values = jnp.concatenate(
        [qkv_bias.reshape(-1), pool_kernel.reshape(-1), up_bias.reshape(-1)]
    )
    biases = split_three(bias_values)
    extra = -(-biases.size // (4 * local))
    packed = jnp.concatenate(
        [
            jnp.concatenate([w_qkv.reshape(shard_rows, 3 * local), w_out], axis=1),
            jnp.pad(biases.reshape(-1), (0, extra * 4 * local - biases.size)).reshape(
                extra, 4 * local
            ),
        ],
        axis=0,
    )
    left = shift_right(inputs[rows - HALF :])
    right = shift_left(inputs[:HALF])
    columns = gather_columns(packed)
    wide_rows = (
        columns[:, :shard_rows]
        .reshape(tp, shard_rows, 4, chunks, HEAD_DIM)
        .transpose(1, 2, 3, 0, 4)
        .reshape(shard_rows, 4 * width)
    )
    whole_bias = jnp.sum(
        columns[:, shard_rows:].reshape(tp, -1)[:, : biases.size].reshape(tp, 3, -1).astype(F32),
        axis=1,
    )
    lead = (3 + 2 * TAPS) * local
    featured = (
        whole_bias[:, :lead]
        .reshape(tp, 3 + 2 * TAPS, chunks, HEAD_DIM)
        .transpose(1, 2, 0, 3)
        .reshape(3 + 2 * TAPS, width)
    )
    bias_qkv = featured[:3, None, :]
    taps = jnp.pad(featured[3:].reshape(2, TAPS, width), ((0, 0), (0, 8 - TAPS), (0, 0)))
    bias_up = whole_bias[:, lead:].reshape(1, hidden_units)

    x_wide = jnp.concatenate([left, inputs, right], axis=0).transpose(1, 0, 2)
    wide = rows + 2 * HALF

    seg_rows = segments.T
    padded = jnp.pad(seg_rows, ((0, 0), (HALF, HALF)), constant_values=-1)
    seg_keys = lax.dynamic_slice_in_dim(padded, place * rows, wide, 1)
    seg_own = seg_keys[:, HALF : HALF + rows]
    centers = seg_rows[:, ::STRIDE].reshape(seqs, tp, far_rows)
    centers_cycle = jnp.concatenate(
        [
            lax.dynamic_index_in_dim(centers, place ^ d, 1, keepdims=True)
            for d in range(tp)
        ],
        axis=1,
    ).reshape(seqs, 1, tp * far_rows)
    segs = (seg_own[:, :, None], seg_keys[:, None, :], centers_cycle)
    own_centers = seg_own[:, ::STRIDE]
    same = jnp.stack(
        [
            seg_keys[:, HALF - MARGIN + r : HALF - MARGIN + r + rows : STRIDE][:, :far_rows]
            == own_centers
            for r in range(TAPS)
        ]
        + [jnp.zeros_like(own_centers, dtype=bool)] * (8 - TAPS),
        axis=2,
    ).astype(F32)

    if fast:
        pieces, offs = gather_pieces(wide_rows, (x_wide, same, bias_qkv, taps) + segs)
    else:
        pieces = [lax.all_gather(wide_rows, "fsdp", axis=0, tiled=True)]
        offs = jnp.zeros((1,), jnp.int32)

    weights = lax.all_gather(
        jnp.concatenate([w_up, w_down], axis=1), "tp", axis=0, tiled=False
    )

    made, slots, att = [], [], []

    def send_pooled(j, *waits):
        pooled = made[j][1]
        sent = after(pooled, *waits) if waits else pooled
        slots.append([pooled] + spread_line(sent))

    for j in range(chunks):
        if j:
            offs = after(offs, made[-1][1], *([slots[0][2]] if j > 1 else []))
        made.append(project(j, chunks, pieces, offs, x_wide, bias_qkv, taps, same, far_rows))
        if j == 0:
            send_pooled(0)
        if j == 1:
            send_pooled(1, slots[0][2])
    weights = after(weights, made[0][1])
    weights = lax.all_gather(weights, "fsdp", axis=0, tiled=False)
    for j in range(chunks):
        order = segs
        if j == 1:
            x_cols = after(x_wide, att[0]).reshape(seqs * wide, width).T
            cot = after(cotangent, att[0]).transpose(1, 0, 2)
        if j:
            order = segs[:2] + (after(segs[2], att[-1], x_cols, cot),)
        att.append(attend_forward(made[j][0], slots[j], order))
        if j + 2 < chunks:
            send_pooled(j + 2, att[j], slots[j + 1][2])
    if shard_rows % 16:
        weights = weights.transpose(1, 0, 2, 3).reshape(1, tp, width, -1)

    misc = jnp.concatenate([out_bias, norm_gains, norm_shifts, jnp.zeros((2, width), F32)])
    outputs, grad_residual, grad_att, grad_out, gud, small = dense(
        att, [m[2] for m in made], x_wide, cot, weights, bias_up, misc
    )
    if gud.shape[0] == 1:
        gud = spread_rows(gud.reshape(2 * tp, -1, hidden_local), fsdp)
        gud = gud.reshape(fsdp, tp, 2, -1, hidden_local)
    gud = lax.psum_scatter(gud, "fsdp", scatter_dimension=0, tiled=False)
    grad_up_down = lax.psum_scatter(gud, "tp", scatter_dimension=0, tiled=False).astype(F32)

    if fast:
        mine = lax.axis_index("fsdp")
        group_sizes = (4, 4)
        out_offs = jnp.stack(
            [(mine ^ m) * shard_rows for m in (0, 2, 4, 6, 1, 3, 5, 7)]
        ).astype(jnp.int32)
    else:
        group_sizes = (1,)
        out_offs = jnp.zeros((1,), jnp.int32)
    backs = []
    for j in range(chunks):
        order = segs
        if j:
            waits = (backs[-1][0],) + (tuple(backs[-2][3][:1]) if j > 1 else ())
            order = segs[:2] + (after(segs[2], *waits),)
        dq, dk, dv, dps = attend_backward(made[j][0], slots[j], order, grad_att[j])
        waits = (backs[-1][3][:1] if j else []) + (backs[-2][3][1:] if j > 1 else [])
        arrived = merge_line(*dps, *waits)
        backs.append((dq, dk, dv, arrived, made[j][0], grad_out[j]))
    totals, lows, merged = [], [], []
    for low, high in ((0, chunks - 1), (chunks - 1, chunks)):
        if low == high:
            continue
        cols = (high - low) * 4 * HEAD_DIM
        more = jnp.zeros((EXTRA, cols), F32)
        if not merged:
            flat = small[:6].reshape(-1)
            lines = -(-flat.size // cols)
            flat = jnp.pad(flat, (0, lines * cols - flat.size)).reshape(lines, cols)
            more = jnp.pad(flat, ((TAPS + 1, EXTRA - TAPS - 1 - lines), (0, 0)))
        waits = [backs[-1][0], backs[-1][3][0]] + ([gud] if merged else [])
        groups, low_kv = gather_back(
            low, after(out_offs, *waits), group_sizes, backs[low:high], taps, same, x_cols, more
        )
        lows += low_kv
        if fast:
            merged.append(merge_cores(*[after(g, *backs[-1][3][1:]) for g in groups]))
        else:
            merged.append(spread_rows(groups[0][0], fsdp))
    middle, first, last = input_grad(
        [(backs[n][0], lows[n], made[n][2]) for n in range(chunks)], grad_residual
    )
    middle = middle.transpose(1, 0, 2)
    chips = []
    for n, blocks in enumerate(merged):
        blocks = after(blocks, *chips) if chips else blocks
        if fast:
            chips.append(merge_chips(blocks, *([] if chips else [middle])))
        else:
            chips.append(lax.psum_scatter(blocks, "fsdp", scatter_dimension=0, tiled=False))
    for blocks in chips:
        if len(totals) + 1 == len(chips):
            blocks = after(blocks, middle)
        else:
            blocks = after(blocks, merged[-1])
        totals.append(scatter_tp(blocks))

    first, last = after(first, chips[-1]), after(last, chips[-1])
    to_left = shift_left(first).transpose(1, 0, 2)
    to_right = shift_right(last).transpose(1, 0, 2)
    grad_inputs = middle.at[:HALF].add(to_right.astype(F32))
    grad_inputs = grad_inputs.at[rows - HALF :].add(to_left.astype(F32))

    grad_w_qkv, grad_w_out, extra_rows, sums = finish(totals, chunks)
    sums = sums[TAPS + 1 :].reshape(-1)[: 6 * width].reshape(6, width)
    return (
        outputs.transpose(1, 0, 2),
        grad_inputs,
        grad_w_qkv.transpose(1, 0, 2),
        extra_rows[:, 0],
        extra_rows[1:, 1 : TAPS + 1],
        grad_w_out,
        sums[0:2],
        grad_up_down[0, :shard_rows],
        grad_up_down[0, shard_rows],
        grad_up_down[1, :shard_rows],
        sums[2:4],
        sums[4:6],
    )


def solution(mesh):
    placed = (
        P("tp", "fsdp", None),
        P(None, "fsdp"),
        P("fsdp", None, "tp"),
        P(None, "tp"),
        P(None, None, "tp"),
        P("fsdp", "tp"),
        P(),
        P("fsdp", "tp"),
        P("tp"),
        P("fsdp", "tp"),
        P(),
        P(),
        P("tp", "fsdp", None),
    )
    return jax.shard_map(
        body,
        mesh=mesh,
        in_specs=placed,
        out_specs=(
            P("tp", "fsdp", None),
            P("tp", "fsdp", None),
            P("fsdp", None, "tp"),
            P(None, "tp"),
            P(None, None, "tp"),
            P("fsdp", "tp"),
            P(),
            P("fsdp", "tp"),
            P("tp"),
            P("fsdp", "tp"),
            P(),
            P(),
        ),
        check_vma=False,
    )
```

```python
from functools import partial

import jax
import jax.numpy as jnp
import numpy as np
from jax import lax
from jax.experimental import pallas as pl
from jax.experimental.pallas import tpu as pltpu
from jax.sharding import PartitionSpec as P

HEAD_DIM = 64
HALF = 64
STRIDE = 4
TAPS = 5
MARGIN = TAPS // 2
PAIR = 2 * HEAD_DIM
QB = 128
SB = 128
NEAR = QB + 2 * HALF
EXTRA = 16
RC = 256
EPSILON = 1e-05
NEG = -1e30
SCALE = HEAD_DIM**-0.5
BF = jnp.bfloat16
F32 = jnp.float32
MIB = 2**20


def nt(a, b):
    return lax.dot_general(a, b, (((1,), (1,)), ((), ())), preferred_element_type=F32)


def nn(a, b):
    return lax.dot_general(a, b, (((1,), (0,)), ((), ())), preferred_element_type=F32)


def tn(a, b):
    return lax.dot_general(a, b, (((0,), (0,)), ((), ())), preferred_element_type=F32)


def params(mib):
    return pltpu.CompilerParams(vmem_limit_bytes=mib * MIB)


def cost(flops, mib, trans=0):
    return pl.CostEstimate(flops=1, bytes_accessed=1, transcendentals=0)


def once(shape):
    zeros = (0,) * len(shape)
    return pl.BlockSpec(shape, lambda *_: zeros, pipeline_mode=pl.Buffered(1))


def project_kernel(count, offs, *refs):
    pieces = refs[:count]
    x_ref, bias_ref, taps_ref, same_ref, out_ref, pooled_ref, w_ref, plain = refs[count:]
    part = pl.program_id(0)
    for n in range(count):
        rows = pieces[n].shape[0]
        w_ref[0, pl.ds(pl.multiple_of(offs[n], 16), rows), :] = pieces[n][...]
    seqs, wide, _ = x_ref.shape
    far_rows = pooled_ref.shape[2]

    @pl.when(part < 3)
    def _():
        for s in range(seqs):
            made = (nn(x_ref[s], w_ref[0]) + bias_ref[0]).astype(BF)
            out_ref[0, s] = made
            for half in range(plain.shape[1]):
                plain[s, half] = made[:, half * PAIR : (half + 1) * PAIR].astype(F32)

    @pl.when((part > 0) & (part < 3))
    def _():
        for s in range(seqs):
            for half in range(plain.shape[1]):
                lanes = slice(half * PAIR, (half + 1) * PAIR)
                total = jnp.zeros((far_rows, PAIR), F32)
                for r in range(TAPS):
                    rows = plain[s, half, pl.ds(HALF - MARGIN + r, far_rows, stride=STRIDE), :]
                    total = total + taps_ref[0, r : r + 1, lanes] * rows * same_ref[
                        s, :, r : r + 1
                    ]
                pooled_ref[0, s, :, lanes] = total.astype(BF)


def project(chunk, chunks, pieces, offs, x_wide, bias, taps, same, far_rows):
    seqs, wide, width = x_wide.shape
    span = width // chunks

    def piece_spec(piece):
        return pl.BlockSpec((piece.shape[0], span), lambda c, o: (0, c * chunks + chunk))

    def three(c):
        return jnp.minimum(c, 2)

    def kv(c):
        return jnp.maximum(three(c) - 1, 0)

    return pl.pallas_call(
        partial(project_kernel, len(pieces)),
        grid_spec=pltpu.PrefetchScalarGridSpec(
            num_scalar_prefetch=1,
            grid=(4,),
            in_specs=[piece_spec(p) for p in pieces]
            + [
                once(x_wide.shape),
                pl.BlockSpec((1, 1, span), lambda c, o: (three(c), 0, chunk)),
                pl.BlockSpec((1, 8, span), lambda c, o: (kv(c), 0, chunk)),
                once(same.shape),
            ],
            out_specs=[
                pl.BlockSpec((1, seqs, wide, span), lambda c, o: (three(c), 0, 0, 0)),
                pl.BlockSpec((1, seqs, far_rows, span), lambda c, o: (kv(c), 0, 0, 0)),
                pl.BlockSpec((1, width, span), lambda c, o: (c, 0, 0)),
            ],
            scratch_shapes=[pltpu.VMEM((seqs, span // PAIR, wide, PAIR), F32)],
        ),
        out_shape=[
            jax.ShapeDtypeStruct((3, seqs, wide, span), BF),
            jax.ShapeDtypeStruct((2, seqs, far_rows, span), BF),
            jax.ShapeDtypeStruct((4, width, span), BF),
        ],
        compiler_params=params(32),
        cost_estimate=cost(6 * seqs * wide * width * span, 8),
    )(offs, *pieces, x_wide, bias, taps, same)


def fill_masks(segq_ref, segk_ref, cen_ref, near_bias, far_bias):
    rows = segq_ref.shape[1]
    shape = (QB, NEAR)
    gap = lax.broadcasted_iota(jnp.int32, shape, 1) - lax.broadcasted_iota(jnp.int32, shape, 0)
    band = (gap >= 0) & (gap <= 2 * HALF)
    for first in range(0, rows, QB):
        own = segq_ref[0, first : first + QB, :]
        keys = segk_ref[0, :, first : first + NEAR]
        near_bias[first : first + QB, :] = jnp.where(band & (own == keys), 0.0, NEG)
        far_bias[first : first + QB, :] = jnp.where(own == cen_ref[0], 0.0, NEG)


def head_mask(head):
    lane = lax.broadcasted_iota(jnp.int32, (1, PAIR), 1)
    return lane < HEAD_DIM if head == 0 else lane >= HEAD_DIM


def fold_lanes(*arrays):
    parts = [a[:, n : n + PAIR] for a in arrays for n in range(0, a.shape[1], PAIR)]
    while len(parts) > 1:
        parts = [sum(parts[n : n + 2]) for n in range(0, len(parts), 2)]
    return parts[0]


def softmax_rows(near, far):
    top = jnp.maximum(
        jnp.max(near, axis=-1, keepdims=True), jnp.max(far, axis=-1, keepdims=True)
    )
    near = jnp.exp(near - top)
    far = jnp.exp(far - top)
    total = jnp.sum(near, axis=-1, keepdims=True) + jnp.sum(far, axis=-1, keepdims=True)
    inverse = 1.0 / total
    return near * inverse, far * inverse


def stack_heads(rows, stacked):
    for first in range(0, rows.shape[0], QB):
        part = rows[first : first + QB]
        for head in range(2):
            stacked[2 * first + head * QB : 2 * first + (head + 1) * QB, :] = jnp.where(
                head_mask(head), part, BF(0)
            )


def join_slots(slots, joined):
    rows = slots[0].shape[1]
    for n, slot in enumerate(slots):
        joined[n * rows : (n + 1) * rows, :] = slot[0]


def attend_forward_kernel(blocks, q_ref, k_ref, v_ref, *refs):
    pk, pv = refs[:blocks], refs[blocks : 2 * blocks]
    segq, segk, cen, out_ref = refs[2 * blocks : 2 * blocks + 4]
    near_bias, far_bias, far_keys, far_values, query, far_scores, far_probs = refs[
        2 * blocks + 4 :
    ]

    @pl.when(pl.program_id(1) == 0)
    def _():
        fill_masks(segq, segk, cen, near_bias, far_bias)

    rows = out_ref.shape[1]
    join_slots(pk, far_keys)
    join_slots(pv, far_values)
    stack_heads(q_ref[0, HALF : HALF + rows, :] * BF(SCALE), query)
    far_scores[...] = nt(query[...], far_keys[...])
    outs = []
    for first in range(0, rows, QB):
        span = slice(first, first + NEAR)
        pair = slice(2 * first, 2 * first + 2 * QB)
        near_all = nt(query[pair, :], k_ref[0, span, :])
        lows = []
        for part in range(0, 2 * QB, SB):
            source = first + part % QB
            near, far = softmax_rows(
                near_all[part : part + SB] + near_bias[source : source + SB, :],
                far_scores[2 * first + part : 2 * first + part + SB, :]
                + far_bias[source : source + SB, :],
            )
            far_probs[2 * first + part : 2 * first + part + SB, :] = far.astype(BF)
            lows.append(near.astype(BF))
        outs.append(nn(jnp.concatenate(lows, axis=0), v_ref[0, span, :]))
    far_out = nn(far_probs[...], far_values[...])
    for n, first in enumerate(range(0, rows, QB)):
        both = outs[n] + far_out[2 * first : 2 * first + 2 * QB]
        out_ref[0, first : first + QB, :] = jnp.where(head_mask(0), both[:QB], both[QB:]).astype(BF)


def attend_backward_kernel(blocks, q_ref, k_ref, v_ref, *refs):
    pk, pv = refs[:blocks], refs[blocks : 2 * blocks]
    segq, segk, cen, grad_ref, dq_ref, dk_ref, dv_ref = refs[2 * blocks : 2 * blocks + 7]
    dp_refs = refs[2 * blocks + 7 : 2 * blocks + 9]
    (
        near_bias, far_bias, far_keys, far_values,
        query, far_scores, far_probs, grad, far_dots, far_grads,
    ) = refs[2 * blocks + 9 :]

    @pl.when(pl.program_id(1) == 0)
    def _():
        fill_masks(segq, segk, cen, near_bias, far_bias)

    rows = dq_ref.shape[1]
    join_slots(pk, far_keys)
    join_slots(pv, far_values)
    stack_heads(q_ref[0, HALF : HALF + rows, :] * BF(SCALE), query)
    stack_heads(grad_ref[0], grad)
    far_scores[...] = nt(query[...], far_keys[...])
    far_dots[...] = nt(grad[...], far_values[...])
    dk_ref[...] = jnp.zeros_like(dk_ref)
    dv_ref[...] = jnp.zeros_like(dv_ref)
    dqs = []
    for first in range(0, rows, QB):
        span = slice(first, first + NEAR)
        pair = slice(2 * first, 2 * first + 2 * QB)
        near_all = nt(query[pair, :], k_ref[0, span, :])
        dots_all = nt(grad[pair, :], v_ref[0, span, :])
        lows, grads = [], []
        for part in range(0, 2 * QB, SB):
            source = first + part % QB
            here = slice(2 * first + part, 2 * first + part + SB)
            near, far = softmax_rows(
                near_all[part : part + SB] + near_bias[source : source + SB, :],
                far_scores[here, :] + far_bias[source : source + SB, :],
            )
            near_dot, far_dot = dots_all[part : part + SB], far_dots[here, :]
            row_dot = jnp.sum(
                fold_lanes(near * near_dot, far * far_dot), axis=-1, keepdims=True
            )
            far_probs[here, :] = far.astype(BF)
            far_grads[here, :] = (far * (far_dot - row_dot)).astype(BF)
            lows.append(near.astype(BF))
            grads.append((near * (near_dot - row_dot)).astype(BF))
        low = jnp.concatenate(lows, axis=0)
        ds = jnp.concatenate(grads, axis=0)
        dqs.append(nn(ds, k_ref[0, span, :]))
        dk_ref[0, span, :] += nn(query[pair, :].T, ds).T
        dv_ref[0, span, :] += nn(grad[pair, :].T, low).T
    far_dq = nn(far_grads[...], far_keys[...])
    for n, first in enumerate(range(0, rows, QB)):
        both = (dqs[n] + far_dq[2 * first : 2 * first + 2 * QB]) * SCALE
        dq_ref[0, first : first + QB, :] = jnp.where(head_mask(0), both[:QB], both[QB:]).astype(BF)
    dpk = nn(query[...].T, far_grads[...]).T.astype(BF)
    dpv = nn(grad[...].T, far_probs[...]).T.astype(BF)
    far_rows = dp_refs[0].shape[3]
    for n in range(blocks):
        span = slice(n * far_rows, (n + 1) * far_rows)
        dp_refs[n % 2][n // 2, 0, 0] = dpk[span]
        dp_refs[n % 2][n // 2, 1, 0] = dpv[span]


def attention_specs(wide, blocks, far_rows):
    def own(part):
        return pl.BlockSpec((None, 1, wide, PAIR), lambda s, h: (part, s, 0, h))

    def pooled(part):
        return pl.BlockSpec((None, 1, far_rows, PAIR), lambda s, h: (part, s, 0, h))

    rows = wide - 2 * HALF
    return (
        [own(0), own(1), own(2)]
        + [pooled(0)] * blocks
        + [pooled(1)] * blocks
        + [
            pl.BlockSpec((1, rows, 1), lambda s, h: (s, 0, 0)),
            pl.BlockSpec((1, 1, wide), lambda s, h: (s, 0, 0)),
            pl.BlockSpec((1, 1, blocks * far_rows), lambda s, h: (s, 0, 0)),
        ]
    )


def attention_scratch(rows, far_all):
    return [
        pltpu.VMEM((rows, NEAR), F32),
        pltpu.VMEM((rows, far_all), F32),
        pltpu.VMEM((far_all, PAIR), BF),
        pltpu.VMEM((far_all, PAIR), BF),
        pltpu.VMEM((2 * rows, PAIR), BF),
        pltpu.VMEM((2 * rows, far_all), F32),
        pltpu.VMEM((2 * rows, far_all), BF),
    ]


def attend_forward(proj, slots, segs):
    _, seqs, wide, span = proj.shape
    blocks, far_rows = len(slots), slots[0].shape[2]
    rows = wide - 2 * HALF
    cells = seqs * rows * (NEAR + blocks * far_rows) * (span // HEAD_DIM)
    return pl.pallas_call(
        partial(attend_forward_kernel, blocks),
        grid=(seqs, span // PAIR),
        in_specs=attention_specs(wide, blocks, far_rows),
        out_specs=pl.BlockSpec((1, rows, PAIR), lambda s, h: (s, 0, h)),
        out_shape=jax.ShapeDtypeStruct((seqs, rows, span), BF),
        scratch_shapes=attention_scratch(rows, blocks * far_rows),
        compiler_params=params(60),
        cost_estimate=cost(16 * 64 * cells, 8, cells),
    )(proj, proj, proj, *slots, *slots, *segs)


def attend_backward(proj, slots, segs, grad):
    _, seqs, wide, span = proj.shape
    blocks, far_rows = len(slots), slots[0].shape[2]
    rows = wide - 2 * HALF
    cells = seqs * rows * (NEAR + blocks * far_rows) * (span // HEAD_DIM)
    own_spec = pl.BlockSpec((1, rows, PAIR), lambda s, h: (s, 0, h))
    wide_spec = pl.BlockSpec((1, wide, PAIR), lambda s, h: (s, 0, h))
    wide_shape = jax.ShapeDtypeStruct((seqs, wide, span), F32)
    far_spec = pl.BlockSpec((blocks // 2, 2, 1, far_rows, PAIR), lambda s, h: (0, 0, s, 0, h))
    far_shape = jax.ShapeDtypeStruct((blocks // 2, 2, seqs, far_rows, span), BF)
    out = pl.pallas_call(
        partial(attend_backward_kernel, blocks),
        grid=(seqs, span // PAIR),
        in_specs=attention_specs(wide, blocks, far_rows) + [own_spec],
        out_specs=[own_spec, wide_spec, wide_spec] + [far_spec] * 2,
        out_shape=[jax.ShapeDtypeStruct((seqs, rows, span), BF), wide_shape, wide_shape]
        + [far_shape] * 2,
        scratch_shapes=attention_scratch(rows, blocks * far_rows)
        + [
            pltpu.VMEM((2 * rows, PAIR), BF),
            pltpu.VMEM((2 * rows, blocks * far_rows), F32),
            pltpu.VMEM((2 * rows, blocks * far_rows), BF),
        ],
        compiler_params=params(60),
        cost_estimate=cost(40 * 64 * cells, 16, cells),
    )(proj, proj, proj, *slots, *slots, *segs, grad)
    return out[0], out[1], out[2], out[3:]


def norm_stats(residual):
    row_mean = jnp.mean(residual, axis=-1, keepdims=True)
    centered = residual - row_mean
    variance = jnp.mean(centered * centered, axis=-1, keepdims=True)
    inverse = lax.rsqrt(variance + EPSILON)
    return centered * inverse, inverse


def norm_back(grad, normed, inverse, gain):
    scaled = grad * gain
    first = jnp.mean(scaled, axis=-1, keepdims=True)
    second = jnp.mean(scaled * normed, axis=-1, keepdims=True)
    return (scaled - first - normed * second) * inverse


def column_sum(values):
    return jnp.sum(values.astype(F32), axis=0, keepdims=True)


def dense_kernel(chunks, steps, *refs):
    att, wout = refs[:chunks], refs[chunks : 2 * chunks]
    x_ref, cot_ref, up_blk, down_blk, bup_ref, misc_ref = refs[2 * chunks : 2 * chunks + 6]
    outs = refs[2 * chunks + 6 :]
    out_ref, gres_ref = outs[:2]
    gatt = outs[2 : 2 + chunks]
    gout = outs[2 + chunks : 2 + 2 * chunks]
    gud_ref, small_ref = outs[2 + 2 * chunks : 4 + 2 * chunks]
    (
        inverse, flow, flow_t, acc, gffn, gffn_t, hidden, slope, gpre
    ) = outs[4 + 2 * chunks :]
    step = pl.program_id(0)
    seqs, rows, width = cot_ref.shape
    total = seqs * rows
    span = width // chunks
    units = gpre.shape[1]
    up_ref = up_blk[...].reshape(width, units)
    down_ref = down_blk[...].reshape(width, units)
    bias_one, bias_two = misc_ref[0:1, :], misc_ref[1:2, :]
    gain_one, gain_two = misc_ref[2:3, :], misc_ref[3:4, :]
    shift_one, shift_two = misc_ref[4:5, :], misc_ref[5:6, :]
    parts = [(first, first // rows, first % rows) for first in range(0, total, RC)]

    @pl.when(step == 0)
    def _():
        for first, s, row in parts:
            block = slice(first, first + RC)
            branch = bias_one
            for j in range(chunks):
                branch = branch + nt(
                    att[j][s, row : row + RC, :], wout[j][0]
                )
            n_one, inv = norm_stats(
                x_ref[s, HALF + row : HALF + row + RC, :].astype(F32) + branch
            )
            gres_ref[s, row : row + RC, :] = n_one
            inverse[block, :] = inv
            low = (n_one * gain_one + shift_one).astype(BF)
            flow[block, :] = low
            flow_t[:, block] = low.T
            acc[block, :] = jnp.zeros((RC, width), F32)

    @pl.when(step < steps)
    def _():
        for first, s, row in parts:
            block = slice(first, first + RC)
            pre = nn(flow[block, :], up_ref) + bup_ref[...]
            cdf = 0.5 * (1.0 + lax.erf(pre * np.float32(np.sqrt(0.5))))
            pdf = jnp.exp(-0.5 * (pre * pre)) * np.float32(1.0 / np.sqrt(2.0 * np.pi))
            low = (pre * cdf).astype(BF)
            hidden[step, block, :] = low
            slope[step, block, :] = cdf + pre * pdf
            acc[block, :] += nt(low, down_ref)

    @pl.when(step == steps)
    def _():
        small_ref[...] = jnp.zeros_like(small_ref)
        for first, s, row in parts:
            block = slice(first, first + RC)
            first_out = gres_ref[s, row : row + RC, :] * gain_one + shift_one
            n_two, inv = norm_stats(first_out + (acc[block, :] + bias_two))
            out_ref[s, row : row + RC, :] = (n_two * gain_two + shift_two).astype(BF)
            grad = cot_ref[s, row : row + RC, :].astype(F32)
            second = norm_back(grad, n_two, inv, gain_two)
            acc[block, :] = second
            low = second.astype(BF)
            gffn[block, :] = low
            gffn_t[:, block] = low.T
            small_ref[1:2, :] += column_sum(low)
            small_ref[3:4, :] += column_sum(grad * n_two)
            small_ref[5:6, :] += column_sum(grad)

    @pl.when(step >= steps)
    def _():
        which = 2 * steps - 1 - step
        bias_sum = jnp.zeros((1, units), F32)
        for first, s, row in parts:
            block = slice(first, first + RC)
            grad = nn(gffn[block, :], down_ref)
            low = (grad * slope[which, block, :]).astype(BF)
            gpre[block, :] = low
            bias_sum = bias_sum + column_sum(low)
            acc[block, :] += nt(low, up_ref)
        height = gud_ref.shape[3] - EXTRA
        lead = (gud_ref.shape[0], height, units)
        gud_ref[:, 0, 0, :height] = nn(flow_t[...], gpre[...]).astype(BF).reshape(lead)
        gud_ref[:, 0, 1, :height] = nn(gffn_t[...], hidden[which]).astype(BF).reshape(lead)
        head = lax.broadcasted_iota(jnp.int32, (EXTRA, 1), 0) == 0
        extra = jnp.where(head, bias_sum, 0.0).astype(BF)
        for m in range(gud_ref.shape[0]):
            gud_ref[m, 0, 0, height:] = extra
            gud_ref[m, 0, 1, height:] = jnp.zeros((EXTRA, units), BF)

    @pl.when(step == 2 * steps - 1)
    def _():
        for first, s, row in parts:
            block = slice(first, first + RC)
            grad = acc[block, :]
            n_one = gres_ref[s, row : row + RC, :]
            back = norm_back(grad, n_one, inverse[block, :], gain_one)
            gres_ref[s, row : row + RC, :] = back
            low = back.astype(BF)
            flow_t[:, block] = low.T
            small_ref[0:1, :] += column_sum(low)
            small_ref[2:3, :] += column_sum(grad * n_one)
            small_ref[4:5, :] += column_sum(grad)
            for j in range(chunks):
                gatt[j][s, row : row + RC, :] = nn(
                    low, wout[j][0]
                ).astype(BF)
        for j in range(chunks):
            gout[j][...] = nn(flow_t[...], att[j][...].reshape(total, span)).astype(BF)


def dense(att, projected_weights, x_wide, cot, weights, bias_up, misc):
    chunks = len(att)
    seqs, rows, width = cot.shape
    total = seqs * rows
    span = width // chunks
    row_blocks, steps, height, units = weights.shape
    units //= 2

    def which(i):
        return jnp.where(i < steps, i, 2 * steps - 1 - i)

    def back(i):
        return jnp.where(i < steps, steps - 1, 2 * steps - 1 - i)

    out_shape = (
        [
            jax.ShapeDtypeStruct((seqs, rows, width), BF),
            jax.ShapeDtypeStruct((seqs, rows, width), F32),
        ]
        + [jax.ShapeDtypeStruct((seqs, rows, span), BF)] * chunks
        + [jax.ShapeDtypeStruct((width, span), BF)] * chunks
        + [
            jax.ShapeDtypeStruct((row_blocks, steps, 2, height + EXTRA, units), BF),
            jax.ShapeDtypeStruct((8, width), F32),
        ]
    )
    out_specs = [once(o.shape) for o in out_shape[: 2 + 2 * chunks]] + [
        pl.BlockSpec(
            (row_blocks, 1, 2, height + EXTRA, units), lambda i: (0, back(i), 0, 0, 0)
        ),
        once((8, width)),
    ]
    out = pl.pallas_call(
        partial(dense_kernel, chunks, steps),
        grid=(2 * steps,),
        in_specs=[once(a.shape) for a in att]
        + [
            pl.BlockSpec(
                (1, width, span), lambda i: (3, 0, 0), pipeline_mode=pl.Buffered(1)
            )
        ]
        * chunks
        + [
            once(x_wide.shape),
            once(cot.shape),
            pl.BlockSpec((row_blocks, None, height, units), lambda i: (0, which(i), 0, 0)),
            pl.BlockSpec((row_blocks, None, height, units), lambda i: (0, which(i), 0, 1)),
            pl.BlockSpec((1, units), lambda i: (0, which(i))),
            once(misc.shape),
        ],
        out_specs=out_specs,
        out_shape=out_shape,
        scratch_shapes=[
            pltpu.VMEM((total, 1), F32),
            pltpu.VMEM((total, width), BF),
            pltpu.VMEM((width, total), BF),
            pltpu.VMEM((total, width), F32),
            pltpu.VMEM((total, width), BF),
            pltpu.VMEM((width, total), BF),
            pltpu.VMEM((steps, total, units), BF),
            pltpu.VMEM((steps, total, units), F32),
            pltpu.VMEM((total, units), BF),
        ],
        compiler_params=params(63),
        cost_estimate=cost(1, 1),
    )(*att, *projected_weights, x_wide, cot, weights, weights, bias_up, misc)
    return (
        out[0], out[1], out[2 : 2 + chunks], out[2 + chunks : 2 + 2 * chunks], out[-2], out[-1]
    )


def gather_back_kernel(blocks, chunks, groups, offs, *refs):
    taken = 5 + blocks + 1
    per_chunk = [refs[n * taken : (n + 1) * taken] for n in range(chunks)]
    taps_ref, same_ref, xt_ref, more_ref = refs[chunks * taken : chunks * taken + 4]
    outs = refs[chunks * taken + 4 :]
    gws = outs[:groups]
    lows = outs[groups : groups + chunks]
    small, plain, spread, low_q, total, stage = outs[groups + chunks :]
    width = xt_ref.shape[0]
    seq = pl.program_id(0)
    wide, span = per_chunk[0][0].shape[1:]
    rows = wide - 2 * HALF
    far_rows = per_chunk[0][3].shape[2]

    @pl.when(seq == 0)
    def _():
        small[...] = jnp.zeros_like(small)
        total[...] = jnp.zeros_like(total)

    for n, chunk_refs in enumerate(per_chunk):
        dk_ref, dv_ref, dq_ref = chunk_refs[:3]
        dps = chunk_refs[3 : 3 + blocks]
        proj_k, proj_v = chunk_refs[3 + blocks : 5 + blocks]
        low = lows[n]
        base = n * span
        low_q[:HALF, :] = jnp.zeros((HALF, span), BF)
        low_q[HALF : HALF + rows, :] = dq_ref[0]
        low_q[HALF + rows :, :] = jnp.zeros((HALF, span), BF)
        small[0, 0:1, base : base + span] += column_sum(dq_ref[0])
        for c, (near, proj) in enumerate(((dk_ref, proj_k), (dv_ref, proj_v))):
            for half in range(span // PAIR):
                lanes = slice(half * PAIR, (half + 1) * PAIR)
                wider = slice(base + half * PAIR, base + (half + 1) * PAIR)
                plain[...] = proj[0, 0, :, lanes].astype(F32)
                spread[...] = near[0, :, lanes]
                pooled = dps[0][c, 0, :, lanes].astype(F32)
                for d in range(1, blocks):
                    pooled = pooled + dps[d][c, 0, :, lanes].astype(F32)
                pooled = pooled.astype(BF).astype(F32)
                for r in range(TAPS):
                    place = pl.ds(HALF - MARGIN + r, far_rows, stride=STRIDE)
                    masked = pooled * same_ref[0, :, r : r + 1]
                    small[1 + c, 1 + r : 2 + r, wider] += column_sum(masked * plain[place, :])
                    spread[place, :] = spread[place, :] + taps_ref[c, r : r + 1, wider] * masked
                made = spread[...].astype(BF)
                low[c, 0, :, lanes] = made
                small[1 + c, 0:1, wider] += column_sum(made)
        total[n, 0] += nn(xt_ref[...], low_q[...])
        total[n, 1] += nn(xt_ref[...], low[0, 0])
        total[n, 2] += nn(xt_ref[...], low[1, 0])

    @pl.when(seq == pl.num_programs(0) - 1)
    def _():
        heads = span // HEAD_DIM
        lane = lax.broadcasted_iota(jnp.int32, (1, PAIR), 1) < HEAD_DIM

        def place_four(four, n, u, where):
            turned = [pltpu.roll(value, HEAD_DIM, 1) for value in four]
            for pair in range(2):
                one, two = 2 * pair, 2 * pair + 1
                first = (2 * n + pair) * PAIR
                lanes = slice(first, first + PAIR)
                stage[2 * u, where, lanes] = jnp.where(lane, four[one], turned[two]).astype(BF)
                stage[2 * u + 1, where, lanes] = jnp.where(lane, turned[one], four[two]).astype(BF)

        for n, chunk_refs in enumerate(per_chunk):
            gout_ref = chunk_refs[5 + blocks]
            for u in range(heads // 2):
                lanes = slice(u * PAIR, (u + 1) * PAIR)
                wider = slice(n * span + u * PAIR, n * span + (u + 1) * PAIR)
                four = [total[n, part, :, lanes] for part in range(3)]
                four.append(gout_ref[:, lanes].astype(F32))
                place_four(four, n, u, slice(0, width))
                place_four(
                    [small[part, :, wider] for part in range(4)], n, u, slice(width, width + EXTRA)
                )
        last = slice(width, width + EXTRA)
        head = lax.broadcasted_iota(jnp.int32, (EXTRA, 1), 0) <= TAPS
        for t in range(heads):
            stage[t, last, :] = jnp.where(
                head, stage[t, last, :].astype(F32), more_ref[...]
            ).astype(BF)
        height = gws[0].shape[2] - EXTRA
        number = 0
        for group in gws:
            for m in range(group.shape[0]):
                place = pl.ds(pl.multiple_of(offs[number], 16), height)
                group[m, :, :height] = stage[:, place, :]
                group[m, :, height:] = stage[:, last, :]
                number += 1


def gather_back(first_chunk, offs, group_sizes, parts, taps, same, xt, more):
    chunks = len(parts)
    seqs, wide, span = parts[0][1].shape
    width = xt.shape[0]
    rows = wide - 2 * HALF
    blocks, far_rows = len(parts[0][3]), parts[0][3][0].shape[2]
    height = width // sum(group_sizes)
    heads = span // HEAD_DIM
    in_specs, operands = [], []
    for dq, dk, dv, dps, proj, gout in parts:
        in_specs += [pl.BlockSpec((1, wide, span), lambda s, o: (s, 0, 0))] * 2
        in_specs += [pl.BlockSpec((1, rows, span), lambda s, o: (s, 0, 0))]
        in_specs += [pl.BlockSpec((2, 1, far_rows, span), lambda s, o: (0, s, 0, 0))] * blocks
        in_specs += [
            pl.BlockSpec((1, 1, wide, span), lambda s, o: (1, s, 0, 0)),
            pl.BlockSpec((1, 1, wide, span), lambda s, o: (2, s, 0, 0)),
            once(gout.shape),
        ]
        operands += [dk, dv, dq, *dps, proj, proj, gout]
    out = pl.pallas_call(
        partial(gather_back_kernel, blocks, chunks, len(group_sizes)),
        grid_spec=pltpu.PrefetchScalarGridSpec(
            num_scalar_prefetch=1,
            grid=(seqs,),
            in_specs=in_specs
            + [
                once((2, 8, span * chunks)),
                pl.BlockSpec((1, far_rows, 8), lambda s, o: (s, 0, 0)),
                pl.BlockSpec((width, wide), lambda s, o: (0, s)),
                once(more.shape),
            ],
            out_specs=[
                once((size, heads, height + EXTRA, 4 * HEAD_DIM * chunks)) for size in group_sizes
            ]
            + [pl.BlockSpec((2, 1, wide, span), lambda s, o: (0, s, 0, 0))] * chunks,
            scratch_shapes=[
                pltpu.VMEM((4, EXTRA, span * chunks), F32),
                pltpu.VMEM((wide, PAIR), F32),
                pltpu.VMEM((wide, PAIR), F32),
                pltpu.VMEM((wide, span), BF),
                pltpu.VMEM((chunks, 3, width, span), F32),
                pltpu.VMEM((heads, width + EXTRA, 4 * HEAD_DIM * chunks), BF),
            ],
        ),
        out_shape=[
            jax.ShapeDtypeStruct((size, heads, height + EXTRA, 4 * HEAD_DIM * chunks), BF)
            for size in group_sizes
        ]
        + [jax.ShapeDtypeStruct((2, seqs, wide, span), BF)] * chunks,
        compiler_params=params(60),
        cost_estimate=cost(6 * chunks * seqs * wide * width * span, 12 * chunks),
    )(offs, *operands, taps[:, :, first_chunk * span : (first_chunk + chunks) * span], same, xt, more)
    return out[: len(group_sizes)], out[len(group_sizes) :]


def input_grad_kernel(chunks, *refs):
    per_chunk = [refs[3 * n : 3 * n + 3] for n in range(chunks)]
    res_ref, mid_ref, first_ref, last_ref = refs[3 * chunks :]
    rows = mid_ref.shape[1]
    edge = None
    inner = res_ref[0]
    for dq_ref, low_ref, w_ref in per_chunk:
        inner = inner + nt(dq_ref[0], w_ref[0])
        for c in range(2):
            term = nt(low_ref[c, 0], w_ref[1 + c])
            edge = term if edge is None else edge + term
    mid_ref[0] = inner + edge[HALF : HALF + rows]
    first_ref[0] = edge[:HALF].astype(BF)
    last_ref[0] = edge[HALF + rows :].astype(BF)


def input_grad(parts, residual):
    seqs, rows, width = residual.shape
    wide, span = parts[0][1].shape[2:]
    in_specs, operands = [], []
    for dq, low, w in parts:
        in_specs += [
            pl.BlockSpec((1, rows, span), lambda s: (s, 0, 0)),
            pl.BlockSpec((2, 1, wide, span), lambda s: (0, s, 0, 0)),
            pl.BlockSpec(
                (3,) + w.shape[1:], lambda s: (0, 0, 0), pipeline_mode=pl.Buffered(1)
            ),
        ]
        operands += [dq, low, w]
    own = pl.BlockSpec((1, rows, width), lambda s: (s, 0, 0))
    edge = pl.BlockSpec((1, HALF, width), lambda s: (s, 0, 0))
    return pl.pallas_call(
        partial(input_grad_kernel, len(parts)),
        grid=(seqs,),
        in_specs=in_specs + [own],
        out_specs=[own, edge, edge],
        out_shape=[
            jax.ShapeDtypeStruct((seqs, rows, width), F32),
            jax.ShapeDtypeStruct((seqs, HALF, width), BF),
            jax.ShapeDtypeStruct((seqs, HALF, width), BF),
        ],
        compiler_params=params(60),
        cost_estimate=cost(6 * len(parts) * seqs * wide * width * span, 16),
    )(*operands, residual)


def after(value, *others):
    return lax.optimization_barrier((value,) + others)[0]


def finish_kernel(terms, chunks, *refs):
    groups = [refs[:terms], refs[terms : 2 * terms]]
    qkv_ref, out_ref, extra_ref, sums_ref = refs[2 * terms :]
    totals = []
    for group in groups:
        total = group[0][...].astype(F32)
        for ref in group[1:]:
            total = total + ref[...].astype(F32)
        totals.append(total)
    rows = out_ref.shape[0]
    sums_ref[...] = totals[0][rows:]
    lane = lax.broadcasted_iota(jnp.int32, (1, PAIR), 1) < HEAD_DIM
    first_count = totals[0].shape[1] // (4 * HEAD_DIM)

    def part(chunk, which, high):
        source = totals[0] if chunk < first_count else totals[1]
        chunk = chunk if chunk < first_count else chunk - first_count
        tile = 2 * chunk + which // 2
        values = source[:, tile * PAIR : (tile + 1) * PAIR]
        return values if which % 2 == high else pltpu.roll(values, HEAD_DIM, 1)

    for which in range(4):
        for chunk in range(0, chunks, 2):
            first = chunk * HEAD_DIM
            if chunk + 1 < chunks:
                made = jnp.where(lane, part(chunk, which, 0), part(chunk + 1, which, 1))
            else:
                made = part(chunk, which, 0)[:, :HEAD_DIM]
            lanes = slice(first, first + made.shape[1])
            if which < 3:
                qkv_ref[which, :, lanes] = made[:rows]
                extra_ref[which, :, lanes] = made[rows:]
            else:
                out_ref[:, lanes] = made[:rows]


def finish(groups, chunks):
    rows = groups[0][0].shape[0] - EXTRA
    local = chunks * HEAD_DIM
    return pl.pallas_call(
        partial(finish_kernel, len(groups[0]), chunks),
        out_shape=[
            jax.ShapeDtypeStruct((3, rows, local), F32),
            jax.ShapeDtypeStruct((rows, local), F32),
            jax.ShapeDtypeStruct((3, EXTRA, local), F32),
            jax.ShapeDtypeStruct((EXTRA, groups[0][0].shape[1]), F32),
        ],
        compiler_params=params(16),
        cost_estimate=cost(1, 1),
    )(*groups[0], *groups[1])


def swap(values, axis, mask):
    count = lax.axis_size(axis)
    return lax.ppermute(values, axis, [(i, i ^ mask) for i in range(count)])


def shift_right(rows):
    count = lax.axis_size("tp")
    return lax.ppermute(rows, "tp", [(i, i + 1) for i in range(count - 1)])


def shift_left(rows):
    count = lax.axis_size("tp")
    return lax.ppermute(rows, "tp", [(i + 1, i) for i in range(count - 1)])


def gather_columns(shard):
    if lax.axis_size("tp") != 4:
        return lax.all_gather(shard, "tp", axis=0, tiled=False)
    me = lax.axis_index("tp")
    found = [shard] + [swap(shard, "tp", mask) for mask in (1, 2, 3)]
    odd, high = me % 2 == 1, me >= 2
    found = [jnp.where(odd, found[n ^ 1], found[n]) for n in range(4)]
    return jnp.stack([jnp.where(high, found[n ^ 2], found[n]) for n in range(4)])


def gather_pieces(shard, beside):
    mine = lax.axis_index("fsdp")
    rows = shard.shape[0]
    half = rows // 2
    across = swap(shard, "fsdp", 2)
    along = swap(shard, "fsdp", 4)
    onward = after(across[:half], *beside)
    corner = [swap(onward, "fsdp", 4), swap(along[half:], "fsdp", 2)]
    own = [shard, across, along] + corner
    other = [swap(piece, "fsdp", 1) for piece in own]
    place = [
        (mine ^ mask) * rows + extra
        for core in (0, 1)
        for mask, extra in ((core, 0), (2 + core, 0), (4 + core, 0), (6 + core, 0), (6 + core, half))
    ]
    return own + other, jnp.stack(place).astype(jnp.int32)


def spread_line(values):
    two = swap(values, "tp", 2)
    return [swap(values, "tp", 1), two, swap(two, "tp", 1)]


def merge_line(own, other, *waits):
    sent = after(other, *waits) if waits else other
    merged = add_low(own, swap(sent, "tp", 1)).astype(BF)
    return [merged[0], swap(merged[1], "tp", 2)]


def add_low(first, *others):
    total = first.astype(F32)
    for other in others:
        total = total + other.astype(F32)
    return total


def merge_cores(keep, send):
    return add_low(keep, swap(send, "fsdp", 1)).astype(BF)


def merge_chips(blocks, *beside):
    own = after(blocks[0], *beside) if beside else blocks[0]
    return add_low(own, *[swap(blocks[n], "fsdp", 2 * n) for n in (1, 2, 3)]).astype(BF)


def scatter_tp(blocks):
    count = lax.axis_size("tp")
    me = lax.axis_index("tp")

    def pick(d):
        return lax.dynamic_index_in_dim(blocks, me ^ d, 0, keepdims=False)

    return [pick(0)] + [swap(pick(d), "tp", d) for d in range(1, count)]


def spread_rows(whole, blocks):
    parts, rows, cols = whole.shape
    rows -= EXTRA
    main = whole[:, :rows].reshape(parts, blocks, rows // blocks, cols).transpose(1, 0, 2, 3)
    more = jnp.broadcast_to(whole[None, :, rows:], (blocks, parts, EXTRA, cols))
    return jnp.concatenate([main, more], axis=2)


def split_three(values):
    high = lax.reduce_precision(values, 8, 7)
    rest = values - high
    middle = lax.reduce_precision(rest, 8, 7)
    return jnp.stack([high, middle, rest - middle]).astype(BF)


def body(
    inputs, segments, w_qkv, qkv_bias, pool_kernel, w_out, out_bias,
    w_up, up_bias, w_down, norm_gains, norm_shifts, cotangent,
):
    rows, seqs, width = inputs.shape
    tp = lax.axis_size("tp")
    fsdp = lax.axis_size("fsdp")
    place = lax.axis_index("tp")
    shard_rows = w_qkv.shape[0]
    local = w_qkv.shape[2]
    chunks = local // HEAD_DIM
    span = tp * HEAD_DIM
    hidden_local = w_up.shape[1]
    hidden_units = hidden_local * tp
    far_rows = rows // STRIDE
    fast = fsdp == 8 and shard_rows % 32 == 0

    bias_values = jnp.concatenate(
        [qkv_bias.reshape(-1), pool_kernel.reshape(-1), up_bias.reshape(-1)]
    )
    biases = split_three(bias_values)
    extra = -(-biases.size // (4 * local))
    packed = jnp.concatenate(
        [
            jnp.concatenate([w_qkv.reshape(shard_rows, 3 * local), w_out], axis=1),
            jnp.pad(biases.reshape(-1), (0, extra * 4 * local - biases.size)).reshape(
                extra, 4 * local
            ),
        ],
        axis=0,
    )
    left = shift_right(inputs[rows - HALF :])
    right = shift_left(inputs[:HALF])
    columns = gather_columns(packed)
    wide_rows = (
        columns[:, :shard_rows]
        .reshape(tp, shard_rows, 4, chunks, HEAD_DIM)
        .transpose(1, 2, 3, 0, 4)
        .reshape(shard_rows, 4 * width)
    )
    whole_bias = jnp.sum(
        columns[:, shard_rows:].reshape(tp, -1)[:, : biases.size].reshape(tp, 3, -1).astype(F32),
        axis=1,
    )
    lead = (3 + 2 * TAPS) * local
    featured = (
        whole_bias[:, :lead]
        .reshape(tp, 3 + 2 * TAPS, chunks, HEAD_DIM)
        .transpose(1, 2, 0, 3)
        .reshape(3 + 2 * TAPS, width)
    )
    bias_qkv = featured[:3, None, :]
    taps = jnp.pad(featured[3:].reshape(2, TAPS, width), ((0, 0), (0, 8 - TAPS), (0, 0)))
    bias_up = whole_bias[:, lead:].reshape(1, hidden_units)

    x_wide = jnp.concatenate([left, inputs, right], axis=0).transpose(1, 0, 2)
    wide = rows + 2 * HALF

    seg_rows = segments.T
    padded = jnp.pad(seg_rows, ((0, 0), (HALF, HALF)), constant_values=-1)
    seg_keys = lax.dynamic_slice_in_dim(padded, place * rows, wide, 1)
    seg_own = seg_keys[:, HALF : HALF + rows]
    centers = seg_rows[:, ::STRIDE].reshape(seqs, tp, far_rows)
    centers_cycle = jnp.concatenate(
        [
            lax.dynamic_index_in_dim(centers, place ^ d, 1, keepdims=True)
            for d in range(tp)
        ],
        axis=1,
    ).reshape(seqs, 1, tp * far_rows)
    segs = (seg_own[:, :, None], seg_keys[:, None, :], centers_cycle)
    own_centers = seg_own[:, ::STRIDE]
    same = jnp.stack(
        [
            seg_keys[:, HALF - MARGIN + r : HALF - MARGIN + r + rows : STRIDE][:, :far_rows]
            == own_centers
            for r in range(TAPS)
        ]
        + [jnp.zeros_like(own_centers, dtype=bool)] * (8 - TAPS),
        axis=2,
    ).astype(F32)

    if fast:
        pieces, offs = gather_pieces(wide_rows, (x_wide, same, bias_qkv, taps) + segs)
    else:
        pieces = [lax.all_gather(wide_rows, "fsdp", axis=0, tiled=True)]
        offs = jnp.zeros((1,), jnp.int32)

    weights = lax.all_gather(
        jnp.concatenate([w_up, w_down], axis=1), "tp", axis=0, tiled=False
    )

    made, slots, att = [], [], []

    def send_pooled(j, *waits):
        pooled = made[j][1]
        sent = after(pooled, *waits) if waits else pooled
        slots.append([pooled] + spread_line(sent))

    for j in range(chunks):
        if j:
            offs = after(offs, made[-1][1], *([slots[0][2]] if j > 1 else []))
        made.append(project(j, chunks, pieces, offs, x_wide, bias_qkv, taps, same, far_rows))
        if j == 0:
            send_pooled(0)
        if j == 1:
            send_pooled(1, slots[0][2])
    weights = after(weights, made[0][1])
    weights = lax.all_gather(weights, "fsdp", axis=0, tiled=False)
    for j in range(chunks):
        order = segs
        if j == 1:
            x_cols = after(x_wide, att[0]).reshape(seqs * wide, width).T
            cot = after(cotangent, att[0]).transpose(1, 0, 2)
        if j:
            order = segs[:2] + (after(segs[2], att[-1], x_cols, cot),)
        att.append(attend_forward(made[j][0], slots[j], order))
        if j + 2 < chunks:
            send_pooled(j + 2, att[j], slots[j + 1][2])
    if shard_rows % 16:
        weights = weights.transpose(1, 0, 2, 3).reshape(1, tp, width, -1)

    misc = jnp.concatenate([out_bias, norm_gains, norm_shifts, jnp.zeros((2, width), F32)])
    outputs, grad_residual, grad_att, grad_out, gud, small = dense(
        att, [m[2] for m in made], x_wide, cot, weights, bias_up, misc
    )
    if gud.shape[0] == 1:
        gud = spread_rows(gud.reshape(2 * tp, -1, hidden_local), fsdp)
        gud = gud.reshape(fsdp, tp, 2, -1, hidden_local)
    gud = lax.psum_scatter(gud, "fsdp", scatter_dimension=0, tiled=False)
    grad_up_down = lax.psum_scatter(gud, "tp", scatter_dimension=0, tiled=False).astype(F32)

    if fast:
        mine = lax.axis_index("fsdp")
        group_sizes = (4, 4)
        out_offs = jnp.stack(
            [(mine ^ m) * shard_rows for m in (0, 2, 4, 6, 1, 3, 5, 7)]
        ).astype(jnp.int32)
    else:
        group_sizes = (1,)
        out_offs = jnp.zeros((1,), jnp.int32)
    backs = []
    for j in range(chunks):
        order = segs
        if j:
            waits = (backs[-1][0],) + (tuple(backs[-2][3][:1]) if j > 1 else ())
            order = segs[:2] + (after(segs[2], *waits),)
        dq, dk, dv, dps = attend_backward(made[j][0], slots[j], order, grad_att[j])
        waits = (backs[-1][3][:1] if j else []) + (backs[-2][3][1:] if j > 1 else [])
        arrived = merge_line(*dps, *waits)
        backs.append((dq, dk, dv, arrived, made[j][0], grad_out[j]))
    totals, lows, merged = [], [], []
    for low, high in ((0, chunks - 1), (chunks - 1, chunks)):
        if low == high:
            continue
        cols = (high - low) * 4 * HEAD_DIM
        more = jnp.zeros((EXTRA, cols), F32)
        if not merged:
            flat = small[:6].reshape(-1)
            lines = -(-flat.size // cols)
            flat = jnp.pad(flat, (0, lines * cols - flat.size)).reshape(lines, cols)
            more = jnp.pad(flat, ((TAPS + 1, EXTRA - TAPS - 1 - lines), (0, 0)))
        waits = [backs[-1][0], backs[-1][3][0]] + ([gud] if merged else [])
        groups, low_kv = gather_back(
            low, after(out_offs, *waits), group_sizes, backs[low:high], taps, same, x_cols, more
        )
        lows += low_kv
        if fast:
            merged.append(merge_cores(*[after(g, *backs[-1][3][1:]) for g in groups]))
        else:
            merged.append(spread_rows(groups[0][0], fsdp))
    middle, first, last = input_grad(
        [(backs[n][0], lows[n], made[n][2]) for n in range(chunks)], grad_residual
    )
    middle = middle.transpose(1, 0, 2)
    chips = []
    for n, blocks in enumerate(merged):
        blocks = after(blocks, *chips) if chips else blocks
        if fast:
            chips.append(merge_chips(blocks, *([] if chips else [middle])))
        else:
            chips.append(lax.psum_scatter(blocks, "fsdp", scatter_dimension=0, tiled=False))
    for blocks in chips:
        if len(totals) + 1 == len(chips):
            blocks = after(blocks, middle)
        else:
            blocks = after(blocks, merged[-1])
        totals.append(scatter_tp(blocks))

    first, last = after(first, chips[0]), after(last, chips[0])
    to_left = shift_left(first).transpose(1, 0, 2)
    to_right = shift_right(last).transpose(1, 0, 2)
    grad_inputs = middle.at[:HALF].add(to_right.astype(F32))
    grad_inputs = grad_inputs.at[rows - HALF :].add(to_left.astype(F32))

    out_rows = outputs.transpose(1, 0, 2)
    grad_up, grad_down = grad_up_down[0, :shard_rows], grad_up_down[1, :shard_rows]
    grad_up_bias = grad_up_down[0, shard_rows]
    totals[-1][0] = after(totals[-1][0], grad_inputs, out_rows, grad_up, grad_down, grad_up_bias)
    grad_w_qkv, grad_w_out, extra_rows, sums = finish(totals, chunks)
    sums = sums[TAPS + 1 :].reshape(-1)[: 6 * width].reshape(6, width)
    return (
        out_rows,
        grad_inputs,
        grad_w_qkv.transpose(1, 0, 2),
        extra_rows[:, 0],
        extra_rows[1:, 1 : TAPS + 1],
        grad_w_out,
        sums[0:2],
        grad_up,
        grad_up_bias,
        grad_down,
        sums[2:4],
        sums[4:6],
    )


def solution(mesh):
    placed = (
        P("tp", "fsdp", None),
        P(None, "fsdp"),
        P("fsdp", None, "tp"),
        P(None, "tp"),
        P(None, None, "tp"),
        P("fsdp", "tp"),
        P(),
        P("fsdp", "tp"),
        P("tp"),
        P("fsdp", "tp"),
        P(),
        P(),
        P("tp", "fsdp", None),
    )
    return jax.shard_map(
        body,
        mesh=mesh,
        in_specs=placed,
        out_specs=(
            P("tp", "fsdp", None),
            P("tp", "fsdp", None),
            P("fsdp", None, "tp"),
            P(None, "tp"),
            P(None, None, "tp"),
            P("fsdp", "tp"),
            P(),
            P("fsdp", "tp"),
            P("tp"),
            P("fsdp", "tp"),
            P(),
            P(),
        ),
        check_vma=False,
    )
```

```python
from functools import partial

import jax
import jax.numpy as jnp
import numpy as np
from jax import lax
from jax.experimental import pallas as pl
from jax.experimental.pallas import tpu as pltpu
from jax.sharding import PartitionSpec as P

HEAD_DIM = 64
HALF = 64
STRIDE = 4
TAPS = 5
MARGIN = TAPS // 2
PAIR = 2 * HEAD_DIM
QB = 128
SB = 128
NEAR = QB + 2 * HALF
EXTRA = 16
RC = 256
EPSILON = 1e-05
NEG = -1e30
SCALE = HEAD_DIM**-0.5
BF = jnp.bfloat16
F32 = jnp.float32
MIB = 2**20


def nt(a, b):
    return lax.dot_general(a, b, (((1,), (1,)), ((), ())), preferred_element_type=F32)


def nn(a, b):
    return lax.dot_general(a, b, (((1,), (0,)), ((), ())), preferred_element_type=F32)


def tn(a, b):
    return lax.dot_general(a, b, (((0,), (0,)), ((), ())), preferred_element_type=F32)


def params(mib):
    return pltpu.CompilerParams(vmem_limit_bytes=mib * MIB)


def cost(flops, mib, trans=0):
    return pl.CostEstimate(flops=1, bytes_accessed=1, transcendentals=0)


def once(shape):
    zeros = (0,) * len(shape)
    return pl.BlockSpec(shape, lambda *_: zeros, pipeline_mode=pl.Buffered(1))


def project_kernel(count, offs, *refs):
    pieces = refs[:count]
    x_ref, bias_ref, taps_ref, same_ref, out_ref, pooled_ref, w_ref, plain = refs[count:]
    part = pl.program_id(0)
    for n in range(count):
        rows = pieces[n].shape[0]
        w_ref[0, pl.ds(pl.multiple_of(offs[n], 16), rows), :] = pieces[n][...]
    seqs, wide, _ = x_ref.shape
    far_rows = pooled_ref.shape[2]

    @pl.when(part < 3)
    def _():
        for s in range(seqs):
            made = (nn(x_ref[s], w_ref[0]) + bias_ref[0]).astype(BF)
            out_ref[0, s] = made
            for half in range(plain.shape[1]):
                plain[s, half] = made[:, half * PAIR : (half + 1) * PAIR].astype(F32)

    @pl.when((part > 0) & (part < 3))
    def _():
        for s in range(seqs):
            for half in range(plain.shape[1]):
                lanes = slice(half * PAIR, (half + 1) * PAIR)
                total = jnp.zeros((far_rows, PAIR), F32)
                for r in range(TAPS):
                    rows = plain[s, half, pl.ds(HALF - MARGIN + r, far_rows, stride=STRIDE), :]
                    total = total + taps_ref[0, r : r + 1, lanes] * rows * same_ref[
                        s, :, r : r + 1
                    ]
                pooled_ref[0, s, :, lanes] = total.astype(BF)


def project(chunk, chunks, pieces, offs, x_wide, bias, taps, same, far_rows):
    seqs, wide, width = x_wide.shape
    span = width // chunks

    def piece_spec(piece):
        return pl.BlockSpec((piece.shape[0], span), lambda c, o: (0, c * chunks + chunk))

    def three(c):
        return jnp.minimum(c, 2)

    def kv(c):
        return jnp.maximum(three(c) - 1, 0)

    return pl.pallas_call(
        partial(project_kernel, len(pieces)),
        grid_spec=pltpu.PrefetchScalarGridSpec(
            num_scalar_prefetch=1,
            grid=(4,),
            in_specs=[piece_spec(p) for p in pieces]
            + [
                once(x_wide.shape),
                pl.BlockSpec((1, 1, span), lambda c, o: (three(c), 0, chunk)),
                pl.BlockSpec((1, 8, span), lambda c, o: (kv(c), 0, chunk)),
                once(same.shape),
            ],
            out_specs=[
                pl.BlockSpec((1, seqs, wide, span), lambda c, o: (three(c), 0, 0, 0)),
                pl.BlockSpec((1, seqs, far_rows, span), lambda c, o: (kv(c), 0, 0, 0)),
                pl.BlockSpec((1, width, span), lambda c, o: (c, 0, 0)),
            ],
            scratch_shapes=[pltpu.VMEM((seqs, span // PAIR, wide, PAIR), F32)],
        ),
        out_shape=[
            jax.ShapeDtypeStruct((3, seqs, wide, span), BF),
            jax.ShapeDtypeStruct((2, seqs, far_rows, span), BF),
            jax.ShapeDtypeStruct((4, width, span), BF),
        ],
        compiler_params=params(32),
        cost_estimate=cost(6 * seqs * wide * width * span, 8),
    )(offs, *pieces, x_wide, bias, taps, same)


def fill_masks(segq_ref, segk_ref, cen_ref, near_bias, far_bias):
    rows = segq_ref.shape[1]
    shape = (QB, NEAR)
    gap = lax.broadcasted_iota(jnp.int32, shape, 1) - lax.broadcasted_iota(jnp.int32, shape, 0)
    band = (gap >= 0) & (gap <= 2 * HALF)
    for first in range(0, rows, QB):
        own = segq_ref[0, first : first + QB, :]
        keys = segk_ref[0, :, first : first + NEAR]
        near_bias[first : first + QB, :] = jnp.where(band & (own == keys), 0.0, NEG)
        far_bias[first : first + QB, :] = jnp.where(own == cen_ref[0], 0.0, NEG)


def head_mask(head):
    lane = lax.broadcasted_iota(jnp.int32, (1, PAIR), 1)
    return lane < HEAD_DIM if head == 0 else lane >= HEAD_DIM


def fold_lanes(*arrays):
    parts = [a[:, n : n + PAIR] for a in arrays for n in range(0, a.shape[1], PAIR)]
    while len(parts) > 1:
        parts = [sum(parts[n : n + 2]) for n in range(0, len(parts), 2)]
    return parts[0]


def softmax_rows(near, far):
    top = jnp.maximum(
        jnp.max(near, axis=-1, keepdims=True), jnp.max(far, axis=-1, keepdims=True)
    )
    near = jnp.exp(near - top)
    far = jnp.exp(far - top)
    total = jnp.sum(near, axis=-1, keepdims=True) + jnp.sum(far, axis=-1, keepdims=True)
    inverse = 1.0 / total
    return near * inverse, far * inverse


def stack_heads(rows, stacked):
    for first in range(0, rows.shape[0], QB):
        part = rows[first : first + QB]
        for head in range(2):
            stacked[2 * first + head * QB : 2 * first + (head + 1) * QB, :] = jnp.where(
                head_mask(head), part, BF(0)
            )


def join_slots(slots, joined):
    rows = slots[0].shape[1]
    for n, slot in enumerate(slots):
        joined[n * rows : (n + 1) * rows, :] = slot[0]


def attend_forward_kernel(blocks, q_ref, k_ref, v_ref, *refs):
    pk, pv = refs[:blocks], refs[blocks : 2 * blocks]
    segq, segk, cen, out_ref = refs[2 * blocks : 2 * blocks + 4]
    near_bias, far_bias, far_keys, far_values, query, far_scores, far_probs = refs[
        2 * blocks + 4 :
    ]

    @pl.when(pl.program_id(1) == 0)
    def _():
        fill_masks(segq, segk, cen, near_bias, far_bias)

    rows = out_ref.shape[1]
    join_slots(pk, far_keys)
    join_slots(pv, far_values)
    stack_heads(q_ref[0, HALF : HALF + rows, :] * BF(SCALE), query)
    far_scores[...] = nt(query[...], far_keys[...])
    outs = []
    for first in range(0, rows, QB):
        span = slice(first, first + NEAR)
        pair = slice(2 * first, 2 * first + 2 * QB)
        near_all = nt(query[pair, :], k_ref[0, span, :])
        lows = []
        for part in range(0, 2 * QB, SB):
            source = first + part % QB
            near, far = softmax_rows(
                near_all[part : part + SB] + near_bias[source : source + SB, :],
                far_scores[2 * first + part : 2 * first + part + SB, :]
                + far_bias[source : source + SB, :],
            )
            far_probs[2 * first + part : 2 * first + part + SB, :] = far.astype(BF)
            lows.append(near.astype(BF))
        outs.append(nn(jnp.concatenate(lows, axis=0), v_ref[0, span, :]))
    far_out = nn(far_probs[...], far_values[...])
    for n, first in enumerate(range(0, rows, QB)):
        both = outs[n] + far_out[2 * first : 2 * first + 2 * QB]
        out_ref[0, first : first + QB, :] = jnp.where(head_mask(0), both[:QB], both[QB:]).astype(BF)


def attend_backward_kernel(blocks, q_ref, k_ref, v_ref, *refs):
    pk, pv = refs[:blocks], refs[blocks : 2 * blocks]
    segq, segk, cen, grad_ref, dq_ref, dk_ref, dv_ref = refs[2 * blocks : 2 * blocks + 7]
    dp_refs = refs[2 * blocks + 7 : 2 * blocks + 9]
    (
        near_bias, far_bias, far_keys, far_values,
        query, far_scores, far_probs, grad, far_dots, far_grads,
    ) = refs[2 * blocks + 9 :]

    @pl.when(pl.program_id(1) == 0)
    def _():
        fill_masks(segq, segk, cen, near_bias, far_bias)

    rows = dq_ref.shape[1]
    join_slots(pk, far_keys)
    join_slots(pv, far_values)
    stack_heads(q_ref[0, HALF : HALF + rows, :] * BF(SCALE), query)
    stack_heads(grad_ref[0], grad)
    far_scores[...] = nt(query[...], far_keys[...])
    far_dots[...] = nt(grad[...], far_values[...])
    dk_ref[...] = jnp.zeros_like(dk_ref)
    dv_ref[...] = jnp.zeros_like(dv_ref)
    dqs = []
    for first in range(0, rows, QB):
        span = slice(first, first + NEAR)
        pair = slice(2 * first, 2 * first + 2 * QB)
        near_all = nt(query[pair, :], k_ref[0, span, :])
        dots_all = nt(grad[pair, :], v_ref[0, span, :])
        lows, grads = [], []
        for part in range(0, 2 * QB, SB):
            source = first + part % QB
            here = slice(2 * first + part, 2 * first + part + SB)
            near, far = softmax_rows(
                near_all[part : part + SB] + near_bias[source : source + SB, :],
                far_scores[here, :] + far_bias[source : source + SB, :],
            )
            near_dot, far_dot = dots_all[part : part + SB], far_dots[here, :]
            row_dot = jnp.sum(
                fold_lanes(near * near_dot, far * far_dot), axis=-1, keepdims=True
            )
            far_probs[here, :] = far.astype(BF)
            far_grads[here, :] = (far * (far_dot - row_dot)).astype(BF)
            lows.append(near.astype(BF))
            grads.append((near * (near_dot - row_dot)).astype(BF))
        low = jnp.concatenate(lows, axis=0)
        ds = jnp.concatenate(grads, axis=0)
        dqs.append(nn(ds, k_ref[0, span, :]))
        dk_ref[0, span, :] += nn(query[pair, :].T, ds).T
        dv_ref[0, span, :] += nn(grad[pair, :].T, low).T
    far_dq = nn(far_grads[...], far_keys[...])
    for n, first in enumerate(range(0, rows, QB)):
        both = (dqs[n] + far_dq[2 * first : 2 * first + 2 * QB]) * SCALE
        dq_ref[0, first : first + QB, :] = jnp.where(head_mask(0), both[:QB], both[QB:]).astype(BF)
    dpk = nn(query[...].T, far_grads[...]).T.astype(BF)
    dpv = nn(grad[...].T, far_probs[...]).T.astype(BF)
    far_rows = dp_refs[0].shape[3]
    for n in range(blocks):
        span = slice(n * far_rows, (n + 1) * far_rows)
        dp_refs[n % 2][n // 2, 0, 0] = dpk[span]
        dp_refs[n % 2][n // 2, 1, 0] = dpv[span]


def attention_specs(wide, blocks, far_rows):
    def own(part):
        return pl.BlockSpec((None, 1, wide, PAIR), lambda s, h: (part, s, 0, h))

    def pooled(part):
        return pl.BlockSpec((None, 1, far_rows, PAIR), lambda s, h: (part, s, 0, h))

    rows = wide - 2 * HALF
    return (
        [own(0), own(1), own(2)]
        + [pooled(0)] * blocks
        + [pooled(1)] * blocks
        + [
            pl.BlockSpec((1, rows, 1), lambda s, h: (s, 0, 0)),
            pl.BlockSpec((1, 1, wide), lambda s, h: (s, 0, 0)),
            pl.BlockSpec((1, 1, blocks * far_rows), lambda s, h: (s, 0, 0)),
        ]
    )


def attention_scratch(rows, far_all):
    return [
        pltpu.VMEM((rows, NEAR), F32),
        pltpu.VMEM((rows, far_all), F32),
        pltpu.VMEM((far_all, PAIR), BF),
        pltpu.VMEM((far_all, PAIR), BF),
        pltpu.VMEM((2 * rows, PAIR), BF),
        pltpu.VMEM((2 * rows, far_all), F32),
        pltpu.VMEM((2 * rows, far_all), BF),
    ]


def attend_forward(proj, slots, segs):
    _, seqs, wide, span = proj.shape
    blocks, far_rows = len(slots), slots[0].shape[2]
    rows = wide - 2 * HALF
    cells = seqs * rows * (NEAR + blocks * far_rows) * (span // HEAD_DIM)
    return pl.pallas_call(
        partial(attend_forward_kernel, blocks),
        grid=(seqs, span // PAIR),
        in_specs=attention_specs(wide, blocks, far_rows),
        out_specs=pl.BlockSpec((1, rows, PAIR), lambda s, h: (s, 0, h)),
        out_shape=jax.ShapeDtypeStruct((seqs, rows, span), BF),
        scratch_shapes=attention_scratch(rows, blocks * far_rows),
        compiler_params=params(60),
        cost_estimate=cost(16 * 64 * cells, 8, cells),
    )(proj, proj, proj, *slots, *slots, *segs)


def attend_backward(proj, slots, segs, grad):
    _, seqs, wide, span = proj.shape
    blocks, far_rows = len(slots), slots[0].shape[2]
    rows = wide - 2 * HALF
    cells = seqs * rows * (NEAR + blocks * far_rows) * (span // HEAD_DIM)
    own_spec = pl.BlockSpec((1, rows, PAIR), lambda s, h: (s, 0, h))
    wide_spec = pl.BlockSpec((1, wide, PAIR), lambda s, h: (s, 0, h))
    wide_shape = jax.ShapeDtypeStruct((seqs, wide, span), F32)
    far_spec = pl.BlockSpec((blocks // 2, 2, 1, far_rows, PAIR), lambda s, h: (0, 0, s, 0, h))
    far_shape = jax.ShapeDtypeStruct((blocks // 2, 2, seqs, far_rows, span), BF)
    out = pl.pallas_call(
        partial(attend_backward_kernel, blocks),
        grid=(seqs, span // PAIR),
        in_specs=attention_specs(wide, blocks, far_rows) + [own_spec],
        out_specs=[own_spec, wide_spec, wide_spec] + [far_spec] * 2,
        out_shape=[jax.ShapeDtypeStruct((seqs, rows, span), BF), wide_shape, wide_shape]
        + [far_shape] * 2,
        scratch_shapes=attention_scratch(rows, blocks * far_rows)
        + [
            pltpu.VMEM((2 * rows, PAIR), BF),
            pltpu.VMEM((2 * rows, blocks * far_rows), F32),
            pltpu.VMEM((2 * rows, blocks * far_rows), BF),
        ],
        compiler_params=params(60),
        cost_estimate=cost(40 * 64 * cells, 16, cells),
    )(proj, proj, proj, *slots, *slots, *segs, grad)
    return out[0], out[1], out[2], out[3:]


def norm_stats(residual):
    row_mean = jnp.mean(residual, axis=-1, keepdims=True)
    centered = residual - row_mean
    variance = jnp.mean(centered * centered, axis=-1, keepdims=True)
    inverse = lax.rsqrt(variance + EPSILON)
    return centered * inverse, inverse


def norm_back(grad, normed, inverse, gain):
    scaled = grad * gain
    first = jnp.mean(scaled, axis=-1, keepdims=True)
    second = jnp.mean(scaled * normed, axis=-1, keepdims=True)
    return (scaled - first - normed * second) * inverse


def column_sum(values):
    return jnp.sum(values.astype(F32), axis=0, keepdims=True)


def dense_kernel(chunks, steps, *refs):
    att, wout = refs[:chunks], refs[chunks : 2 * chunks]
    x_ref, cot_ref, up_blk, down_blk, bup_ref, misc_ref = refs[2 * chunks : 2 * chunks + 6]
    outs = refs[2 * chunks + 6 :]
    out_ref, gres_ref = outs[:2]
    gatt = outs[2 : 2 + chunks]
    gout = outs[2 + chunks : 2 + 2 * chunks]
    gud_ref, small_ref = outs[2 + 2 * chunks : 4 + 2 * chunks]
    (
        inverse, flow, flow_t, acc, gffn, gffn_t, hidden, slope, gpre
    ) = outs[4 + 2 * chunks :]
    step = pl.program_id(0)
    seqs, rows, width = cot_ref.shape
    total = seqs * rows
    span = width // chunks
    units = gpre.shape[1]
    up_ref = up_blk[...].reshape(width, units)
    down_ref = down_blk[...].reshape(width, units)
    bias_one, bias_two = misc_ref[0:1, :], misc_ref[1:2, :]
    gain_one, gain_two = misc_ref[2:3, :], misc_ref[3:4, :]
    shift_one, shift_two = misc_ref[4:5, :], misc_ref[5:6, :]
    parts = [(first, first // rows, first % rows) for first in range(0, total, RC)]

    @pl.when(step == 0)
    def _():
        for first, s, row in parts:
            block = slice(first, first + RC)
            branch = bias_one
            for j in range(chunks):
                branch = branch + nt(
                    att[j][s, row : row + RC, :], wout[j][0]
                )
            n_one, inv = norm_stats(
                x_ref[s, HALF + row : HALF + row + RC, :].astype(F32) + branch
            )
            gres_ref[s, row : row + RC, :] = n_one
            inverse[block, :] = inv
            low = (n_one * gain_one + shift_one).astype(BF)
            flow[block, :] = low
            flow_t[:, block] = low.T
            acc[block, :] = jnp.zeros((RC, width), F32)

    @pl.when(step < steps)
    def _():
        for first, s, row in parts:
            block = slice(first, first + RC)
            pre = nn(flow[block, :], up_ref) + bup_ref[...]
            cdf = 0.5 * (1.0 + lax.erf(pre * np.float32(np.sqrt(0.5))))
            pdf = jnp.exp(-0.5 * (pre * pre)) * np.float32(1.0 / np.sqrt(2.0 * np.pi))
            low = (pre * cdf).astype(BF)
            hidden[step, block, :] = low
            slope[step, block, :] = cdf + pre * pdf
            acc[block, :] += nt(low, down_ref)

    @pl.when(step == steps)
    def _():
        small_ref[...] = jnp.zeros_like(small_ref)
        for first, s, row in parts:
            block = slice(first, first + RC)
            first_out = gres_ref[s, row : row + RC, :] * gain_one + shift_one
            n_two, inv = norm_stats(first_out + (acc[block, :] + bias_two))
            out_ref[s, row : row + RC, :] = (n_two * gain_two + shift_two).astype(BF)
            grad = cot_ref[s, row : row + RC, :].astype(F32)
            second = norm_back(grad, n_two, inv, gain_two)
            acc[block, :] = second
            low = second.astype(BF)
            gffn[block, :] = low
            gffn_t[:, block] = low.T
            small_ref[1:2, :] += column_sum(low)
            small_ref[3:4, :] += column_sum(grad * n_two)
            small_ref[5:6, :] += column_sum(grad)

    @pl.when(step >= steps)
    def _():
        which = 2 * steps - 1 - step
        bias_sum = jnp.zeros((1, units), F32)
        for first, s, row in parts:
            block = slice(first, first + RC)
            grad = nn(gffn[block, :], down_ref)
            low = (grad * slope[which, block, :]).astype(BF)
            gpre[block, :] = low
            bias_sum = bias_sum + column_sum(low)
            acc[block, :] += nt(low, up_ref)
        height = gud_ref.shape[3] - EXTRA
        lead = (gud_ref.shape[0], height, units)
        gud_ref[:, 0, 0, :height] = nn(flow_t[...], gpre[...]).astype(BF).reshape(lead)
        gud_ref[:, 0, 1, :height] = nn(gffn_t[...], hidden[which]).astype(BF).reshape(lead)
        head = lax.broadcasted_iota(jnp.int32, (EXTRA, 1), 0) == 0
        extra = jnp.where(head, bias_sum, 0.0).astype(BF)
        for m in range(gud_ref.shape[0]):
            gud_ref[m, 0, 0, height:] = extra
            gud_ref[m, 0, 1, height:] = jnp.zeros((EXTRA, units), BF)

    @pl.when(step == 2 * steps - 1)
    def _():
        for first, s, row in parts:
            block = slice(first, first + RC)
            grad = acc[block, :]
            n_one = gres_ref[s, row : row + RC, :]
            back = norm_back(grad, n_one, inverse[block, :], gain_one)
            gres_ref[s, row : row + RC, :] = back
            low = back.astype(BF)
            flow_t[:, block] = low.T
            small_ref[0:1, :] += column_sum(low)
            small_ref[2:3, :] += column_sum(grad * n_one)
            small_ref[4:5, :] += column_sum(grad)
            for j in range(chunks):
                gatt[j][s, row : row + RC, :] = nn(
                    low, wout[j][0]
                ).astype(BF)
        for j in range(chunks):
            gout[j][...] = nn(flow_t[...], att[j][...].reshape(total, span)).astype(BF)


def dense(att, projected_weights, x_wide, cot, weights, bias_up, misc):
    chunks = len(att)
    seqs, rows, width = cot.shape
    total = seqs * rows
    span = width // chunks
    row_blocks, steps, height, units = weights.shape
    units //= 2

    def which(i):
        return jnp.where(i < steps, i, 2 * steps - 1 - i)

    def back(i):
        return jnp.where(i < steps, steps - 1, 2 * steps - 1 - i)

    out_shape = (
        [
            jax.ShapeDtypeStruct((seqs, rows, width), BF),
            jax.ShapeDtypeStruct((seqs, rows, width), F32),
        ]
        + [jax.ShapeDtypeStruct((seqs, rows, span), BF)] * chunks
        + [jax.ShapeDtypeStruct((width, span), BF)] * chunks
        + [
            jax.ShapeDtypeStruct((row_blocks, steps, 2, height + EXTRA, units), BF),
            jax.ShapeDtypeStruct((8, width), F32),
        ]
    )
    out_specs = [once(o.shape) for o in out_shape[: 2 + 2 * chunks]] + [
        pl.BlockSpec(
            (row_blocks, 1, 2, height + EXTRA, units), lambda i: (0, back(i), 0, 0, 0)
        ),
        once((8, width)),
    ]
    out = pl.pallas_call(
        partial(dense_kernel, chunks, steps),
        grid=(2 * steps,),
        in_specs=[once(a.shape) for a in att]
        + [
            pl.BlockSpec(
                (1, width, span), lambda i: (3, 0, 0), pipeline_mode=pl.Buffered(1)
            )
        ]
        * chunks
        + [
            once(x_wide.shape),
            once(cot.shape),
            pl.BlockSpec((row_blocks, None, height, units), lambda i: (0, which(i), 0, 0)),
            pl.BlockSpec((row_blocks, None, height, units), lambda i: (0, which(i), 0, 1)),
            pl.BlockSpec((1, units), lambda i: (0, which(i))),
            once(misc.shape),
        ],
        out_specs=out_specs,
        out_shape=out_shape,
        scratch_shapes=[
            pltpu.VMEM((total, 1), F32),
            pltpu.VMEM((total, width), BF),
            pltpu.VMEM((width, total), BF),
            pltpu.VMEM((total, width), F32),
            pltpu.VMEM((total, width), BF),
            pltpu.VMEM((width, total), BF),
            pltpu.VMEM((steps, total, units), BF),
            pltpu.VMEM((steps, total, units), F32),
            pltpu.VMEM((total, units), BF),
        ],
        compiler_params=params(63),
        cost_estimate=cost(1, 1),
    )(*att, *projected_weights, x_wide, cot, weights, weights, bias_up, misc)
    return (
        out[0], out[1], out[2 : 2 + chunks], out[2 + chunks : 2 + 2 * chunks], out[-2], out[-1]
    )


def gather_back_kernel(blocks, chunks, groups, offs, *refs):
    taken = 5 + blocks + 1
    per_chunk = [refs[n * taken : (n + 1) * taken] for n in range(chunks)]
    taps_ref, same_ref, xt_ref, more_ref = refs[chunks * taken : chunks * taken + 4]
    outs = refs[chunks * taken + 4 :]
    gws = outs[:groups]
    lows = outs[groups : groups + chunks]
    small, plain, spread, low_q, total, stage = outs[groups + chunks :]
    width = xt_ref.shape[0]
    seq = pl.program_id(0)
    wide, span = per_chunk[0][0].shape[1:]
    rows = wide - 2 * HALF
    far_rows = per_chunk[0][3].shape[2]

    @pl.when(seq == 0)
    def _():
        small[...] = jnp.zeros_like(small)
        total[...] = jnp.zeros_like(total)

    for n, chunk_refs in enumerate(per_chunk):
        dk_ref, dv_ref, dq_ref = chunk_refs[:3]
        dps = chunk_refs[3 : 3 + blocks]
        proj_k, proj_v = chunk_refs[3 + blocks : 5 + blocks]
        low = lows[n]
        base = n * span
        low_q[:HALF, :] = jnp.zeros((HALF, span), BF)
        low_q[HALF : HALF + rows, :] = dq_ref[0]
        low_q[HALF + rows :, :] = jnp.zeros((HALF, span), BF)
        small[0, 0:1, base : base + span] += column_sum(dq_ref[0])
        for c, (near, proj) in enumerate(((dk_ref, proj_k), (dv_ref, proj_v))):
            for half in range(span // PAIR):
                lanes = slice(half * PAIR, (half + 1) * PAIR)
                wider = slice(base + half * PAIR, base + (half + 1) * PAIR)
                plain[...] = proj[0, 0, :, lanes].astype(F32)
                spread[...] = near[0, :, lanes]
                pooled = dps[0][c, 0, :, lanes].astype(F32)
                for d in range(1, blocks):
                    pooled = pooled + dps[d][c, 0, :, lanes].astype(F32)
                pooled = pooled.astype(BF).astype(F32)
                for r in range(TAPS):
                    place = pl.ds(HALF - MARGIN + r, far_rows, stride=STRIDE)
                    masked = pooled * same_ref[0, :, r : r + 1]
                    small[1 + c, 1 + r : 2 + r, wider] += column_sum(masked * plain[place, :])
                    spread[place, :] = spread[place, :] + taps_ref[c, r : r + 1, wider] * masked
                made = spread[...].astype(BF)
                low[c, 0, :, lanes] = made
                small[1 + c, 0:1, wider] += column_sum(made)
        total[n, 0] += nn(xt_ref[...], low_q[...])
        total[n, 1] += nn(xt_ref[...], low[0, 0])
        total[n, 2] += nn(xt_ref[...], low[1, 0])

    @pl.when(seq == pl.num_programs(0) - 1)
    def _():
        heads = span // HEAD_DIM
        lane = lax.broadcasted_iota(jnp.int32, (1, PAIR), 1) < HEAD_DIM

        def place_four(four, n, u, where):
            turned = [pltpu.roll(value, HEAD_DIM, 1) for value in four]
            for pair in range(2):
                one, two = 2 * pair, 2 * pair + 1
                first = (2 * n + pair) * PAIR
                lanes = slice(first, first + PAIR)
                stage[2 * u, where, lanes] = jnp.where(lane, four[one], turned[two]).astype(BF)
                stage[2 * u + 1, where, lanes] = jnp.where(lane, turned[one], four[two]).astype(BF)

        for n, chunk_refs in enumerate(per_chunk):
            gout_ref = chunk_refs[5 + blocks]
            for u in range(heads // 2):
                lanes = slice(u * PAIR, (u + 1) * PAIR)
                wider = slice(n * span + u * PAIR, n * span + (u + 1) * PAIR)
                four = [total[n, part, :, lanes] for part in range(3)]
                four.append(gout_ref[:, lanes].astype(F32))
                place_four(four, n, u, slice(0, width))
                place_four(
                    [small[part, :, wider] for part in range(4)], n, u, slice(width, width + EXTRA)
                )
        last = slice(width, width + EXTRA)
        head = lax.broadcasted_iota(jnp.int32, (EXTRA, 1), 0) <= TAPS
        for t in range(heads):
            stage[t, last, :] = jnp.where(
                head, stage[t, last, :].astype(F32), more_ref[...]
            ).astype(BF)
        height = gws[0].shape[2] - EXTRA
        number = 0
        for group in gws:
            for m in range(group.shape[0]):
                place = pl.ds(pl.multiple_of(offs[number], 16), height)
                group[m, :, :height] = stage[:, place, :]
                group[m, :, height:] = stage[:, last, :]
                number += 1


def gather_back(first_chunk, offs, group_sizes, parts, taps, same, xt, more):
    chunks = len(parts)
    seqs, wide, span = parts[0][1].shape
    width = xt.shape[0]
    rows = wide - 2 * HALF
    blocks, far_rows = len(parts[0][3]), parts[0][3][0].shape[2]
    height = width // sum(group_sizes)
    heads = span // HEAD_DIM
    in_specs, operands = [], []
    for dq, dk, dv, dps, proj, gout in parts:
        in_specs += [pl.BlockSpec((1, wide, span), lambda s, o: (s, 0, 0))] * 2
        in_specs += [pl.BlockSpec((1, rows, span), lambda s, o: (s, 0, 0))]
        in_specs += [pl.BlockSpec((2, 1, far_rows, span), lambda s, o: (0, s, 0, 0))] * blocks
        in_specs += [
            pl.BlockSpec((1, 1, wide, span), lambda s, o: (1, s, 0, 0)),
            pl.BlockSpec((1, 1, wide, span), lambda s, o: (2, s, 0, 0)),
            once(gout.shape),
        ]
        operands += [dk, dv, dq, *dps, proj, proj, gout]
    out = pl.pallas_call(
        partial(gather_back_kernel, blocks, chunks, len(group_sizes)),
        grid_spec=pltpu.PrefetchScalarGridSpec(
            num_scalar_prefetch=1,
            grid=(seqs,),
            in_specs=in_specs
            + [
                once((2, 8, span * chunks)),
                pl.BlockSpec((1, far_rows, 8), lambda s, o: (s, 0, 0)),
                pl.BlockSpec((width, wide), lambda s, o: (0, s)),
                once(more.shape),
            ],
            out_specs=[
                once((size, heads, height + EXTRA, 4 * HEAD_DIM * chunks)) for size in group_sizes
            ]
            + [pl.BlockSpec((2, 1, wide, span), lambda s, o: (0, s, 0, 0))] * chunks,
            scratch_shapes=[
                pltpu.VMEM((4, EXTRA, span * chunks), F32),
                pltpu.VMEM((wide, PAIR), F32),
                pltpu.VMEM((wide, PAIR), F32),
                pltpu.VMEM((wide, span), BF),
                pltpu.VMEM((chunks, 3, width, span), F32),
                pltpu.VMEM((heads, width + EXTRA, 4 * HEAD_DIM * chunks), BF),
            ],
        ),
        out_shape=[
            jax.ShapeDtypeStruct((size, heads, height + EXTRA, 4 * HEAD_DIM * chunks), BF)
            for size in group_sizes
        ]
        + [jax.ShapeDtypeStruct((2, seqs, wide, span), BF)] * chunks,
        compiler_params=params(60),
        cost_estimate=cost(6 * chunks * seqs * wide * width * span, 12 * chunks),
    )(offs, *operands, taps[:, :, first_chunk * span : (first_chunk + chunks) * span], same, xt, more)
    return out[: len(group_sizes)], out[len(group_sizes) :]


def input_grad_kernel(chunks, *refs):
    per_chunk = [refs[3 * n : 3 * n + 3] for n in range(chunks)]
    res_ref, mid_ref, first_ref, last_ref = refs[3 * chunks :]
    rows = mid_ref.shape[1]
    edge = None
    inner = res_ref[0]
    for dq_ref, low_ref, w_ref in per_chunk:
        inner = inner + nt(dq_ref[0], w_ref[0])
        for c in range(2):
            term = nt(low_ref[c, 0], w_ref[1 + c])
            edge = term if edge is None else edge + term
    mid_ref[0] = inner + edge[HALF : HALF + rows]
    first_ref[0] = edge[:HALF].astype(BF)
    last_ref[0] = edge[HALF + rows :].astype(BF)


def input_grad(parts, residual):
    seqs, rows, width = residual.shape
    wide, span = parts[0][1].shape[2:]
    in_specs, operands = [], []
    for dq, low, w in parts:
        in_specs += [
            pl.BlockSpec((1, rows, span), lambda s: (s, 0, 0)),
            pl.BlockSpec((2, 1, wide, span), lambda s: (0, s, 0, 0)),
            pl.BlockSpec(
                (3,) + w.shape[1:], lambda s: (0, 0, 0), pipeline_mode=pl.Buffered(1)
            ),
        ]
        operands += [dq, low, w]
    own = pl.BlockSpec((1, rows, width), lambda s: (s, 0, 0))
    edge = pl.BlockSpec((1, HALF, width), lambda s: (s, 0, 0))
    return pl.pallas_call(
        partial(input_grad_kernel, len(parts)),
        grid=(seqs,),
        in_specs=in_specs + [own],
        out_specs=[own, edge, edge],
        out_shape=[
            jax.ShapeDtypeStruct((seqs, rows, width), F32),
            jax.ShapeDtypeStruct((seqs, HALF, width), BF),
            jax.ShapeDtypeStruct((seqs, HALF, width), BF),
        ],
        compiler_params=params(60),
        cost_estimate=cost(6 * len(parts) * seqs * wide * width * span, 16),
    )(*operands, residual)


def after(value, *others):
    return lax.optimization_barrier((value,) + others)[0]


def finish_kernel(terms, chunks, *refs):
    groups = [refs[:terms], refs[terms : 2 * terms]]
    qkv_ref, out_ref, extra_ref, sums_ref = refs[2 * terms :]
    totals = []
    for group in groups:
        total = group[0][...].astype(F32)
        for ref in group[1:]:
            total = total + ref[...].astype(F32)
        totals.append(total)
    rows = out_ref.shape[0]
    sums_ref[...] = totals[0][rows:]
    lane = lax.broadcasted_iota(jnp.int32, (1, PAIR), 1) < HEAD_DIM
    first_count = totals[0].shape[1] // (4 * HEAD_DIM)

    def part(chunk, which, high):
        source = totals[0] if chunk < first_count else totals[1]
        chunk = chunk if chunk < first_count else chunk - first_count
        tile = 2 * chunk + which // 2
        values = source[:, tile * PAIR : (tile + 1) * PAIR]
        return values if which % 2 == high else pltpu.roll(values, HEAD_DIM, 1)

    for which in range(4):
        for chunk in range(0, chunks, 2):
            first = chunk * HEAD_DIM
            if chunk + 1 < chunks:
                made = jnp.where(lane, part(chunk, which, 0), part(chunk + 1, which, 1))
            else:
                made = part(chunk, which, 0)[:, :HEAD_DIM]
            lanes = slice(first, first + made.shape[1])
            if which < 3:
                qkv_ref[which, :, lanes] = made[:rows]
                extra_ref[which, :, lanes] = made[rows:]
            else:
                out_ref[:, lanes] = made[:rows]


def finish(groups, chunks):
    rows = groups[0][0].shape[0] - EXTRA
    local = chunks * HEAD_DIM
    return pl.pallas_call(
        partial(finish_kernel, len(groups[0]), chunks),
        out_shape=[
            jax.ShapeDtypeStruct((3, rows, local), F32),
            jax.ShapeDtypeStruct((rows, local), F32),
            jax.ShapeDtypeStruct((3, EXTRA, local), F32),
            jax.ShapeDtypeStruct((EXTRA, groups[0][0].shape[1]), F32),
        ],
        compiler_params=params(16),
        cost_estimate=cost(1, 1),
    )(*groups[0], *groups[1])


def swap(values, axis, mask):
    count = lax.axis_size(axis)
    return lax.ppermute(values, axis, [(i, i ^ mask) for i in range(count)])


def shift_right(rows):
    count = lax.axis_size("tp")
    return lax.ppermute(rows, "tp", [(i, i + 1) for i in range(count - 1)])


def shift_left(rows):
    count = lax.axis_size("tp")
    return lax.ppermute(rows, "tp", [(i + 1, i) for i in range(count - 1)])


def gather_columns(shard):
    if lax.axis_size("tp") != 4:
        return lax.all_gather(shard, "tp", axis=0, tiled=False)
    me = lax.axis_index("tp")
    found = [shard] + [swap(shard, "tp", mask) for mask in (1, 2, 3)]
    odd, high = me % 2 == 1, me >= 2
    found = [jnp.where(odd, found[n ^ 1], found[n]) for n in range(4)]
    return jnp.stack([jnp.where(high, found[n ^ 2], found[n]) for n in range(4)])


def gather_pieces(shard, beside):
    mine = lax.axis_index("fsdp")
    rows = shard.shape[0]
    half = rows // 2
    across = swap(shard, "fsdp", 2)
    along = swap(shard, "fsdp", 4)
    onward = after(across[:half], *beside)
    corner = [swap(onward, "fsdp", 4), swap(along[half:], "fsdp", 2)]
    own = [shard, across, along] + corner
    other = [swap(piece, "fsdp", 1) for piece in own]
    place = [
        (mine ^ mask) * rows + extra
        for core in (0, 1)
        for mask, extra in ((core, 0), (2 + core, 0), (4 + core, 0), (6 + core, 0), (6 + core, half))
    ]
    return own + other, jnp.stack(place).astype(jnp.int32)


def spread_line(values):
    two = swap(values, "tp", 2)
    return [swap(after(values, two), "tp", 1), two, swap(two, "tp", 1)]


def merge_line(own, other, *waits):
    sent = after(other, *waits) if waits else other
    merged = add_low(own, swap(sent, "tp", 1)).astype(BF)
    return [merged[0], swap(merged[1], "tp", 2)]


def add_low(first, *others):
    total = first.astype(F32)
    for other in others:
        total = total + other.astype(F32)
    return total


def merge_cores(keep, send):
    return add_low(keep, swap(send, "fsdp", 1)).astype(BF)


def merge_chips(blocks, *beside):
    own = after(blocks[0], *beside) if beside else blocks[0]
    return add_low(own, *[swap(blocks[n], "fsdp", 2 * n) for n in (1, 2, 3)]).astype(BF)


def scatter_tp(blocks):
    count = lax.axis_size("tp")
    me = lax.axis_index("tp")

    def pick(d):
        return lax.dynamic_index_in_dim(blocks, me ^ d, 0, keepdims=False)

    return [pick(0)] + [swap(pick(d), "tp", d) for d in range(1, count)]


def spread_rows(whole, blocks):
    parts, rows, cols = whole.shape
    rows -= EXTRA
    main = whole[:, :rows].reshape(parts, blocks, rows // blocks, cols).transpose(1, 0, 2, 3)
    more = jnp.broadcast_to(whole[None, :, rows:], (blocks, parts, EXTRA, cols))
    return jnp.concatenate([main, more], axis=2)


def split_three(values):
    high = lax.reduce_precision(values, 8, 7)
    rest = values - high
    middle = lax.reduce_precision(rest, 8, 7)
    return jnp.stack([high, middle, rest - middle]).astype(BF)


def body(
    inputs, segments, w_qkv, qkv_bias, pool_kernel, w_out, out_bias,
    w_up, up_bias, w_down, norm_gains, norm_shifts, cotangent,
):
    rows, seqs, width = inputs.shape
    tp = lax.axis_size("tp")
    fsdp = lax.axis_size("fsdp")
    place = lax.axis_index("tp")
    shard_rows = w_qkv.shape[0]
    local = w_qkv.shape[2]
    chunks = local // HEAD_DIM
    span = tp * HEAD_DIM
    hidden_local = w_up.shape[1]
    hidden_units = hidden_local * tp
    far_rows = rows // STRIDE
    fast = fsdp == 8 and shard_rows % 32 == 0

    bias_values = jnp.concatenate(
        [qkv_bias.reshape(-1), pool_kernel.reshape(-1), up_bias.reshape(-1)]
    )
    biases = split_three(bias_values)
    extra = -(-biases.size // (4 * local))
    packed = jnp.concatenate(
        [
            jnp.concatenate([w_qkv.reshape(shard_rows, 3 * local), w_out], axis=1),
            jnp.pad(biases.reshape(-1), (0, extra * 4 * local - biases.size)).reshape(
                extra, 4 * local
            ),
        ],
        axis=0,
    )
    left = shift_right(inputs[rows - HALF :])
    right = shift_left(inputs[:HALF])
    columns = gather_columns(packed)
    wide_rows = (
        columns[:, :shard_rows]
        .reshape(tp, shard_rows, 4, chunks, HEAD_DIM)
        .transpose(1, 2, 3, 0, 4)
        .reshape(shard_rows, 4 * width)
    )
    whole_bias = jnp.sum(
        columns[:, shard_rows:].reshape(tp, -1)[:, : biases.size].reshape(tp, 3, -1).astype(F32),
        axis=1,
    )
    lead = (3 + 2 * TAPS) * local
    featured = (
        whole_bias[:, :lead]
        .reshape(tp, 3 + 2 * TAPS, chunks, HEAD_DIM)
        .transpose(1, 2, 0, 3)
        .reshape(3 + 2 * TAPS, width)
    )
    bias_qkv = featured[:3, None, :]
    taps = jnp.pad(featured[3:].reshape(2, TAPS, width), ((0, 0), (0, 8 - TAPS), (0, 0)))
    bias_up = whole_bias[:, lead:].reshape(1, hidden_units)

    x_wide = jnp.concatenate([left, inputs, right], axis=0).transpose(1, 0, 2)
    wide = rows + 2 * HALF

    seg_rows = segments.T
    padded = jnp.pad(seg_rows, ((0, 0), (HALF, HALF)), constant_values=-1)
    seg_keys = lax.dynamic_slice_in_dim(padded, place * rows, wide, 1)
    seg_own = seg_keys[:, HALF : HALF + rows]
    centers = seg_rows[:, ::STRIDE].reshape(seqs, tp, far_rows)
    centers_cycle = jnp.concatenate(
        [
            lax.dynamic_index_in_dim(centers, place ^ d, 1, keepdims=True)
            for d in range(tp)
        ],
        axis=1,
    ).reshape(seqs, 1, tp * far_rows)
    segs = (seg_own[:, :, None], seg_keys[:, None, :], centers_cycle)
    own_centers = seg_own[:, ::STRIDE]
    same = jnp.stack(
        [
            seg_keys[:, HALF - MARGIN + r : HALF - MARGIN + r + rows : STRIDE][:, :far_rows]
            == own_centers
            for r in range(TAPS)
        ]
        + [jnp.zeros_like(own_centers, dtype=bool)] * (8 - TAPS),
        axis=2,
    ).astype(F32)

    if fast:
        pieces, offs = gather_pieces(wide_rows, (x_wide, same, bias_qkv, taps) + segs)
    else:
        pieces = [lax.all_gather(wide_rows, "fsdp", axis=0, tiled=True)]
        offs = jnp.zeros((1,), jnp.int32)

    weights = lax.all_gather(
        jnp.concatenate([w_up, w_down], axis=1), "tp", axis=0, tiled=False
    )

    made, slots, att = [], [], []

    def send_pooled(j, *waits):
        pooled = made[j][1]
        sent = after(pooled, *waits) if waits else pooled
        slots.append([pooled] + spread_line(sent))

    for j in range(chunks):
        if j:
            offs = after(offs, made[-1][1], *([slots[0][2]] if j > 1 else []))
        made.append(project(j, chunks, pieces, offs, x_wide, bias_qkv, taps, same, far_rows))
        if j == 0:
            send_pooled(0)
    if chunks > 1:
        send_pooled(1, slots[0][2], made[-1][1])
    weights = after(weights, made[0][1])
    weights = lax.all_gather(weights, "fsdp", axis=0, tiled=False)
    for j in range(chunks):
        waits = att[-1:]
        if j == 1:
            x_cols = after(x_wide, att[0]).reshape(seqs * wide, width).T
            cot = after(cotangent, att[0]).transpose(1, 0, 2)
            waits += [x_cols, cot]
        order = segs[:2] + (after(segs[2], *waits) if waits else segs[2],)
        att.append(attend_forward(made[j][0], slots[j], order))
        if j + 2 < chunks:
            send_pooled(j + 2, att[j], slots[j + 1][2])
    if shard_rows % 16:
        weights = weights.transpose(1, 0, 2, 3).reshape(1, tp, width, -1)

    misc = jnp.concatenate([out_bias, norm_gains, norm_shifts, jnp.zeros((2, width), F32)])
    outputs, grad_residual, grad_att, grad_out, gud, small = dense(
        att, [m[2] for m in made], x_wide, cot, weights, bias_up, misc
    )
    if gud.shape[0] == 1:
        gud = spread_rows(gud.reshape(2 * tp, -1, hidden_local), fsdp)
        gud = gud.reshape(fsdp, tp, 2, -1, hidden_local)
    gud = lax.psum_scatter(gud, "fsdp", scatter_dimension=0, tiled=False)
    grad_up_down = lax.psum_scatter(gud, "tp", scatter_dimension=0, tiled=False).astype(F32)

    if fast:
        mine = lax.axis_index("fsdp")
        group_sizes = (4, 4)
        out_offs = jnp.stack(
            [(mine ^ m) * shard_rows for m in (0, 2, 4, 6, 1, 3, 5, 7)]
        ).astype(jnp.int32)
    else:
        group_sizes = (1,)
        out_offs = jnp.zeros((1,), jnp.int32)
    backs = []
    for j in range(chunks):
        order = segs
        if j:
            waits = (backs[-1][0],) + (tuple(backs[-2][3][:1]) if j > 1 else ())
            order = segs[:2] + (after(segs[2], *waits),)
        dq, dk, dv, dps = attend_backward(made[j][0], slots[j], order, grad_att[j])
        waits = (backs[-1][3][:1] if j else []) + (backs[-2][3][1:] if j > 1 else [])
        arrived = merge_line(*dps, *waits)
        backs.append((dq, dk, dv, arrived, made[j][0], grad_out[j]))
    totals, lows, merged = [], [], []
    for low, high in ((0, chunks - 1), (chunks - 1, chunks)):
        if low == high:
            continue
        cols = (high - low) * 4 * HEAD_DIM
        more = jnp.zeros((EXTRA, cols), F32)
        if not merged:
            flat = small[:6].reshape(-1)
            lines = -(-flat.size // cols)
            flat = jnp.pad(flat, (0, lines * cols - flat.size)).reshape(lines, cols)
            more = jnp.pad(flat, ((TAPS + 1, EXTRA - TAPS - 1 - lines), (0, 0)))
        waits = [backs[-1][0], backs[-1][3][0]] + ([gud] if merged else [])
        groups, low_kv = gather_back(
            low, after(out_offs, *waits), group_sizes, backs[low:high], taps, same, x_cols, more
        )
        lows += low_kv
        if fast:
            merged.append(merge_cores(*[after(g, *backs[-1][3][1:]) for g in groups]))
        else:
            merged.append(spread_rows(groups[0][0], fsdp))
    middle, first, last = input_grad(
        [(backs[n][0], lows[n], made[n][2]) for n in range(chunks)], grad_residual
    )
    middle = middle.transpose(1, 0, 2)
    chips = []
    for n, blocks in enumerate(merged):
        blocks = after(blocks, *chips) if chips else blocks
        if fast:
            chips.append(merge_chips(blocks, *([] if chips else [middle])))
        else:
            chips.append(lax.psum_scatter(blocks, "fsdp", scatter_dimension=0, tiled=False))
    for blocks in chips:
        if len(totals) + 1 == len(chips):
            blocks = after(blocks, middle)
        else:
            blocks = after(blocks, merged[-1])
        totals.append(scatter_tp(blocks))

    first, last = after(first, chips[0]), after(last, chips[0])
    to_left = shift_left(first).transpose(1, 0, 2)
    to_right = shift_right(last).transpose(1, 0, 2)
    grad_inputs = middle.at[:HALF].add(to_right.astype(F32))
    grad_inputs = grad_inputs.at[rows - HALF :].add(to_left.astype(F32))

    out_rows = outputs.transpose(1, 0, 2)
    grad_up, grad_down = grad_up_down[0, :shard_rows], grad_up_down[1, :shard_rows]
    grad_up_bias = grad_up_down[0, shard_rows]
    totals[-1][0] = after(totals[-1][0], grad_inputs, out_rows, grad_up, grad_down, grad_up_bias)
    grad_w_qkv, grad_w_out, extra_rows, sums = finish(totals, chunks)
    sums = sums[TAPS + 1 :].reshape(-1)[: 6 * width].reshape(6, width)
    return (
        out_rows,
        grad_inputs,
        grad_w_qkv.transpose(1, 0, 2),
        extra_rows[:, 0],
        extra_rows[1:, 1 : TAPS + 1],
        grad_w_out,
        sums[0:2],
        grad_up,
        grad_up_bias,
        grad_down,
        sums[2:4],
        sums[4:6],
    )


def solution(mesh):
    placed = (
        P("tp", "fsdp", None),
        P(None, "fsdp"),
        P("fsdp", None, "tp"),
        P(None, "tp"),
        P(None, None, "tp"),
        P("fsdp", "tp"),
        P(),
        P("fsdp", "tp"),
        P("tp"),
        P("fsdp", "tp"),
        P(),
        P(),
        P("tp", "fsdp", None),
    )
    return jax.shard_map(
        body,
        mesh=mesh,
        in_specs=placed,
        out_specs=(
            P("tp", "fsdp", None),
            P("tp", "fsdp", None),
            P("fsdp", None, "tp"),
            P(None, "tp"),
            P(None, None, "tp"),
            P("fsdp", "tp"),
            P(),
            P("fsdp", "tp"),
            P("tp"),
            P("fsdp", "tp"),
            P(),
            P(),
        ),
        check_vma=False,
    )
```
